128 devices in a mesh: dp: 16 (over z_hi, y, core), tensor: 8 (over z_lo, x).
Axes of the slice: x: 4, y: 4, z: 4 (z_hi: 2, z_lo: 2; z = z_hi * 2 + z_lo), core: 2. Of those that a mesh axis runs over, the one named last changes fastest.
Arguments:
- layer_in: bfloat16 [16384, 2048], P(('dp', 'tensor')), may hold values from -6 to 6
- cotangent: bfloat16 [16384, 2048], P(('dp', 'tensor')), may hold values from -6 to 6
- seq_lengths: int32 [16, 4], P('dp'), may hold values from 1 to 768, 1024 in all within a row
- w_qkv: float32 [2048, 3, 2048], P('dp', None, 'tensor'), may hold values from -0.125 to 0.125
- w_out: float32 [2048, 2048], P('tensor', 'dp'), may hold values from -0.75 to 0.75
- w_up: float32 [2048, 8192], P('dp', 'tensor'), may hold values from -0.125 to 0.125
- w_down: float32 [8192, 2048], P('tensor', 'dp'), may hold values from -0.0625 to 0.0625
- b_qkv: float32 [3, 2048], P(None, 'tensor'), may hold values from -1.75 to 1.75
- b_up: float32 [8192], P('tensor'), may hold values from -1.75 to 1.75
- norm_gains: float32 [2, 2048], replicated, may hold values from 0.5 to 1.5
- row_biases: float32 [4, 2048], replicated, may hold values from -1.25 to 1.25
- m_qkv: float32 [2048, 3, 2048], P('dp', None, 'tensor'), may hold values from -80 to 80
- v_qkv: float32 [2048, 3, 2048], P('dp', None, 'tensor'), may hold values from 868.352 to 3440.64
- m_out: float32 [2048, 2048], P('tensor', 'dp'), may hold values from -24 to 24
- v_out: float32 [2048, 2048], P('tensor', 'dp'), may hold values from 78.6432 to 311.296
- m_up: float32 [2048, 8192], P('dp', 'tensor'), may hold values from -32 to 32
- v_up: float32 [2048, 8192], P('dp', 'tensor'), may hold values from 106.496 to 425.984
- m_down: float32 [8192, 2048], P('tensor', 'dp'), may hold values from -56 to 56
- v_down: float32 [8192, 2048], P('tensor', 'dp'), may hold values from 360.448 to 1458.176
- m_bqkv: float32 [3, 2048], P(None, 'tensor'), may hold values from -80 to 80
- v_bqkv: float32 [3, 2048], P(None, 'tensor'), may hold values from 868.352 to 3440.64
- m_bup: float32 [8192], P('tensor'), may hold values from -32 to 32
- v_bup: float32 [8192], P('tensor'), may hold values from 106.496 to 425.984
- m_gains: float32 [2, 2048], replicated, may hold values from -96 to 96
- v_gains: float32 [2, 2048], replicated, may hold values from 1245.184 to 4915.2
- m_biases: float32 [4, 2048], replicated, may hold values from -80 to 80
- v_biases: float32 [4, 2048], replicated, may hold values from 868.352 to 3440.64
Outputs:
- out_rows: bfloat16 [16384, 2048], P(('dp', 'tensor'))
- input_grad: float32 [16384, 2048], P(('dp', 'tensor'))
- qkv_first: float32 [2048, 3, 2048], P('dp', None, 'tensor')
- qkv_second: float32 [2048, 3, 2048], P('dp', None, 'tensor')
- qkv_new: float32 [2048, 3, 2048], P('dp', None, 'tensor')
- out_first: float32 [2048, 2048], P('tensor', 'dp')
- out_second: float32 [2048, 2048], P('tensor', 'dp')
- out_new: float32 [2048, 2048], P('tensor', 'dp')
- up_first: float32 [2048, 8192], P('dp', 'tensor')
- up_second: float32 [2048, 8192], P('dp', 'tensor')
- up_new: float32 [2048, 8192], P('dp', 'tensor')
- down_first: float32 [8192, 2048], P('tensor', 'dp')
- down_second: float32 [8192, 2048], P('tensor', 'dp')
- down_new: float32 [8192, 2048], P('tensor', 'dp')
- bqkv_first: float32 [3, 2048], P(None, 'tensor')
- bqkv_second: float32 [3, 2048], P(None, 'tensor')
- bqkv_new: float32 [3, 2048], P(None, 'tensor')
- bup_first: float32 [8192], P('tensor')
- bup_second: float32 [8192], P('tensor')
- bup_new: float32 [8192], P('tensor')
- gains_first: float32 [2, 2048], replicated
- gains_second: float32 [2, 2048], replicated
- gains_new: float32 [2, 2048], replicated
- biases_first: float32 [4, 2048], replicated
- biases_second: float32 [4, 2048], replicated
- biases_new: float32 [4, 2048], replicated
The draws below stay inside these ranges and needn't reach their ends.
Inputs may be any that keep to these rules, and one draw needn't show every extreme that they name: `seq_lengths`: each row lists the lengths of the 4 sequences packed in one data group in order; a row sums to 1024 and its longest length is exactly 768.
All inputs are finite; a program needn't handle non-finite values.
Results may differ from the reference program's by a relative error of at most 0.025.
Values may be sent and summed in bfloat16 or wider, within the bound.
A program may use at most 128 MiB of HBM per device.

```python
import math
import jax
import jax.numpy as jnp
import numpy as np
from jax import lax

D = 2048
HEADS = 8
HEAD_DIM = 256
FF = 8192
ROT = 64
PACK = 1024
SEQS = 4
MAXLEN = 768
STEP = 10
TOKENS = 16384
N_DP = 16


def steps_of(rng, extent, shards, least, largest):
    level, own = 1.0, jax.random.fold_in(rng, 6)
    for dim, blocks in shards:
        steps = jnp.exp(jax.random.uniform(jax.random.fold_in(own, dim), (blocks,), jnp.float32, least / len(shards), largest / len(shards)))
        level = level * jnp.repeat(steps, extent[dim] // blocks).reshape([-1 if axis == dim else 1 for axis in range(len(extent))])
    return level


def split_up(number_of, total, most, slope):
    loads = [(1 << 20) // math.isqrt(standing ** slope) + 1 for standing in range(2, number_of + 1)]
    rest, counts = total - most - (number_of - 1), [1] * (number_of - 1)
    while rest > 0:
        movable = [i for i in range(number_of - 1) if counts[i] < most]
        whole, left = sum([loads[i] for i in movable]), rest
        for i in movable:
            extra = min(most - counts[i], max(1, left * loads[i] // whole), rest)
            counts[i] = counts[i] + extra
            rest = rest - extra
    return np.array([most] + counts)


def uneven(own_key, amount, total, most, skew):
    if amount == 2:
        one = jax.random.randint(own_key, (), max(1, total - most), min(most, total - 1) + 1)
        return jnp.stack([one, total - one])
    tallies = jnp.asarray(split_up(amount, total, most, skew), jnp.int32)
    twos = (amount - 1) // 2
    giver, taker = tallies[1:1 + 2 * twos:2], tallies[2:2 + 2 * twos:2]
    room = jnp.minimum(giver - 1, most - taker)
    moved = jax.random.randint(jax.random.fold_in(own_key, 1), (twos,), 0, 1 << 20) % (room + 1)
    tallies = tallies.at[1:1 + 2 * twos:2].set(giver - moved).at[2:2 + 2 * twos:2].set(taker + moved)
    return tallies[jax.random.permutation(jax.random.fold_in(own_key, 2), amount)]


def bell_draw(stream_key, dims, scale, bound, cuts=(), kind=jnp.bfloat16):
    gain = steps_of(stream_key, dims, cuts, -0.22, 0.18) if cuts else 1.0
    entries = jax.random.normal(stream_key, dims, jnp.float32) * scale * gain
    return jnp.minimum(jnp.maximum(entries, -bound), bound).astype(kind)


def setup_inputs(seed: int = 0) -> dict:
    splits = jax.random.split(jax.random.key(seed), 28)
    layer_in = bell_draw(splits[0], (TOKENS, D), 1.0, 6.0, ((0, 128),))
    cotangent = bell_draw(splits[1], (TOKENS, D), 1.0, 6.0, ((0, 128),))
    seq_lengths = jax.vmap(lambda own: uneven(own, SEQS, PACK, MAXLEN, 2))(jax.random.split(splits[2], N_DP)).reshape((N_DP, SEQS)).astype(jnp.int32)
    w_qkv = bell_draw(splits[3], (D, 3, D), D ** -0.5, 0.125, ((0, 16), (2, 8)), jnp.float32)
    w_out = bell_draw(splits[4], (D, D), (D // 32) ** -0.5, 0.75, ((0, 8), (1, 16)), jnp.float32)
    w_up = bell_draw(splits[5], (D, FF), D ** -0.5, 0.125, ((0, 16), (1, 8)), jnp.float32)
    w_down = bell_draw(splits[6], (FF, D), FF ** -0.5, 0.0625, ((0, 8), (1, 16)), jnp.float32)
    b_qkv = bell_draw(splits[7], (3, D), 0.3, 1.75, ((1, 8),), jnp.float32)
    b_up = bell_draw(splits[8], (FF,), 0.3, 1.75, ((0, 8),), jnp.float32)
    norm_gains = jnp.clip(1.0 + 0.1 * jax.random.normal(splits[9], (2, D), jnp.float32), 0.5, 1.5)
    row_biases = bell_draw(splits[10], (4, D), 0.2, 1.25, (), jnp.float32)
    m_qkv = bell_draw(splits[11], (D, 3, D), (0.11 * (PACK * N_DP) ** 0.5), 80.0, ((0, 16), (2, 8)), jnp.float32)
    v_qkv = jnp.clip(jnp.exp(math.log(3440.64) - 1.3768156 * jax.random.uniform(splits[12], (D, 3, D), jnp.float32) ** steps_of(splits[12], (D, 3, D), ((0, 16), (2, 8)), -0.2, 0.2)), 868.352, 3440.64)
    m_out = bell_draw(splits[13], (D, D), (0.033 * (PACK * N_DP) ** 0.5), 24.0, ((0, 8), (1, 16)), jnp.float32)
    v_out = jnp.clip(jnp.exp(math.log(311.296) - 1.375823 * jax.random.uniform(splits[14], (D, D), jnp.float32) ** steps_of(splits[14], (D, D), ((0, 8), (1, 16)), -0.2, 0.2)), 78.6432, 311.296)
    m_up = bell_draw(splits[15], (D, FF), (0.039 * (PACK * N_DP) ** 0.5), 32.0, ((0, 16), (1, 8)), jnp.float32)
    v_up = jnp.clip(jnp.exp(math.log(425.984) - 1.3862944 * jax.random.uniform(splits[16], (D, FF), jnp.float32) ** steps_of(splits[16], (D, FF), ((0, 16), (1, 8)), -0.2, 0.2)), 106.496, 425.984)
    m_down = bell_draw(splits[17], (FF, D), (0.072 * (PACK * N_DP) ** 0.5), 56.0, ((0, 8), (1, 16)), jnp.float32)
    v_down = jnp.clip(jnp.exp(math.log(1458.176) - 1.397594 * jax.random.uniform(splits[18], (FF, D), jnp.float32) ** steps_of(splits[18], (FF, D), ((0, 8), (1, 16)), -0.2, 0.2)), 360.448, 1458.176)
    m_bqkv = bell_draw(splits[19], (3, D), (0.11 * (PACK * N_DP) ** 0.5), 80.0, ((1, 8),), jnp.float32)
    v_bqkv = jnp.clip(jnp.exp(math.log(3440.64) - 1.3768156 * jax.random.uniform(splits[20], (3, D), jnp.float32) ** steps_of(splits[20], (3, D), ((1, 8),), -0.2, 0.2)), 868.352, 3440.64)
    m_bup = bell_draw(splits[21], (FF,), (0.039 * (PACK * N_DP) ** 0.5), 32.0, ((0, 8),), jnp.float32)
    v_bup = jnp.clip(jnp.exp(math.log(425.984) - 1.3862944 * jax.random.uniform(splits[22], (FF,), jnp.float32) ** steps_of(splits[22], (FF,), ((0, 8),), -0.2, 0.2)), 106.496, 425.984)
    m_gains = bell_draw(splits[23], (2, D), (0.13 * (PACK * N_DP) ** 0.5), 96.0, (), jnp.float32)
    v_gains = jnp.clip(jnp.exp(jax.random.uniform(splits[24], (2, D), jnp.float32, math.log(1245.184), math.log(4915.2))), 1245.184, 4915.2)
    m_biases = bell_draw(splits[25], (4, D), (0.11 * (PACK * N_DP) ** 0.5), 80.0, (), jnp.float32)
    v_biases = jnp.clip(jnp.exp(jax.random.uniform(splits[26], (4, D), jnp.float32, math.log(868.352), math.log(3440.64))), 868.352, 3440.64)
    return {"layer_in": layer_in, "cotangent": cotangent, "seq_lengths": seq_lengths, "w_qkv": w_qkv, "w_out": w_out, "w_up": w_up, "w_down": w_down, "b_qkv": b_qkv, "b_up": b_up, "norm_gains": norm_gains, "row_biases": row_biases, "m_qkv": m_qkv, "v_qkv": v_qkv, "m_out": m_out, "v_out": v_out, "m_up": m_up, "v_up": v_up, "m_down": m_down, "v_down": v_down, "m_bqkv": m_bqkv, "v_bqkv": v_bqkv, "m_bup": m_bup, "v_bup": v_bup, "m_gains": m_gains, "v_gains": v_gains, "m_biases": m_biases, "v_biases": v_biases}


NORM_EPS = 1e-05
HIGHEST_PRECISION = lax.Precision.HIGHEST
BETA_ONE = 0.9
BETA_TWO = 0.95
ADAM_EPS = 1e-08
STEP_RATES = (0.04, 0.2, 0.04, 0.02, 0.3, 0.3, 0.5, 0.3)
DECAY_RATES = (0.01, 0.01, 0.01, 0.01, 0.0, 0.0, 0.0, 0.0)

@jax.custom_vjp
def low(v):
    return lax.optimization_barrier(v.astype(jnp.bfloat16)).astype(jnp.float32)

@jax.custom_vjp
def low_back(v):
    return v

def low_keep(v):
    return (low(v), None)

def low_pass(kept, grad):
    return (grad,)

def back_keep(v):
    return (v, None)

def back_low(kept, grad):
    return (low(grad),)
low.defvjp(low_keep, low_pass)
low_back.defvjp(back_keep, back_low)

def segment_info(lengths, token_count):
    indices = jnp.arange(token_count, dtype=jnp.int32)
    ends = jnp.cumsum(lengths).astype(jnp.int32)
    starts = (ends - lengths).astype(jnp.int32)
    segment = lax.optimization_barrier(jnp.sum((indices[:, None] >= ends[None, :]).astype(jnp.int32), axis=1)).astype(jnp.int32)
    own_seq = (segment[:, None] == jnp.arange(lengths.shape[0], dtype=jnp.int32)[None, :]).astype(jnp.int32)
    position = (indices - lax.optimization_barrier(jnp.sum(own_seq * starts[None, :], axis=1))).astype(jnp.int32)
    return (segment, position)

def rotary_tables(position, rot_dims):
    half_rot = rot_dims // 2
    frequency = 10000.0 ** (-jnp.arange(half_rot, dtype=jnp.float32) * 2.0 / rot_dims)
    angles = position.astype(jnp.float32)[:, None] * frequency[None, :]
    angles = jnp.concatenate([angles, angles], axis=1)
    return (jnp.cos(angles), jnp.sin(angles))

def rotate(tensor_in, cosines, sine_rows, rot_dims):
    half_rot = rot_dims // 2
    rotated = tensor_in[..., :rot_dims]
    turned = jnp.concatenate([-rotated[..., half_rot:], rotated[..., :half_rot]], axis=-1)
    moved = rotated * cosines[:, None, :] + turned * sine_rows[:, None, :]
    return jnp.concatenate([moved, tensor_in[..., rot_dims:]], axis=-1)

def attend(queries, keys_low, values, segment, block_rows):
    token_count = queries.shape[0]
    block_count = token_count // block_rows
    indices = jnp.arange(token_count, dtype=jnp.int32)
    score_scale = HEAD_DIM ** (-0.5)

    def one_block(block_args):
        query_block, query_segment, query_index = block_args
        scores = jnp.einsum('qhd,khd->hqk', query_block, keys_low, precision=HIGHEST_PRECISION)
        scores = low_back(scores * score_scale)
        allowed = (query_segment[:, None] == segment[None, :]) & (query_index[:, None] >= indices[None, :])
        scores = jnp.where(allowed[None], scores, -jnp.inf)
        row_max = lax.optimization_barrier(jnp.max(scores, axis=-1, keepdims=True))
        expo = jnp.exp(scores - row_max)
        probs = expo / lax.optimization_barrier(jnp.sum(expo, axis=-1, keepdims=True))
        return jnp.einsum('hqk,khd->qhd', low(probs), values, precision=HIGHEST_PRECISION)
    result = lax.map(jax.checkpoint(one_block), (queries.reshape(block_count, block_rows, HEADS, HEAD_DIM), segment.reshape(block_count, block_rows), indices.reshape(block_count, block_rows)))
    return result.reshape(token_count, HEADS, HEAD_DIM)

def forward_group(group_in, w_qkv, w_out, w_up, w_down, b_qkv, b_up, norm_gains, row_biases, segment, position):
    token_count = group_in.shape[0]
    row_mean = lax.optimization_barrier(jnp.mean(group_in, axis=-1, keepdims=True))
    centered = group_in - row_mean
    variance = lax.optimization_barrier(jnp.mean(centered * centered, axis=-1, keepdims=True))
    unit = centered * lax.rsqrt(variance + NORM_EPS)
    unit_low = low(unit)
    first_normed = low(unit_low * norm_gains[0] + row_biases[0])
    second_normed = low(unit_low * norm_gains[1] + row_biases[1])
    projected = low_back(jnp.dot(first_normed, low(w_qkv).reshape(D, 3 * D), precision=HIGHEST_PRECISION))
    projected = projected.reshape(token_count, 3, HEADS, HEAD_DIM) + b_qkv.reshape(1, 3, HEADS, HEAD_DIM)
    cosines, sine_rows = rotary_tables(position, ROT)
    queries = low(rotate(projected[:, 0], cosines, sine_rows, ROT))
    keys_low = low(rotate(projected[:, 1], cosines, sine_rows, ROT))
    values = low(projected[:, 2])
    mixed = attend(queries, keys_low, values, segment, min(512, token_count))
    mixed = low(low_back(mixed)).reshape(token_count, D)
    inner_pre = low_back(jnp.dot(second_normed, low(w_up), precision=HIGHEST_PRECISION)) + b_up
    activation = low(jax.nn.gelu(inner_pre, approximate=False))
    branch = jnp.dot(mixed, low(w_out), precision=HIGHEST_PRECISION) + jnp.dot(activation, low(w_down), precision=HIGHEST_PRECISION)
    return group_in + branch + row_biases[2] + row_biases[3]

def adam_step(weight, gradient, moment_one, moment_two, step_rate, decay_rate):
    moment_one = BETA_ONE * moment_one + (1.0 - BETA_ONE) * gradient
    moment_two = BETA_TWO * moment_two + (1.0 - BETA_TWO) * gradient * gradient
    ratio = moment_one / (1.0 - BETA_ONE ** STEP) / (jnp.sqrt(moment_two / (1.0 - BETA_TWO ** STEP)) + ADAM_EPS)
    return (moment_one, moment_two, weight - step_rate * (ratio + decay_rate * weight))

def reference(layer_in, cotangent, seq_lengths, w_qkv, w_out, w_up, w_down, b_qkv, b_up, norm_gains, row_biases, m_qkv, v_qkv, m_out, v_out, m_up, v_up, m_down, v_down, m_bqkv, v_bqkv, m_bup, v_bup, m_gains, v_gains, m_biases, v_biases):
    params = (w_qkv, w_out, w_up, w_down, b_qkv, b_up, norm_gains, row_biases)

    def group_step(running, group_item):
        group_in, group_grad, lengths = group_item
        segment, position = segment_info(lengths, PACK)

        def run(rows_in, weights):
            return forward_group(rows_in, weights[0], weights[1], weights[2], weights[3], weights[4], weights[5], weights[6], weights[7], segment, position)
        result, pullback = jax.vjp(run, group_in.astype(jnp.float32), params)
        rows_grad, weight_grads = pullback(group_grad.astype(jnp.float32))
        running = jax.tree.map(jnp.add, running, weight_grads)
        return (running, (result.astype(jnp.bfloat16), rows_grad))
    zero_grads = jax.tree.map(jnp.zeros_like, params)
    grad_sums, (out_rows, input_grad) = lax.scan(group_step, zero_grads, (layer_in.reshape(N_DP, PACK, D), cotangent.reshape(N_DP, PACK, D), seq_lengths))
    moments = ((m_qkv, v_qkv), (m_out, v_out), (m_up, v_up), (m_down, v_down), (m_bqkv, v_bqkv), (m_bup, v_bup), (m_gains, v_gains), (m_biases, v_biases))
    updated = []
    for which in range(8):
        updated.append(adam_step(params[which], grad_sums[which], moments[which][0], moments[which][1], STEP_RATES[which], DECAY_RATES[which]))
    return (out_rows.reshape(N_DP * PACK, D), input_grad.reshape(N_DP * PACK, D), updated[0][0], updated[0][1], updated[0][2], updated[1][0], updated[1][1], updated[1][2], updated[2][0], updated[2][1], updated[2][2], updated[3][0], updated[3][1], updated[3][2], updated[4][0], updated[4][1], updated[4][2], updated[5][0], updated[5][1], updated[5][2], updated[6][0], updated[6][1], updated[6][2], updated[7][0], updated[7][1], updated[7][2])
```

```python
import functools
import math

import jax
import jax.numpy as jnp
from jax import lax
from jax.experimental import pallas as pl
from jax.experimental.pallas import tpu as pltpu
from jax.sharding import PartitionSpec as P

F32 = jnp.float32
BF16 = jnp.bfloat16
MESH = pl.DeviceIdType.MESH

D = 2048
HEAD = 256
QKV = 3 * HEAD
UNITS = 1024
WIDE = QKV + UNITS
DEEP = HEAD + UNITS
TOK = 1024
OWN = 128
TILE = 512
QROWS = 256
ROT = 64
STEP = 10

NORM_EPS = 1e-05
BETA_ONE = 0.9
BETA_TWO = 0.95
ADAM_EPS = 1e-08
STEP_RATES = (0.04, 0.2, 0.04, 0.02, 0.3, 0.3, 0.5, 0.3)
DECAY_RATES = (0.01, 0.01, 0.01, 0.01, 0.0, 0.0, 0.0, 0.0)


def place():
    dp = lax.axis_index("dp")
    tensor = lax.axis_index("tensor")
    return (
        lax.div(dp, 8),
        lax.rem(lax.div(dp, 2), 4),
        lax.rem(dp, 2),
        lax.div(tensor, 4),
        lax.rem(tensor, 4),
    )


def device(zh, y, core, zl, x):
    return ((zh * 4 + y) * 2 + core, zl * 4 + x)


def around(pos, step):
    return lax.rem(pos + step + 4, 4)


def neighbours(spot):
    zh, y, core, zl, x = spot
    return {
        "x+": device(zh, y, core, zl, around(x, 1)),
        "x-": device(zh, y, core, zl, around(x, -1)),
        "y+": device(zh, around(y, 1), core, zl, x),
        "y-": device(zh, around(y, -1), core, zl, x),
        "zl": device(zh, y, core, 1 - zl, x),
        "zh": device(1 - zh, y, core, zl, x),
        "core": device(zh, y, 1 - core, zl, x),
    }


class Links:
    def __init__(self, send_sems, recv_sems):
        self.send_sems, self.recv_sems = send_sems, recv_sems
        self.copies = []

    def send(self, src, dst, target):
        index = len(self.copies)
        copy = pltpu.make_async_remote_copy(
            src_ref=src,
            dst_ref=dst,
            send_sem=self.send_sems.at[index],
            recv_sem=self.recv_sems.at[index],
            device_id=target,
            device_id_type=MESH,
        )
        copy.start()
        self.copies.append(copy)
        return copy

    def drain(self):
        for copy in self.copies:
            copy.wait_send()


class Gather:
    def __init__(self, links, block, z, ring, z_dev, plus, minus, core=None):
        self.links, self.block, self.z, self.ring = links, block, z, ring
        self.z_dev, self.plus, self.minus, self.core = z_dev, plus, minus, core
        self.core_copies = []

    def pass_on(self, z, ring, half=None):
        if self.core is not None:
            part = self.block(z, ring, half)
            self.core_copies.append(self.links.send(part, part, self.core))

    def to(self, z, ring, half, target):
        part = self.block(z, ring, half)
        return self.links.send(part, part, target)

    def start(self):
        self.by_z = self.to(self.z, self.ring, None, self.z_dev)
        self.first = (
            self.to(self.z, self.ring, None, self.plus),
            self.to(self.z, self.ring, None, self.minus),
        )
        self.pass_on(self.z, self.ring)

    def partner(self):
        self.by_z.wait_recv()
        self.second = (
            self.to(1 - self.z, self.ring, None, self.plus),
            self.to(1 - self.z, self.ring, None, self.minus),
        )
        self.pass_on(1 - self.z, self.ring)

    def forward(self, z, copies):
        copies[0].wait_recv()
        up = self.to(z, around(self.ring, -1), 0, self.plus)
        copies[1].wait_recv()
        down = self.to(z, around(self.ring, 1), 1, self.minus)
        self.pass_on(z, around(self.ring, -1))
        self.pass_on(z, around(self.ring, 1))
        return (up, down)

    def near(self):
        self.third = self.forward(self.z, self.first)

    def far(self):
        self.fourth = self.forward(1 - self.z, self.second)

    def last(self):
        for z, copies in ((self.z, self.third), (1 - self.z, self.fourth)):
            copies[0].wait_recv()
            copies[1].wait_recv()
            self.pass_on(z, around(self.ring, 2))

    def finish(self):
        for copy in self.core_copies:
            copy.wait_recv()


def rows_of(ref, start, count):
    return ref.at[pl.ds(pl.multiple_of(start, 16), count)]


def gelu_parts(pre):
    cdf = 0.5 * (1.0 + lax.erf(pre * (1.0 / math.sqrt(2.0))))
    density = jnp.exp(-0.5 * pre * pre) * (1.0 / math.sqrt(2.0 * math.pi))
    return pre * cdf, cdf + pre * density


def spin(rows, cosines, sines, back):
    low = rows[:, :128]
    lane = lax.broadcasted_iota(jnp.int32, low.shape, 1)
    ahead = pltpu.roll(low, 96, 1)
    behind = pltpu.roll(low, 32, 1)
    turned = jnp.where(lane < 32, -ahead, jnp.where(lane < 64, behind, 0.0))
    if back:
        turned = -turned
    return jnp.concatenate([low * cosines + turned * sines, rows[:, 128:]], axis=1)


def forward_kernel(
    lens,
    x_in,
    cot_in,
    w_qkv,
    w_out,
    w_up,
    w_down,
    b_qkv,
    b_up,
    gains,
    biases,
    unit_out,
    cot_out,
    wide_out,
    deep_out,
    q_out,
    k_out,
    v_out,
    acts_out,
    slope_out,
    probs_out,
    turn_out,
    branch_out,
    unit,
    cot,
    wide,
    deep,
    q,
    k,
    v,
    acts,
    slope,
    probs,
    turn,
    branch,
    begins,
    normed,
    send_sems,
    recv_sems,
    out_sems,
):
    spot = place()
    zh, y, core, zl, x = spot
    near = neighbours(spot)
    barrier = pltpu.get_barrier_semaphore()
    for target in near.values():
        pl.semaphore_signal(barrier, inc=1, device_id=target, device_id_type=MESH)

    links = Links(send_sems, recv_sems)
    stores = []

    def store(src, dst):
        copy = pltpu.make_async_copy(src, dst, out_sems.at[len(stores)])
        copy.start()
        stores.append(copy)

    def token_block(ref):
        def block(z, ring, half):
            start = (z * 4 + ring) * OWN
            if half is None:
                return rows_of(ref, start, OWN)
            return rows_of(ref, start + half * (OWN // 2), OWN // 2)

        return block

    def wide_block(z, ring, half):
        start = ((z * 4 + ring) * 2 + core) * OWN
        if half is None:
            return rows_of(wide, start, OWN)
        return rows_of(wide, start + half * (OWN // 2), OWN // 2)

    def deep_block(z, ring, half):
        columns = pl.ds(pl.multiple_of(((z * 4 + ring) * 2 + core) * OWN, OWN), OWN)
        if half is None:
            return deep.at[:, columns]
        return deep.at[pl.ds(half * (DEEP // 2), DEEP // 2), columns]

    tensor_ends = (zl, x, near["zl"], near["x+"], near["x-"])
    data_ends = (zh, y, near["zh"], near["y+"], near["y-"], near["core"])
    units = Gather(links, token_block(unit), *tensor_ends)
    grads = Gather(links, token_block(cot), *tensor_ends)
    wides = Gather(links, wide_block, *data_ends)
    deeps = Gather(links, deep_block, *data_ends)

    rows = x_in[...].astype(F32)
    centred = rows - jnp.mean(rows, axis=-1, keepdims=True)
    variance = jnp.mean(centred * centred, axis=-1, keepdims=True)
    mine = pl.ds(pl.multiple_of((zl * 4 + x) * OWN, OWN), OWN)
    unit[mine, :] = (centred * lax.rsqrt(variance + NORM_EPS)).astype(BF16)
    own = pl.ds(pl.multiple_of(((zh * 4 + y) * 2 + core) * OWN, OWN), OWN)
    wide[own, :QKV] = w_qkv[...].astype(BF16)
    wide[own, QKV:] = w_up[...].astype(BF16)
    pl.semaphore_wait(barrier, len(near))
    units.start()
    wides.start()
    cot[mine, :] = cot_in[...]
    deep[:HEAD, own] = w_out[...].astype(BF16)
    deep[HEAD:, own] = w_down[...].astype(BF16)

    index = lax.broadcasted_iota(jnp.int32, (TOK, 128), 0)
    ends = [lens[0, 0]]
    for seq in range(1, 3):
        ends.append(ends[-1] + lens[0, seq])
    begin = jnp.zeros((TOK, 128), jnp.int32)
    for end in ends:
        begin = jnp.where(index >= end, end, begin)
    begins[...] = begin
    lane = lax.broadcasted_iota(jnp.int32, (TOK, 128), 1)
    rate = jnp.exp(lax.rem(lane, 32).astype(F32) * (-2.0 * math.log(10000.0) / ROT))
    angle = (index - begin).astype(F32) * rate
    turn[0] = jnp.where(lane < ROT, jnp.cos(angle), 1.0)
    turn[1] = jnp.where(lane < ROT, jnp.sin(angle), 0.0)
    store(turn, turn_out)

    units.partner()
    wides.partner()
    wides.near()
    units.near()
    wides.far()
    units.far()
    deeps.start()
    grads.start()
    wides.last()
    units.last()
    wides.finish()
    units.finish()
    grads.partner()
    deeps.partner()
    store(unit, unit_out)
    store(wide, wide_out)

    def project(tile, _):
        part = pl.ds(pl.multiple_of(tile * TILE, TILE), TILE)
        unit_rows = unit[part, :].astype(F32)
        normed[0] = (unit_rows * gains[0:1, :] + biases[0:1, :]).astype(BF16)
        normed[1] = (unit_rows * gains[1:2, :] + biases[1:2, :]).astype(BF16)
        cosines, sines = turn[0, part, :], turn[1, part, :]
        for which, target in enumerate((q, k, v)):
            columns = slice(which * HEAD, (which + 1) * HEAD)
            head = jnp.dot(normed[0], wide[:, columns], preferred_element_type=F32)
            head = head + b_qkv[which : which + 1, :]
            if which < 2:
                head = spin(head, cosines, sines, False)
            target[part, :] = head.astype(BF16)

        def hidden(piece, _):
            shift = pl.multiple_of(piece * 256, 256)
            pre = jnp.dot(normed[1], wide[:, pl.ds(QKV + shift, 256)], preferred_element_type=F32)
            pre = pre + b_up[0:1, pl.ds(shift, 256)]
            value, rise = gelu_parts(pre)
            acts[part, pl.ds(HEAD + shift, 256)] = value.astype(BF16)
            slope[part, pl.ds(shift, 256)] = rise.astype(BF16)
            return 0

        lax.fori_loop(0, UNITS // 256, hidden, 0)
        return 0

    project(0, 0)
    deeps.near()
    grads.near()
    project(1, 0)
    deeps.far()
    store(q, q_out)
    store(k, k_out)
    store(v, v_out)
    store(slope, slope_out)

    for block in range(TOK // QROWS):
        part = slice(block * QROWS, (block + 1) * QROWS)
        keys = (block + 1) * QROWS
        scores = lax.dot_general(
            q[part, :], k[:keys, :], (((1,), (1,)), ((), ())), preferred_element_type=F32
        ) * (HEAD**-0.5)
        key = lax.broadcasted_iota(jnp.int32, (QROWS, keys), 1)
        row = lax.broadcasted_iota(jnp.int32, (QROWS, keys), 0) + block * QROWS
        allowed = (key <= row) & (key >= begins[part, 0:1])
        scores = jnp.where(allowed, scores, -jnp.inf)
        expo = jnp.exp(scores - jnp.max(scores, axis=-1, keepdims=True))
        share = (expo / jnp.sum(expo, axis=-1, keepdims=True)).astype(BF16)
        probs[part, :keys] = share
        acts[part, :HEAD] = jnp.dot(share, v[:keys, :], preferred_element_type=F32).astype(BF16)
    store(probs, probs_out)
    store(acts, acts_out)
    grads.far()
    deeps.last()
    deeps.finish()
    store(deep, deep_out)

    def mix(tile, _):
        part = pl.ds(pl.multiple_of(tile * TILE, TILE), TILE)

        def piece(step, _):
            columns = pl.ds(pl.multiple_of(step * 256, 256), 256)
            branch[part, columns] = jnp.dot(
                acts[part, :], deep[:, columns], preferred_element_type=F32
            ).astype(BF16)
            return 0

        return lax.fori_loop(0, D // 256, piece, 0)

    lax.fori_loop(0, TOK // TILE, mix, 0)
    store(branch, branch_out)
    grads.last()
    store(cot, cot_out)
    for copy in stores:
        copy.wait()
    links.drain()


FORWARD_KEPT = (
    ((TOK, D), BF16),
    ((TOK, D), BF16),
    ((D, WIDE), BF16),
    ((DEEP, D), BF16),
    ((TOK, HEAD), BF16),
    ((TOK, HEAD), BF16),
    ((TOK, HEAD), BF16),
    ((TOK, DEEP), BF16),
    ((TOK, UNITS), BF16),
    ((TOK, TOK), BF16),
    ((2, TOK, 128), F32),
    ((TOK, D), BF16),
)


def run_forward(lens, *inputs):
    vmem = pl.BlockSpec(memory_space=pltpu.VMEM)
    return pl.pallas_call(
        forward_kernel,
        out_shape=[jax.ShapeDtypeStruct(*kept) for kept in FORWARD_KEPT],
        in_specs=[pl.BlockSpec(memory_space=pltpu.SMEM)] + [vmem] * len(inputs),
        out_specs=[pl.BlockSpec(memory_space=pl.ANY)] * len(FORWARD_KEPT),
        scratch_shapes=[pltpu.VMEM(*kept) for kept in FORWARD_KEPT]
        + [
            pltpu.VMEM((TOK, 128), jnp.int32),
            pltpu.VMEM((2, TILE, D), BF16),
            pltpu.SemaphoreType.DMA((64,)),
            pltpu.SemaphoreType.DMA((64,)),
            pltpu.SemaphoreType.DMA((len(FORWARD_KEPT),)),
        ],
        compiler_params=pltpu.CompilerParams(
            collective_id=0, has_side_effects=True, vmem_limit_bytes=60 * 2**20
        ),
        cost_estimate=pl.CostEstimate(flops=14 * 10**9, bytes_accessed=40 * 10**6, transcendentals=0),
        name="forward",
    )(lens, *inputs)


def over_rows(left, right):
    return lax.dot_general(left, right, (((0,), (0,)), ((), ())), preferred_element_type=F32)


def by_rows(left, right):
    return lax.dot_general(left, right, (((1,), (1,)), ((), ())), preferred_element_type=F32)


def adam_step(weight, gradient, moment_one, moment_two, step_rate, decay_rate):
    moment_one = BETA_ONE * moment_one + (1.0 - BETA_ONE) * gradient
    moment_two = BETA_TWO * moment_two + (1.0 - BETA_TWO) * gradient * gradient
    ratio = (
        moment_one
        / (1.0 - BETA_ONE**STEP)
        / (jnp.sqrt(moment_two / (1.0 - BETA_TWO**STEP)) + ADAM_EPS)
    )
    return (moment_one, moment_two, weight - step_rate * (ratio + decay_rate * weight))


def local(
    layer_in, cotangent, seq_lengths, w_qkv, w_out, w_up, w_down, b_qkv, b_up, norm_gains, row_biases,
    m_qkv, v_qkv, m_out, v_out, m_up, v_up, m_down, v_down, m_bqkv, v_bqkv, m_bup, v_bup,
    m_gains, v_gains, m_biases, v_biases,
):
    tensor_size = lax.axis_size("tensor")
    tensor_place = lax.axis_index("tensor")
    resid = layer_in.astype(F32)
    row_mean = jnp.mean(resid, axis=-1, keepdims=True)
    centered = resid - row_mean
    variance = jnp.mean(centered * centered, axis=-1, keepdims=True)
    inverse = lax.rsqrt(variance + NORM_EPS)
    own_unit = centered * inverse
    (unit, grad_rows, wide, deep, q, k, v, acts, slope, probs, turn, branch) = run_forward(
        seq_lengths, layer_in, cotangent, w_qkv.reshape(OWN, QKV), w_out, w_up, w_down,
        b_qkv, b_up.reshape(1, UNITS), norm_gains, row_biases)
    branch = lax.psum_scatter(branch, "tensor", scatter_dimension=0, tiled=True).astype(F32)
    out_rows = (resid + branch + row_biases[2] + row_biases[3]).astype(BF16)
    deep_grad = over_rows(acts, grad_rows)
    back = by_rows(grad_rows, deep)
    mixed_grad = back[:, :HEAD].astype(BF16)
    inner_grad = back[:, HEAD:] * slope.astype(F32)
    inner_low = inner_grad.astype(BF16)
    unit_f = unit.astype(F32)
    first_normed = (unit_f * norm_gains[0] + row_biases[0]).astype(BF16)
    second_normed = (unit_f * norm_gains[1] + row_biases[1]).astype(BF16)
    up_grad = over_rows(second_normed, inner_low)
    second_part = by_rows(inner_low, wide[:, QKV:])
    index = jnp.arange(TOK)
    pf = jnp.where(index[:, None] // QROWS >= index[None, :] // QROWS, probs.astype(F32), 0.0)
    prob_grad = by_rows(mixed_grad, v)
    delta = jnp.sum(pf * prob_grad, axis=-1, keepdims=True)
    score_grad = (pf * (prob_grad - delta)).astype(BF16)
    scale = HEAD**-0.5
    query_grad = jnp.dot(score_grad, k, preferred_element_type=F32) * scale
    key_grad = over_rows(score_grad, q) * scale
    value_grad = over_rows(pf.astype(BF16), mixed_grad)

    def back_spin(rows):
        cosines, sines = turn[0, :, :64], turn[1, :, :64]
        sined = rows[:, :64] * sines
        turned = jnp.concatenate([sined[:, 32:], -sined[:, :32]], axis=1)
        return jnp.concatenate([rows[:, :64] * cosines + turned, rows[:, 64:]], axis=1)

    projected_grad = jnp.concatenate([back_spin(query_grad), back_spin(key_grad), value_grad], axis=1)
    projected_low = projected_grad.astype(BF16)
    qkv_grad = over_rows(first_normed, projected_low)
    first_part = by_rows(projected_low, wide[:, :QKV])
    qkv_bias_grad = jnp.sum(projected_grad, axis=0).reshape(3, HEAD)
    up_bias_grad = jnp.sum(inner_grad, axis=0)
    grad_own = cotangent.astype(F32)
    out_bias_grad = jnp.sum(grad_own, axis=0)
    gain_part = jnp.stack([jnp.sum(first_part * unit_f, axis=0), jnp.sum(second_part * unit_f, axis=0)])
    shift_part = jnp.stack([jnp.sum(first_part, axis=0), jnp.sum(second_part, axis=0)])
    unit_grad = lax.psum_scatter(
        (first_part * norm_gains[0] + second_part * norm_gains[1]).astype(BF16),
        "tensor", scatter_dimension=0, tiled=True).astype(F32)
    unit_mean = jnp.mean(unit_grad, axis=-1, keepdims=True)
    unit_proj = jnp.mean(unit_grad * own_unit, axis=-1, keepdims=True)
    input_grad = grad_own + inverse * (unit_grad - unit_mean - own_unit * unit_proj)
    bias_part = jnp.concatenate([shift_part, out_bias_grad[None, :], out_bias_grad[None, :]], axis=0)
    gain_sum, bias_sum = lax.psum((gain_part, bias_part), ("dp", "tensor"))
    qkv_bias_sum, up_bias_sum = lax.psum((qkv_bias_grad, up_bias_grad), "dp")
    wide_grad = jnp.concatenate([qkv_grad, up_grad], axis=1).astype(BF16)
    wide_sum = lax.psum_scatter(wide_grad, "dp", scatter_dimension=0, tiled=True).astype(F32)
    deep_sum = lax.psum_scatter(deep_grad.astype(BF16), "dp", scatter_dimension=1, tiled=True).astype(F32)
    params = (w_qkv, w_out, w_up, w_down, b_qkv, b_up, norm_gains, row_biases)
    grad_list = (wide_sum[:, :QKV].reshape(OWN, 3, HEAD), deep_sum[:HEAD], wide_sum[:, QKV:], deep_sum[HEAD:],
                 qkv_bias_sum, up_bias_sum, gain_sum, bias_sum)
    moments = ((m_qkv, v_qkv), (m_out, v_out), (m_up, v_up), (m_down, v_down), (m_bqkv, v_bqkv),
               (m_bup, v_bup), (m_gains, v_gains), (m_biases, v_biases))
    updated = []
    for which in range(8):
        updated.extend(adam_step(params[which], grad_list[which], moments[which][0], moments[which][1],
                                 STEP_RATES[which], DECAY_RATES[which]))
    return (out_rows, input_grad, *updated)


def solution(mesh):
    rows = P(("dp", "tensor"), None)
    qkv, out, up, down = P("dp", None, "tensor"), P("tensor", "dp"), P("dp", "tensor"), P("tensor", "dp")
    bqkv, bup = P(None, "tensor"), P("tensor")
    params = (qkv, out, up, down, bqkv, bup, P(), P())
    moments = [spec for spec in params for _ in range(2)]
    return jax.shard_map(
        local,
        mesh=mesh,
        in_specs=(rows, rows, P("dp", None), *params, *moments),
        out_specs=(rows, rows, *[spec for spec in params for _ in range(3)]),
        check_vma=False,
    )
```

```python
import functools
import math

import jax
import jax.numpy as jnp
from jax import lax
from jax.experimental import pallas as pl
from jax.experimental.pallas import tpu as pltpu
from jax.sharding import PartitionSpec as P

F32 = jnp.float32
BF16 = jnp.bfloat16
MESH = pl.DeviceIdType.MESH

D = 2048
HEAD = 256
QKV = 3 * HEAD
UNITS = 1024
WIDE = QKV + UNITS
DEEP = HEAD + UNITS
TOK = 1024
OWN = 128
TILE = 512
QROWS = 256
ROT = 64
STEP = 10

NORM_EPS = 1e-05
BETA_ONE = 0.9
BETA_TWO = 0.95
ADAM_EPS = 1e-08
STEP_RATES = (0.04, 0.2, 0.04, 0.02, 0.3, 0.3, 0.5, 0.3)
DECAY_RATES = (0.01, 0.01, 0.01, 0.01, 0.0, 0.0, 0.0, 0.0)


def place():
    dp = lax.axis_index("dp")
    tensor = lax.axis_index("tensor")
    return (
        lax.div(dp, 8),
        lax.rem(lax.div(dp, 2), 4),
        lax.rem(dp, 2),
        lax.div(tensor, 4),
        lax.rem(tensor, 4),
    )


def device(zh, y, core, zl, x):
    return ((zh * 4 + y) * 2 + core, zl * 4 + x)


def around(pos, step):
    return lax.rem(pos + step + 4, 4)


def neighbours(spot):
    zh, y, core, zl, x = spot
    return {
        "x+": device(zh, y, core, zl, around(x, 1)),
        "x-": device(zh, y, core, zl, around(x, -1)),
        "y+": device(zh, around(y, 1), core, zl, x),
        "y-": device(zh, around(y, -1), core, zl, x),
        "zl": device(zh, y, core, 1 - zl, x),
        "zh": device(1 - zh, y, core, zl, x),
        "core": device(zh, y, 1 - core, zl, x),
    }


class Links:
    def __init__(self, send_sems, recv_sems):
        self.send_sems, self.recv_sems = send_sems, recv_sems
        self.copies = []

    def send(self, src, dst, target):
        index = len(self.copies)
        copy = pltpu.make_async_remote_copy(
            src_ref=src,
            dst_ref=dst,
            send_sem=self.send_sems.at[index],
            recv_sem=self.recv_sems.at[index],
            device_id=target,
            device_id_type=MESH,
        )
        copy.start()
        self.copies.append(copy)
        return copy

    def drain(self):
        for copy in self.copies:
            copy.wait_send()


class Gather:
    def __init__(self, links, block, z, ring, z_dev, plus, minus, core=None):
        self.links, self.block, self.z, self.ring = links, block, z, ring
        self.z_dev, self.plus, self.minus, self.core = z_dev, plus, minus, core
        self.core_copies = []

    def pass_on(self, z, ring, half=None):
        if self.core is not None:
            part = self.block(z, ring, half)
            self.core_copies.append(self.links.send(part, part, self.core))

    def to(self, z, ring, half, target):
        part = self.block(z, ring, half)
        return self.links.send(part, part, target)

    def start(self):
        self.by_z = self.to(self.z, self.ring, None, self.z_dev)
        self.first = (
            self.to(self.z, self.ring, None, self.plus),
            self.to(self.z, self.ring, None, self.minus),
        )
        self.pass_on(self.z, self.ring)

    def partner(self):
        self.by_z.wait_recv()
        self.second = (
            self.to(1 - self.z, self.ring, None, self.plus),
            self.to(1 - self.z, self.ring, None, self.minus),
        )
        self.pass_on(1 - self.z, self.ring)

    def forward(self, z, copies):
        copies[0].wait_recv()
        up = self.to(z, around(self.ring, -1), 0, self.plus)
        copies[1].wait_recv()
        down = self.to(z, around(self.ring, 1), 1, self.minus)
        self.pass_on(z, around(self.ring, -1))
        self.pass_on(z, around(self.ring, 1))
        return (up, down)

    def near(self):
        self.third = self.forward(self.z, self.first)

    def far(self):
        self.fourth = self.forward(1 - self.z, self.second)

    def last(self):
        for z, copies in ((self.z, self.third), (1 - self.z, self.fourth)):
            copies[0].wait_recv()
            copies[1].wait_recv()
            self.pass_on(z, around(self.ring, 2))

    def finish(self):
        for copy in self.core_copies:
            copy.wait_recv()


def rows_of(ref, start, count):
    return ref.at[pl.ds(pl.multiple_of(start, 16), count)]


def gelu_parts(pre):
    cdf = 0.5 * (1.0 + lax.erf(pre * (1.0 / math.sqrt(2.0))))
    density = jnp.exp(-0.5 * pre * pre) * (1.0 / math.sqrt(2.0 * math.pi))
    return pre * cdf, cdf + pre * density


def spin(rows, cosines, sines, back):
    low = rows[:, :128]
    lane = lax.broadcasted_iota(jnp.int32, low.shape, 1)
    ahead = pltpu.roll(low, 96, 1)
    behind = pltpu.roll(low, 32, 1)
    turned = jnp.where(lane < 32, -ahead, jnp.where(lane < 64, behind, 0.0))
    if back:
        turned = -turned
    return jnp.concatenate([low * cosines + turned * sines, rows[:, 128:]], axis=1)


def forward_kernel(
    lens,
    x_in,
    cot_in,
    w_qkv,
    w_out,
    w_up,
    w_down,
    b_qkv,
    b_up,
    gains,
    biases,
    unit_out,
    cot_out,
    wide_out,
    deep_out,
    q_out,
    k_out,
    v_out,
    acts_out,
    slope_out,
    probs_out,
    turn_out,
    branch_out,
    unit,
    cot,
    wide,
    deep,
    q,
    k,
    v,
    acts,
    slope,
    probs,
    turn,
    branch,
    begins,
    normed,
    send_sems,
    recv_sems,
    out_sems,
):
    spot = place()
    zh, y, core, zl, x = spot
    near = neighbours(spot)
    barrier = pltpu.get_barrier_semaphore()
    for target in near.values():
        pl.semaphore_signal(barrier, inc=1, device_id=target, device_id_type=MESH)

    links = Links(send_sems, recv_sems)
    stores = []

    def store(src, dst):
        copy = pltpu.make_async_copy(src, dst, out_sems.at[len(stores)])
        copy.start()
        stores.append(copy)

    def token_block(ref):
        def block(z, ring, half):
            start = (z * 4 + ring) * OWN
            if half is None:
                return rows_of(ref, start, OWN)
            return rows_of(ref, start + half * (OWN // 2), OWN // 2)

        return block

    def wide_block(z, ring, half):
        start = ((z * 4 + ring) * 2 + core) * OWN
        if half is None:
            return rows_of(wide, start, OWN)
        return rows_of(wide, start + half * (OWN // 2), OWN // 2)

    def deep_block(z, ring, half):
        columns = pl.ds(pl.multiple_of(((z * 4 + ring) * 2 + core) * OWN, OWN), OWN)
        if half is None:
            return deep.at[:, columns]
        return deep.at[pl.ds(half * (DEEP // 2), DEEP // 2), columns]

    tensor_ends = (zl, x, near["zl"], near["x+"], near["x-"])
    data_ends = (zh, y, near["zh"], near["y+"], near["y-"], near["core"])
    units = Gather(links, token_block(unit), *tensor_ends)
    grads = Gather(links, token_block(cot), *tensor_ends)
    wides = Gather(links, wide_block, *data_ends)
    deeps = Gather(links, deep_block, *data_ends)

    rows = x_in[...].astype(F32)
    centred = rows - jnp.mean(rows, axis=-1, keepdims=True)
    variance = jnp.mean(centred * centred, axis=-1, keepdims=True)
    mine = pl.ds(pl.multiple_of((zl * 4 + x) * OWN, OWN), OWN)
    unit[mine, :] = (centred * lax.rsqrt(variance + NORM_EPS)).astype(BF16)
    own = pl.ds(pl.multiple_of(((zh * 4 + y) * 2 + core) * OWN, OWN), OWN)
    wide[own, :QKV] = w_qkv[...].astype(BF16)
    wide[own, QKV:] = w_up[...].astype(BF16)
    pl.semaphore_wait(barrier, len(near))
    units.start()
    wides.start()
    cot[mine, :] = cot_in[...]
    deep[:HEAD, own] = w_out[...].astype(BF16)
    deep[HEAD:, own] = w_down[...].astype(BF16)

    index = lax.broadcasted_iota(jnp.int32, (TOK, 128), 0)
    ends = [lens[0, 0]]
    for seq in range(1, 3):
        ends.append(ends[-1] + lens[0, seq])
    begin = jnp.zeros((TOK, 128), jnp.int32)
    for end in ends:
        begin = jnp.where(index >= end, end, begin)
    begins[...] = begin
    lane = lax.broadcasted_iota(jnp.int32, (TOK, 128), 1)
    rate = jnp.exp(lax.rem(lane, 32).astype(F32) * (-2.0 * math.log(10000.0) / ROT))
    angle = (index - begin).astype(F32) * rate
    turn[0] = jnp.where(lane < ROT, jnp.cos(angle), 1.0)
    turn[1] = jnp.where(lane < ROT, jnp.sin(angle), 0.0)
    store(turn, turn_out)

    units.partner()
    wides.partner()
    wides.near()
    units.near()
    wides.far()
    units.far()
    deeps.start()
    grads.start()
    wides.last()
    units.last()
    wides.finish()
    units.finish()
    grads.partner()
    deeps.partner()
    store(unit, unit_out)
    store(wide, wide_out)

    def project(tile, _):
        part = pl.ds(pl.multiple_of(tile * TILE, TILE), TILE)
        unit_rows = unit[part, :].astype(F32)
        normed[0] = (unit_rows * gains[0:1, :] + biases[0:1, :]).astype(BF16)
        normed[1] = (unit_rows * gains[1:2, :] + biases[1:2, :]).astype(BF16)
        cosines, sines = turn[0, part, :], turn[1, part, :]
        for which, target in enumerate((q, k, v)):
            columns = slice(which * HEAD, (which + 1) * HEAD)
            head = jnp.dot(normed[0], wide[:, columns], preferred_element_type=F32)
            head = head + b_qkv[which : which + 1, :]
            if which < 2:
                head = spin(head, cosines, sines, False)
            target[part, :] = head.astype(BF16)

        def hidden(piece, _):
            shift = pl.multiple_of(piece * 256, 256)
            pre = jnp.dot(normed[1], wide[:, pl.ds(QKV + shift, 256)], preferred_element_type=F32)
            pre = pre + b_up[0:1, pl.ds(shift, 256)]
            value, rise = gelu_parts(pre)
            acts[part, pl.ds(HEAD + shift, 256)] = value.astype(BF16)
            slope[part, pl.ds(shift, 256)] = rise.astype(BF16)
            return 0

        lax.fori_loop(0, UNITS // 256, hidden, 0)
        return 0

    project(0, 0)
    deeps.near()
    grads.near()
    project(1, 0)
    deeps.far()
    store(q, q_out)
    store(k, k_out)
    store(v, v_out)
    store(slope, slope_out)

    for block in range(TOK // QROWS):
        part = slice(block * QROWS, (block + 1) * QROWS)
        keys = (block + 1) * QROWS
        scores = lax.dot_general(
            q[part, :], k[:keys, :], (((1,), (1,)), ((), ())), preferred_element_type=F32
        ) * (HEAD**-0.5)
        key = lax.broadcasted_iota(jnp.int32, (QROWS, keys), 1)
        row = lax.broadcasted_iota(jnp.int32, (QROWS, keys), 0) + block * QROWS
        allowed = (key <= row) & (key >= begins[part, 0:1])
        scores = jnp.where(allowed, scores, -jnp.inf)
        expo = jnp.exp(scores - jnp.max(scores, axis=-1, keepdims=True))
        share = (expo / jnp.sum(expo, axis=-1, keepdims=True)).astype(BF16)
        probs[part, :keys] = share
        acts[part, :HEAD] = jnp.dot(share, v[:keys, :], preferred_element_type=F32).astype(BF16)
    store(probs, probs_out)
    store(acts, acts_out)
    grads.far()
    deeps.last()
    deeps.finish()
    store(deep, deep_out)

    def mix(tile, _):
        part = pl.ds(pl.multiple_of(tile * TILE, TILE), TILE)

        def piece(step, _):
            columns = pl.ds(pl.multiple_of(step * 256, 256), 256)
            branch[part, columns] = jnp.dot(
                acts[part, :], deep[:, columns], preferred_element_type=F32
            ).astype(BF16)
            return 0

        return lax.fori_loop(0, D // 256, piece, 0)

    lax.fori_loop(0, TOK // TILE, mix, 0)
    store(branch, branch_out)
    grads.last()
    store(cot, cot_out)
    for copy in stores:
        copy.wait()
    links.drain()


FORWARD_KEPT = (
    ((TOK, D), BF16),
    ((TOK, D), BF16),
    ((D, WIDE), BF16),
    ((DEEP, D), BF16),
    ((TOK, HEAD), BF16),
    ((TOK, HEAD), BF16),
    ((TOK, HEAD), BF16),
    ((TOK, DEEP), BF16),
    ((TOK, UNITS), BF16),
    ((TOK, TOK), BF16),
    ((2, TOK, 128), F32),
    ((TOK, D), BF16),
)


def run_forward(lens, *inputs):
    vmem = pl.BlockSpec(memory_space=pltpu.VMEM)
    return pl.pallas_call(
        forward_kernel,
        out_shape=[jax.ShapeDtypeStruct(*kept) for kept in FORWARD_KEPT],
        in_specs=[pl.BlockSpec(memory_space=pltpu.SMEM)] + [vmem] * len(inputs),
        out_specs=[pl.BlockSpec(memory_space=pl.ANY)] * len(FORWARD_KEPT),
        scratch_shapes=[pltpu.VMEM(*kept) for kept in FORWARD_KEPT]
        + [
            pltpu.VMEM((TOK, 128), jnp.int32),
            pltpu.VMEM((2, TILE, D), BF16),
            pltpu.SemaphoreType.DMA((64,)),
            pltpu.SemaphoreType.DMA((64,)),
            pltpu.SemaphoreType.DMA((len(FORWARD_KEPT),)),
        ],
        compiler_params=pltpu.CompilerParams(
            collective_id=0, has_side_effects=True, vmem_limit_bytes=60 * 2**20
        ),
        cost_estimate=pl.CostEstimate(flops=14 * 10**9, bytes_accessed=40 * 10**6, transcendentals=0),
        name="forward",
    )(lens, *inputs)


def over_rows(left, right):
    return lax.dot_general(left, right, (((0,), (0,)), ((), ())), preferred_element_type=F32)


def by_rows(left, right):
    return lax.dot_general(left, right, (((1,), (1,)), ((), ())), preferred_element_type=F32)


class Scatter:
    def __init__(self, links, part, slots, last, z, ring, z_dev, plus, minus):
        self.links, self.part, self.slots, self.last = links, part, slots, last
        self.ring, self.z_dev, self.plus, self.minus = ring, z_dev, plus, minus
        self.zs = (1 - z, z)
        self.sent = {}

    def push(self, way, message, order, ring, half):
        self.sent[way, message, order] = self.links.send(
            self.part(self.zs[order], ring, half),
            self.slots.at[way, message, order],
            self.minus if way else self.plus,
        )

    def arrived(self, way, message, order):
        self.sent[way, message, order].wait_recv()
        return self.slots[way, message, order].astype(F32)

    def far(self):
        for order in range(2):
            self.push(0, 0, order, around(self.ring, 2), 0)
            self.push(1, 0, order, around(self.ring, 2), 1)

    def near(self, way):
        for order in range(2):
            self.push(way, 1, order, around(self.ring, -1 if way else 1), 1 - way)

    def join(self, order):
        for way in range(2):
            ring = around(self.ring, -1 if way else 1)
            part = self.part(self.zs[order], ring, way)
            part[...] = (part[...].astype(F32) + self.arrived(way, 0, order)).astype(BF16)
            self.push(way, 2, order, ring, way)

    def total(self, order, half):
        part = self.part(self.zs[order], self.ring, half)
        return (
            part[...].astype(F32) + self.arrived(half, 2, order) + self.arrived(1 - half, 1, order)
        )

    def partner(self):
        for half in range(2):
            part = self.part(self.zs[0], self.ring, half)
            part[...] = self.total(0, half).astype(BF16)
        self.by_z = self.links.send(
            self.part(self.zs[0], self.ring, None), self.last, self.z_dev
        )

    def finish(self, out):
        sums = [self.total(1, half) for half in range(2)]
        self.by_z.wait_recv()
        rows = out.shape[0] // 2
        for half in range(2):
            part = pl.ds(half * rows, rows)
            out[part, :] = sums[half] + self.last[part, :].astype(F32)


def backward_kernel(
    unit_in,
    cot_in,
    wide_in,
    deep_in,
    q_in,
    k_in,
    v_in,
    acts_in,
    slope_in,
    probs_in,
    turn_in,
    branch_in,
    gains,
    biases,
    branch_sum,
    unit_sum,
    wide_sum,
    deep_sum,
    vector_sum,
    unit,
    cot,
    wide,
    deep,
    q,
    k,
    v,
    acts,
    probs,
    turn,
    branch,
    grads,
    mixed_grad,
    pair,
    normed,
    sums,
    low_sums,
    vectors,
    vector_slots,
    wide_core,
    deep_core,
    wide_slots,
    deep_slots,
    branch_slots,
    unit_slots,
    wide_last,
    deep_last,
    branch_last,
    unit_last,
    row_total,
    wide_total,
    deep_total,
    send_sems,
    recv_sems,
    core_send,
    core_recv,
    load_sems,
    store_sems,
):
    spot = place()
    zh, y, core, zl, x = spot
    near = neighbours(spot)
    near["x2"] = device(zh, y, core, zl, around(x, 2))
    near["y2"] = device(zh, around(y, 2), core, zl, x)
    barrier = pltpu.get_barrier_semaphore()
    for target in near.values():
        pl.semaphore_signal(barrier, inc=1, device_id=target, device_id_type=MESH)

    loads = {}
    for name, src, dst in (
        ("branch", branch_in, branch),
        ("cot", cot_in, cot),
        ("deep", deep_in, deep),
        ("slope", slope_in, grads.at[:, pl.ds(QKV, UNITS)]),
        ("acts", acts_in, acts),
        ("probs", probs_in, probs),
        ("v", v_in, v),
        ("k", k_in, k),
        ("q", q_in, q),
        ("turn", turn_in, turn),
        ("unit", unit_in, unit),
        ("wide", wide_in, wide),
    ):
        loads[name] = pltpu.make_async_copy(src, dst, load_sems.at[len(loads)])
        loads[name].start()

    links = Links(send_sems, recv_sems)
    stores = []

    def store(src, dst):
        copy = pltpu.make_async_copy(src, dst, store_sems.at[len(stores)])
        copy.start()
        stores.append(copy)
        return copy

    def token_part(ref):
        def part(z, ring, half):
            start = (z * 4 + ring) * OWN
            if half is None:
                return rows_of(ref, start, OWN)
            return rows_of(ref, start + half * (OWN // 2), OWN // 2)

        return part

    def wide_part(z, ring, half):
        start = ((z * 4 + ring) * 2 + core) * OWN
        if half is None:
            return rows_of(wide, start, OWN)
        return rows_of(wide, start + half * (OWN // 2), OWN // 2)

    def deep_part(z, ring, half):
        columns = pl.ds(pl.multiple_of(((z * 4 + ring) * 2 + core) * OWN, OWN), OWN)
        if half is None:
            return deep.at[:, columns]
        return deep.at[pl.ds(half * (DEEP // 2), DEEP // 2), columns]

    tensor_ends = (zl, x, near["zl"], near["x+"], near["x-"])
    data_ends = (zh, y, near["zh"], near["y+"], near["y-"])
    branches = Scatter(links, token_part(branch), branch_slots, branch_last, *tensor_ends)
    units = Scatter(links, token_part(cot), unit_slots, unit_last, *tensor_ends)
    wides = Scatter(links, wide_part, wide_slots, wide_last, *data_ends)
    deeps = Scatter(links, deep_part, deep_slots, deep_last, *data_ends)

    def core_copy(which, buffer, slots, place_of, ring, turn_of):
        number = which * 8 + ring * 2 + turn_of
        z = zh + (1 - 2 * zh) * turn_of
        chip = z * 4 + around(y, ring)
        return pltpu.make_async_remote_copy(
            src_ref=place_of(buffer, chip, 1 - core),
            dst_ref=slots.at[ring * 2 + turn_of],
            send_sem=core_send.at[number],
            recv_sem=core_recv.at[number],
            device_id=near["core"],
            device_id_type=MESH,
        )

    def deep_place(ref, chip, who):
        return ref.at[:, pl.ds(pl.multiple_of((chip * 2 + who) * OWN, OWN), OWN)]

    def wide_place(ref, chip, who):
        return rows_of(ref, (chip * 2 + who) * OWN, OWN)

    def core_add(which, buffer, slots, place_of, ring):
        def one(turn_of, _):
            core_copy(which, buffer, slots, place_of, ring, turn_of).wait_recv()
            z = zh + (1 - 2 * zh) * turn_of
            mine = place_of(buffer, z * 4 + around(y, ring), core)
            mine[...] = (
                mine[...].astype(F32) + slots[ring * 2 + turn_of].astype(F32)
            ).astype(BF16)
            return 0

        lax.fori_loop(0, 2, one, 0)

    pl.semaphore_wait(barrier, len(near))
    loads["branch"].wait()
    branches.far()

    sums[...] = jnp.zeros_like(sums)
    low_sums[...] = jnp.zeros_like(low_sums)
    for name in ("cot", "deep", "slope"):
        loads[name].wait()

    def back(tile, _):
        part = pl.ds(pl.multiple_of(tile * TILE, TILE), TILE)
        mixed_grad[part, :] = by_rows(cot[part, :], deep[:HEAD, :]).astype(BF16)

        def hidden(piece, _):
            shift = pl.multiple_of(piece * 256, 256)
            columns = pl.ds(QKV + shift, 256)
            grad = by_rows(cot[part, :], deep[pl.ds(HEAD + shift, 256), :])
            grad = grad * grads[part, columns].astype(F32)
            low_sums[0:1, columns] += jnp.sum(grad, axis=0, keepdims=True)
            grads[part, columns] = grad.astype(BF16)
            return 0

        return lax.fori_loop(0, UNITS // 256, hidden, 0)

    lax.fori_loop(0, TOK // TILE, back, 0)
    branches.near(0)
    branches.near(1)
    loads["acts"].wait()

    for index, ring in enumerate((2, 1, 3, 0)):

        def deep_tile(turn_of, _):
            z = zh + (1 - 2 * zh) * turn_of
            columns = pl.ds(pl.multiple_of((z * 4 + around(y, ring)) * 256, 256), 256)
            deep[:, columns] = over_rows(acts[...], cot[:, columns]).astype(BF16)
            core_copy(0, deep, deep_core, deep_place, ring, turn_of).start()
            return 0

        lax.fori_loop(0, 2, deep_tile, 0)
        if index == 1:
            core_add(0, deep, deep_core, deep_place, 2)
            deeps.far()
        elif index == 2:
            core_add(0, deep, deep_core, deep_place, 1)
            deeps.near(0)
        elif index == 3:
            core_add(0, deep, deep_core, deep_place, 3)
            deeps.near(1)
    mine = pl.ds(pl.multiple_of((zl * 4 + x) * OWN, OWN), OWN)
    sums[4:5, :] = jnp.sum(cot[mine, :].astype(F32), axis=0, keepdims=True)
    core_add(0, deep, deep_core, deep_place, 0)
    branches.join(0)
    branches.join(1)

    for name in ("probs", "v", "k", "q", "turn"):
        loads[name].wait()
    for block in range(TOK // QROWS):
        part = slice(block * QROWS, (block + 1) * QROWS)
        grad = over_rows(probs[block * QROWS :, part], mixed_grad[block * QROWS :, :])
        low_sums[0:1, 2 * HEAD : QKV] += jnp.sum(grad, axis=0, keepdims=True)
        grads[part, 2 * HEAD : QKV] = grad.astype(BF16)
    for block in range(TOK // QROWS):
        part = slice(block * QROWS, (block + 1) * QROWS)
        keys = (block + 1) * QROWS
        share = probs[part, :keys].astype(F32)
        prob_grad = by_rows(mixed_grad[part, :], v[:keys, :])
        delta = jnp.sum(share * prob_grad, axis=-1, keepdims=True)
        score_grad = (share * (prob_grad - delta)).astype(BF16)
        probs[part, :keys] = score_grad
        grad = jnp.dot(score_grad, k[:keys, :], preferred_element_type=F32) * (HEAD**-0.5)
        grad = spin(grad, turn[0, part, :], turn[1, part, :], True)
        low_sums[0:1, :HEAD] += jnp.sum(grad, axis=0, keepdims=True)
        grads[part, :HEAD] = grad.astype(BF16)
    for block in range(TOK // QROWS):
        part = slice(block * QROWS, (block + 1) * QROWS)
        grad = over_rows(probs[block * QROWS :, part], q[block * QROWS :, :]) * (HEAD**-0.5)
        grad = spin(grad, turn[0, part, :], turn[1, part, :], True)
        low_sums[0:1, HEAD : 2 * HEAD] += jnp.sum(grad, axis=0, keepdims=True)
        grads[part, HEAD : 2 * HEAD] = grad.astype(BF16)
    deeps.join(0)
    deeps.join(1)
    loads["unit"].wait()
    loads["wide"].wait()

    for ring in (2, 1, 3, 0):
        starts = (around(x, ring) * OWN, (4 + around(x, ring)) * OWN)
        pieces = [pl.ds(pl.multiple_of(start, OWN), OWN) for start in starts]
        for half in range(2):
            pair[half * OWN : (half + 1) * OWN, :] = grads[pieces[half], :]

        def unit_tile(step, _):
            columns = pl.ds(pl.multiple_of(step * 512, 512), 512)
            first = by_rows(pair[:, :QKV], wide[columns, :QKV])
            second = by_rows(pair[:, QKV:], wide[columns, QKV:])
            rows = jnp.concatenate([unit[piece, columns] for piece in pieces], axis=0).astype(F32)
            sums[0:1, columns] += jnp.sum(first * rows, axis=0, keepdims=True)
            sums[1:2, columns] += jnp.sum(second * rows, axis=0, keepdims=True)
            sums[2:3, columns] += jnp.sum(first, axis=0, keepdims=True)
            sums[3:4, columns] += jnp.sum(second, axis=0, keepdims=True)
            both = (first * gains[0:1, columns] + second * gains[1:2, columns]).astype(BF16)
            cot[pieces[0], columns] = both[:OWN]
            cot[pieces[1], columns] = both[OWN:]
            return 0

        lax.fori_loop(0, D // 512, unit_tile, 0)
        if ring == 2:
            units.far()
        elif ring != 0:
            units.near(0 if ring == 1 else 1)
    deeps.partner()

    for row in range(5):
        for column in range(16):
            vectors[0, row * 16 + column : row * 16 + column + 1, :] = sums[
                row : row + 1, column * 128 : (column + 1) * 128
            ]
    for column in range(14):
        vectors[0, 80 + column : 81 + column, :] = low_sums[0:1, column * 128 : (column + 1) * 128]
    vectors[0, 94:96, :] = jnp.zeros((2, 128), F32)

    def swap(stage, first_slot, names, count):
        rows = pl.ds(0, count)
        return [
            links.send(
                vectors.at[stage, rows], vector_slots.at[first_slot + index, rows], near[name]
            )
            for index, name in enumerate(names)
        ]

    def combine(stage, first_slot, copies, count):
        for copy in copies:
            copy.wait_recv()
        parts = [vectors[stage, :count, :]]
        parts += [vector_slots[first_slot + index, :count, :] for index in range(len(copies))]
        if len(parts) == 2:
            result = parts[0] + parts[1]
        else:
            result = (parts[0] + parts[3]) + (parts[1] + parts[2])
        vectors[stage + 1, :count, :] = result

    moving = swap(0, 0, ("core",), 96)

    for index, ring in enumerate((2, 1, 3, 0)):

        def wide_tile(turn_of, _):
            z = zh + (1 - 2 * zh) * turn_of
            span = pl.ds(pl.multiple_of((z * 4 + around(y, ring)) * 256, 256), 256)
            rows = unit[:, span].astype(F32)
            normed[0] = (rows * gains[0:1, span] + biases[0:1, span]).astype(BF16)
            normed[1] = (rows * gains[1:2, span] + biases[1:2, span]).astype(BF16)
            wide[span, :QKV] = over_rows(normed[0], grads[:, :QKV]).astype(BF16)
            wide[span, QKV:] = over_rows(normed[1], grads[:, QKV:]).astype(BF16)
            core_copy(1, wide, wide_core, wide_place, ring, turn_of).start()
            return 0

        lax.fori_loop(0, 2, wide_tile, 0)
        if index == 0:
            combine(0, 0, moving, 96)
            moving = swap(1, 1, ("y+", "y-", "y2"), 96)
        elif index == 1:
            core_add(1, wide, wide_core, wide_place, 2)
            wides.far()
            combine(1, 1, moving, 96)
            moving = swap(2, 4, ("zh",), 96)
        elif index == 2:
            core_add(1, wide, wide_core, wide_place, 1)
            wides.near(0)
            combine(2, 4, moving, 96)
            store(vectors.at[3, pl.ds(80, 16)], vector_sum.at[pl.ds(80, 16)])
            moving = swap(3, 5, ("zl",), 80)
            branches.partner()
        elif index == 3:
            core_add(1, wide, wide_core, wide_place, 3)
            wides.near(1)
            combine(3, 5, moving, 80)
            moving = swap(4, 6, ("x+", "x-", "x2"), 80)
    core_add(1, wide, wide_core, wide_place, 0)
    deeps.finish(deep_total)
    store(deep_total, deep_sum)
    units.join(0)
    wides.join(0)
    units.join(1)
    wides.join(1)
    combine(4, 6, moving, 80)
    store(vectors.at[5, pl.ds(0, 80)], vector_sum.at[pl.ds(0, 80)])
    branches.finish(row_total)
    branch_store = store(row_total, branch_sum)
    wides.partner()
    units.partner()
    wides.finish(wide_total)
    store(wide_total, wide_sum)
    branch_store.wait()
    units.finish(row_total)
    store(row_total, unit_sum)

    for which, buffer, slots, place_of in (
        (0, deep, deep_core, deep_place),
        (1, wide, wide_core, wide_place),
    ):
        for ring in range(4):
            for turn_of in range(2):
                core_copy(which, buffer, slots, place_of, ring, turn_of).wait_send()
    for copy in stores:
        if copy is not branch_store:
            copy.wait()
    links.drain()


SUMS = (
    ((OWN, D), F32),
    ((OWN, D), F32),
    ((OWN, WIDE), F32),
    ((DEEP, OWN), F32),
    ((96, 128), F32),
)


def run_backward(kept, gains, biases):
    anywhere = pl.BlockSpec(memory_space=pl.ANY)
    vmem = pl.BlockSpec(memory_space=pltpu.VMEM)
    half = OWN // 2
    return pl.pallas_call(
        backward_kernel,
        out_shape=[jax.ShapeDtypeStruct(*each) for each in SUMS],
        in_specs=[anywhere] * len(kept) + [vmem, vmem],
        out_specs=[anywhere] * len(SUMS),
        scratch_shapes=[
            pltpu.VMEM((TOK, D), BF16),
            pltpu.VMEM((TOK, D), BF16),
            pltpu.VMEM((D, WIDE), BF16),
            pltpu.VMEM((DEEP, D), BF16),
            pltpu.VMEM((TOK, HEAD), BF16),
            pltpu.VMEM((TOK, HEAD), BF16),
            pltpu.VMEM((TOK, HEAD), BF16),
            pltpu.VMEM((TOK, DEEP), BF16),
            pltpu.VMEM((TOK, TOK), BF16),
            pltpu.VMEM((2, TOK, 128), F32),
            pltpu.VMEM((TOK, D), BF16),
            pltpu.VMEM((TOK, WIDE), BF16),
            pltpu.VMEM((TOK, HEAD), BF16),
            pltpu.VMEM((2 * OWN, WIDE), BF16),
            pltpu.VMEM((2, TOK, 256), BF16),
            pltpu.VMEM((8, D), F32),
            pltpu.VMEM((8, WIDE), F32),
            pltpu.VMEM((6, 96, 128), F32),
            pltpu.VMEM((9, 96, 128), F32),
            pltpu.VMEM((8, OWN, WIDE), BF16),
            pltpu.VMEM((8, DEEP, OWN), BF16),
            pltpu.VMEM((2, 3, 2, half, WIDE), BF16),
            pltpu.VMEM((2, 3, 2, DEEP // 2, OWN), BF16),
            pltpu.VMEM((2, 3, 2, half, D), BF16),
            pltpu.VMEM((2, 3, 2, half, D), BF16),
            pltpu.VMEM((OWN, WIDE), BF16),
            pltpu.VMEM((DEEP, OWN), BF16),
            pltpu.VMEM((OWN, D), BF16),
            pltpu.VMEM((OWN, D), BF16),
            pltpu.VMEM((OWN, D), F32),
            pltpu.VMEM((OWN, WIDE), F32),
            pltpu.VMEM((DEEP, OWN), F32),
            pltpu.SemaphoreType.DMA((64,)),
            pltpu.SemaphoreType.DMA((64,)),
            pltpu.SemaphoreType.DMA((16,)),
            pltpu.SemaphoreType.DMA((16,)),
            pltpu.SemaphoreType.DMA((len(kept),)),
            pltpu.SemaphoreType.DMA((8,)),
        ],
        compiler_params=pltpu.CompilerParams(
            collective_id=1, has_side_effects=True, vmem_limit_bytes=63 * 2**20
        ),
        cost_estimate=pl.CostEstimate(flops=28 * 10**9, bytes_accessed=40 * 10**6, transcendentals=0),
        name="backward",
    )(*kept, gains, biases)


def adam_step(weight, gradient, moment_one, moment_two, step_rate, decay_rate):
    moment_one = BETA_ONE * moment_one + (1.0 - BETA_ONE) * gradient
    moment_two = BETA_TWO * moment_two + (1.0 - BETA_TWO) * gradient * gradient
    ratio = (
        moment_one
        / (1.0 - BETA_ONE**STEP)
        / (jnp.sqrt(moment_two / (1.0 - BETA_TWO**STEP)) + ADAM_EPS)
    )
    return (moment_one, moment_two, weight - step_rate * (ratio + decay_rate * weight))


def local(layer_in, cotangent, seq_lengths, *state):
    params, moments = state[:8], state[8:]
    w_qkv, w_out, w_up, w_down, b_qkv, b_up, norm_gains, row_biases = params
    resid = layer_in.astype(F32)
    centered = resid - jnp.mean(resid, axis=-1, keepdims=True)
    variance = jnp.mean(centered * centered, axis=-1, keepdims=True)
    inverse = lax.rsqrt(variance + NORM_EPS)
    own_unit = centered * inverse
    kept = run_forward(
        seq_lengths,
        layer_in,
        cotangent,
        w_qkv.reshape(OWN, QKV),
        w_out,
        w_up,
        w_down,
        b_qkv,
        b_up.reshape(1, UNITS),
        norm_gains,
        row_biases,
    )
    branch, unit_grad, wide_sum, deep_sum, vector_sum = run_backward(kept, norm_gains, row_biases)
    out_rows = (resid + branch + row_biases[2] + row_biases[3]).astype(BF16)
    unit_mean = jnp.mean(unit_grad, axis=-1, keepdims=True)
    unit_proj = jnp.mean(unit_grad * own_unit, axis=-1, keepdims=True)
    input_grad = cotangent.astype(F32) + inverse * (unit_grad - unit_mean - own_unit * unit_proj)
    vectors = vector_sum[:80].reshape(5, D)
    low_vectors = vector_sum[80:94].reshape(WIDE)
    grad_list = (
        wide_sum[:, :QKV].reshape(OWN, 3, HEAD),
        deep_sum[:HEAD],
        wide_sum[:, QKV:],
        deep_sum[HEAD:],
        low_vectors[:QKV].reshape(3, HEAD),
        low_vectors[QKV:],
        vectors[:2],
        jnp.concatenate([vectors[2:5], vectors[4:5]], axis=0),
    )
    updated = []
    for which in range(8):
        updated.extend(
            adam_step(
                params[which],
                grad_list[which],
                moments[2 * which],
                moments[2 * which + 1],
                STEP_RATES[which],
                DECAY_RATES[which],
            )
        )
    return (out_rows, input_grad, *updated)


def solution(mesh):
    rows = P(("dp", "tensor"), None)
    out, up = P("tensor", "dp"), P("dp", "tensor")
    params = (P("dp", None, "tensor"), out, up, out, P(None, "tensor"), P("tensor"), P(), P())
    moments = [spec for spec in params for _ in range(2)]
    return jax.shard_map(
        local,
        mesh=mesh,
        in_specs=(rows, rows, P("dp", None), *params, *moments),
        out_specs=(rows, rows, *[spec for spec in params for _ in range(3)]),
        check_vma=False,
    )
```

```python
import functools
import math

import jax
import jax.numpy as jnp
from jax import lax
from jax.experimental import pallas as pl
from jax.experimental.pallas import tpu as pltpu
from jax.sharding import PartitionSpec as P

F32 = jnp.float32
BF16 = jnp.bfloat16
MESH = pl.DeviceIdType.MESH

D = 2048
HEAD = 256
QKV = 3 * HEAD
UNITS = 1024
WIDE = QKV + UNITS
DEEP = HEAD + UNITS
TOK = 1024
OWN = 128
TILE = 512
MAIN_UNIT, MAIN_COT, MAIN_BRANCH, MAIN_GRAD = 1664, 1408, 1664, 1664
QROWS = 256
ROT = 64
STEP = 10

NORM_EPS = 1e-05
BETA_ONE = 0.9
BETA_TWO = 0.95
ADAM_EPS = 1e-08
STEP_RATES = (0.04, 0.2, 0.04, 0.02, 0.3, 0.3, 0.5, 0.3)
DECAY_RATES = (0.01, 0.01, 0.01, 0.01, 0.0, 0.0, 0.0, 0.0)


def place():
    dp = lax.axis_index("dp")
    tensor = lax.axis_index("tensor")
    return (
        lax.div(dp, 8),
        lax.rem(lax.div(dp, 2), 4),
        lax.rem(dp, 2),
        lax.div(tensor, 4),
        lax.rem(tensor, 4),
    )


def device(zh, y, core, zl, x):
    return ((zh * 4 + y) * 2 + core, zl * 4 + x)


def around(pos, step):
    return lax.rem(pos + step + 4, 4)


def neighbours(spot):
    zh, y, core, zl, x = spot
    return {
        "x+": device(zh, y, core, zl, around(x, 1)),
        "x-": device(zh, y, core, zl, around(x, -1)),
        "y+": device(zh, around(y, 1), core, zl, x),
        "y-": device(zh, around(y, -1), core, zl, x),
        "zl": device(zh, y, core, 1 - zl, x),
        "zh": device(1 - zh, y, core, zl, x),
        "core": device(zh, y, 1 - core, zl, x),
    }


class Links:
    def __init__(self, send_sems, recv_sems):
        self.send_sems, self.recv_sems = send_sems, recv_sems
        self.copies, self.open = [], []

    def send(self, src, dst, target):
        index = len(self.copies)
        copy = pltpu.make_async_remote_copy(
            src_ref=src,
            dst_ref=dst,
            send_sem=self.send_sems.at[index],
            recv_sem=self.recv_sems.at[index],
            device_id=target,
            device_id_type=MESH,
        )
        copy.start()
        self.copies.append(copy)
        self.open.append(copy)
        return copy

    def settle(self, copies):
        for copy in copies:
            copy.wait_send()
        self.open = [each for each in self.open if not any(each is copy for copy in copies)]


class Gather:
    def __init__(self, links, block, z, ring, z_dev, plus, minus, onward):
        self.links, self.block, self.z, self.ring = links, block, z, ring
        self.z_dev, self.ways, self.onward = z_dev, (plus, minus), onward
        self.by_z, self.sent = None, []

    def to(self, z, ring, half, target):
        part = self.block(z, ring, half)
        self.sent.append(self.links.send(part, part, target))
        return self.sent[-1]

    def round(self, z):
        passed = []

        def pass_on(ring):
            if self.onward is not None:
                passed.append(self.to(z, ring, None, self.onward))

        whole = [self.to(z, self.ring, None, way) for way in self.ways]
        pass_on(self.ring)
        halves = []
        for way in range(2):
            yield [whole[way]]
            whole[way].wait_recv()
            from_ring = around(self.ring, 1 if way else -1)
            halves.append(self.to(z, from_ring, way, self.ways[way]))
            pass_on(from_ring)
        yield halves
        for copy in halves:
            copy.wait_recv()
        pass_on(around(self.ring, 2))
        yield passed
        for copy in passed:
            copy.wait_recv()

    def own(self, gate):
        yield [gate]
        if self.z_dev is not None:
            self.by_z = self.to(self.z, self.ring, None, self.z_dev)
        yield from self.round(self.z)

    def far(self, gate):
        yield [gate]
        yield [self.by_z]
        self.by_z.wait_recv()
        yield from self.round(1 - self.z)


class Scatter:
    def __init__(self, links, part, slots, last, z, ring, z_dev, plus, minus):
        self.links, self.part, self.slots, self.last = links, part, slots, last
        self.ring, self.z_dev, self.ways = ring, z_dev, (plus, minus)
        self.zs = (z,) if last is None else (1 - z, z)
        self.sent = {}

    def push(self, way, message, order, ring, half):
        self.sent[way, message, order] = self.links.send(
            self.part(self.zs[order], ring, half),
            self.slots.at[way, message, order],
            self.ways[way],
        )

    def arrived(self, way, message, order):
        self.sent[way, message, order].wait_recv()
        return self.slots[way, message, order].astype(F32)

    def total(self, order, half):
        part = self.part(self.zs[order], self.ring, half)
        return (
            part[...].astype(F32) + self.arrived(half, 2, order) + self.arrived(1 - half, 1, order)
        )

    def feed(self, name, done):
        yield [(name, 2)]
        for order in range(len(self.zs)):
            for way in range(2):
                self.push(way, 0, order, around(self.ring, 2), way)
        for way, step in ((0, 1), (1, 3)):
            yield [(name, step)]
            for order in range(len(self.zs)):
                self.push(way, 1, order, around(self.ring, step), 1 - way)
        done.add((name, "fed"))

    def run(self, name, out, gate):
        yield [(name, "fed")]
        for order in range(len(self.zs)):
            for way in range(2):
                yield [self.sent[way, 0, order]]
                ring = around(self.ring, -1 if way else 1)
                part = self.part(self.zs[order], ring, way)
                part[...] = (part[...].astype(F32) + self.arrived(way, 0, order)).astype(BF16)
                self.push(way, 2, order, ring, way)
        by_z = None
        if self.last is not None:
            yield [(name, 0)] + [self.sent[way, each, 0] for way in range(2) for each in (1, 2)]
            for half in range(2):
                part = self.part(self.zs[0], self.ring, half)
                part[...] = self.total(0, half).astype(BF16)
            by_z = self.links.send(self.part(self.zs[0], self.ring, None), self.last, self.z_dev)
        order = len(self.zs) - 1
        yield [(name, 0), gate] + [
            self.sent[way, each, order] for way in range(2) for each in (1, 2)
        ]
        rows = out.shape[0] // 2
        for half in range(2):
            out[pl.ds(half * rows, rows), :] = self.total(order, half)
        if by_z is not None:
            yield [by_z]
            by_z.wait_recv()
            out[...] = out[...] + self.last[...].astype(F32)


class PairSum:
    def __init__(self, links, part, slots, z, ring, z_dev):
        self.links, self.part, self.slots = links, part, slots
        self.z, self.ring, self.z_dev = z, ring, z_dev

    def run(self, name, flag, done):
        for step in (2, 1, 3, 0):
            yield [(name, step)]
            part = self.part(1 - self.z, around(self.ring, step), None)
            moved = self.links.send(part, self.slots.at[step], self.z_dev)
            yield [moved]
            moved.wait_recv()
            part = self.part(self.z, around(self.ring, step), None)
            part[...] = (part[...].astype(F32) + self.slots[step].astype(F32)).astype(BF16)
            done.add((flag, step))


def rows_of(ref, start, count):
    return ref.at[pl.ds(pl.multiple_of(start, 16), count)]


def row_part(ref, first, count, core=None):
    def part(z, ring, half):
        index, rows = z * 4 + ring, OWN
        if core is not None:
            index = index * 2 + core
        start = index * OWN
        if half is not None:
            start, rows = start + half * (OWN // 2), OWN // 2
        return ref.at[pl.ds(pl.multiple_of(start, 16), rows), pl.ds(first, count)]

    return part


def over_rows(left, right):
    return lax.dot_general(left, right, (((0,), (0,)), ((), ())), preferred_element_type=F32)


def by_rows(left, right):
    return lax.dot_general(left, right, (((1,), (1,)), ((), ())), preferred_element_type=F32)


def gelu_parts(pre):
    cdf = 0.5 * (1.0 + lax.erf(pre * (1.0 / math.sqrt(2.0))))
    density = jnp.exp(-0.5 * pre * pre) * (1.0 / math.sqrt(2.0 * math.pi))
    return pre * cdf, cdf + pre * density


def spin(rows, cosines, sines, back):
    low = rows[:, :128]
    lane = lax.broadcasted_iota(jnp.int32, low.shape, 1)
    ahead = pltpu.roll(low, 96, 1)
    behind = pltpu.roll(low, 32, 1)
    turned = jnp.where(lane < 32, -ahead, jnp.where(lane < 64, behind, 0.0))
    if back:
        turned = -turned
    return jnp.concatenate([low * cosines + turned * sines, rows[:, 128:]], axis=1)


ORDER = (
    ".init", "unit_side", "unit", "unit_far", ".weights", "wide", "wup", "wup_far", "wide_far", ".tables",
    "unit_side", "unit_side", "wide", "wide", "wup", "wup", "unit_far", "unit", "unit", "unit_side", "wide", "wide",
    "wup", "wide_far", "wup", "wide_far", "wide_far", "wup_far", "deep", "deep_far", "unit_far", "unit_far", "cot",
    "cot_far", "cot_side", "wide_far", "wide_far", "unit", "unit", "unit_side", "wup_far", "wup_far", "unit_far",
    "unit_far", ".qkv0", ".qkv1", "deep_far", ".att0", ".att1", "deep", "deep", ".att2", "cot", "cot", ".att3",
    "wup_far", "cot_side", "cot_side", "cot_far", "wup_far", ".hid0a", ".hid0b", "cot", "cot", "cot_side", "deep_far",
    "deep_far", ".hid1a", "deep", ".hid1b", "deep", "deep_far", "cot_far", "cot_far", "deep_far", ".mix2", "cot_side",
    "branch_feed", "branch_pair", ".mix1", "branch_feed", ".mix3", "branch_feed", "branch", ".mix0", "cot_far",
    "cot_far", "branch_pair", "branch_pair", "branch_side_feed", ".back0a", ".back0b", "branch", "branch",
    "branch_pair", "branch_pair", "branch_side_feed", ".back1a", ".back1b", "branch_pair", "branch_pair",
    "branch_side_feed", "branch_side", ".deepg2", "branch", "branch", "deep_share", ".deepg1", "branch_pair",
    ".deepg3", "deep_share", "deep_share", "deep_share", "deep_share", "deep_grad_feed", "deep_grad_feed", ".deepg0",
    "deep_share", "deep_share", "deep_grad_feed", "deep_grad", ".dv", ".dp0", "deep_share", ".dp1", "deep_grad",
    "deep_grad", "branch_side", "branch_side", ".dp2", ".dp3", "deep_grad", "branch", "deep_grad", ".dk", ".g2",
    "unit_grad_feed", "unit_grad_pair", ".g1", "branch", "unit_grad_feed", "branch_side", ".g3", "unit_grad_feed",
    "unit_grad", ".g0", "branch", "unit_grad", "unit_grad", "deep_grad", "unit_grad_pair", "unit_grad_pair",
    "unit_grad_side_feed", ".pack", "vector", ".upg2", "deep_grad", "up_share", "vector", ".upg1", "unit_grad",
    "unit_grad", "up_share", "up_share", "up_grad_feed", ".upg3", "up_share", "up_share", "up_grad_feed", "vector",
    ".upg0", ".qg2", "deep_grad", "up_share", "up_share", "up_grad_feed", "up_grad", "up_grad", "up_grad",
    "qkv_share", ".qg1", "up_share", "qkv_share", "qkv_share", "qkv_grad_feed", "unit_grad_pair", "unit_grad_pair",
    "unit_grad_side_feed", ".qg3", "up_grad", "up_grad", "qkv_share", "qkv_share", "qkv_grad_feed", "vector", ".qg0",
    ".branch_out", "qkv_share", "qkv_share", "qkv_grad_feed", "qkv_grad", "unit_grad_pair", "unit_grad_pair",
    "unit_grad_side_feed", "unit_grad_side", "vector", "qkv_share", "unit_grad", "unit_grad_side", "unit_grad_pair",
    "unit_grad_side", "up_grad", "qkv_grad", "qkv_grad", "unit_grad", "qkv_grad", "qkv_grad", "vector",
    "unit_grad_side", "up_grad", "unit_grad", "up_grad", "qkv_grad", "qkv_grad", "qkv_grad",
)


def layer_kernel(
    lens,
    x_in,
    cot_in,
    w_qkv,
    w_out,
    w_up,
    w_down,
    b_qkv,
    b_up,
    gains,
    biases,
    branch_sum,
    unit_sum,
    qkv_sum,
    up_sum,
    deep_sum,
    vector_sum,
    low_sum,
    unit,
    cot,
    wide,
    deep,
    up,
    q,
    k,
    v,
    acts,
    probs,
    branch,
    grads,
    mixed_grad,
    sums,
    low_sums,
    vectors,
    vector_slots,
    up_core,
    deep_core,
    qkv_slots,
    up_slots,
    deep_slots,
    branch_slots,
    unit_slots,
    branch_side_slots,
    unit_side_slots,
    branch_pairs,
    unit_pairs,
    qkv_last,
    up_last,
    deep_last,
    branch_last,
    unit_last,
    row_total,
    qkv_total,
    up_total,
    deep_total,
    send_sems,
    recv_sems,
    core_send,
    core_recv,
    load_sems,
    store_sems,
):
    spot = place()
    zh, y, core, zl, x = spot
    near = neighbours(spot)
    near["x2"] = device(zh, y, core, zl, around(x, 2))
    near["y2"] = device(zh, around(y, 2), core, zl, x)
    barrier = pltpu.get_barrier_semaphore()
    for target in near.values():
        pl.semaphore_signal(barrier, inc=1, device_id=target, device_id_type=MESH)

    mine = pl.ds(pl.multiple_of((zl * 4 + x) * OWN, OWN), OWN)
    own = pl.ds(pl.multiple_of(((zh * 4 + y) * 2 + core) * OWN, OWN), OWN)
    loads = []
    for src, dst in (
        (x_in, unit.at[mine, :]),
        *((w_qkv.at[head], qkv_total.at[:, pl.ds(head * HEAD, HEAD)]) for head in range(3)),
        (w_up, up_total),
        (w_out, deep_total.at[pl.ds(0, HEAD), :]),
        (w_down, deep_total.at[pl.ds(HEAD, UNITS), :]),
        (cot_in, cot.at[mine, :]),
    ):
        loads.append(pltpu.make_async_copy(src, dst, load_sems.at[len(loads)]))
        loads[-1].start()

    links = Links(send_sems, recv_sems)
    stores = []
    done = set()

    def store(src, dst):
        copy = pltpu.make_async_copy(src, dst, store_sems.at[len(stores)])
        copy.start()
        stores.append(copy)
        return copy

    def deep_part(z, ring, half):
        columns = pl.ds(pl.multiple_of(((z * 4 + ring) * 2 + core) * OWN, OWN), OWN)
        if half is None:
            return deep.at[:, columns]
        return deep.at[pl.ds(half * (DEEP // 2), DEEP // 2), columns]

    def deep_place(chip, who):
        return deep.at[:, pl.ds(pl.multiple_of((chip * 2 + who) * OWN, OWN), OWN)]

    def up_place(chip, who):
        return rows_of(up, (chip * 2 + who) * OWN, OWN)

    def qkv_place(chip, who):
        return rows_of(wide, (chip * 2 + who) * OWN, OWN).at[:, pl.ds(0, QKV)]

    shares = (
        (deep_place, lambda slot: deep_core.at[slot]),
        (up_place, lambda slot: up_core.at[slot]),
        (qkv_place, lambda slot: rows_of(probs, slot * OWN, OWN).at[:, pl.ds(0, QKV)]),
    )

    def chip_at(ring, turn_of):
        return (zh + (1 - 2 * zh) * turn_of) * 4 + around(y, ring)

    def core_copy(which, ring, turn_of):
        number = which * 8 + ring * 2 + turn_of
        place_of, slots = shares[which]
        return pltpu.make_async_remote_copy(
            src_ref=place_of(chip_at(ring, turn_of), 1 - core),
            dst_ref=slots(ring * 2 + turn_of),
            send_sem=core_send.at[number],
            recv_sem=core_recv.at[number],
            device_id=near["core"],
            device_id_type=MESH,
        )

    def share(which, name):
        place_of, slots = shares[which]

        def add(ring, turn_of):
            core_copy(which, ring, turn_of).wait_recv()
            part = place_of(chip_at(ring, turn_of), core)
            part[...] = (
                part[...].astype(F32) + slots(ring * 2 + turn_of)[...].astype(F32)
            ).astype(BF16)
            return ring

        for step in (2, 1, 3, 0):
            yield [(name + "_raw", step)]
            yield []
            lax.fori_loop(0, 2, lambda turn_of, _: add(step, turn_of), 0)
            done.add((name, step))

    def add_vectors():
        yield [("sums", "ready")]
        slot = 0
        for stage, (names, count) in enumerate(
            (
                (("core",), 96),
                (("y+", "y-", "y2"), 96),
                (("zh",), 96),
                (("zl",), 80),
                (("x+", "x-", "x2"), 80),
            )
        ):
            span = pl.ds(0, count)
            copies = [
                links.send(
                    vectors.at[stage, span], vector_slots.at[slot + index, span], near[name]
                )
                for index, name in enumerate(names)
            ]
            yield copies
            for copy in copies:
                copy.wait_recv()
            parts = [vectors[stage, :count, :]]
            parts += [vector_slots[slot + index, :count, :] for index in range(len(copies))]
            if len(parts) == 2:
                total = parts[0] + parts[1]
            else:
                total = (parts[0] + parts[3]) + (parts[1] + parts[2])
            vectors[stage + 1, :count, :] = total
            slot += len(names)
        for row in range(5):
            for column in range(16):
                sums[row : row + 1, column * 128 : (column + 1) * 128] = vectors[
                    5, row * 16 + column : row * 16 + column + 1, :
                ]
        for column in range(14):
            low_sums[0:1, column * 128 : (column + 1) * 128] = vectors[
                3, 80 + column : 81 + column, :
            ]
        store(sums, vector_sum)
        store(low_sums, low_sum)

    def keep(steps, src, dst):
        yield from steps
        store(src, dst)

    tensor_ends = (zl, x, near["zl"], near["x+"], near["x-"])
    side_ends = (zl, x, None, near["x+"], near["x-"], near["zl"])
    data_ends = (zh, y, near["zh"], near["y+"], near["y-"])
    units = Gather(links, row_part(unit, 0, MAIN_UNIT), *tensor_ends, None)
    units_side = Gather(links, row_part(unit, MAIN_UNIT, D - MAIN_UNIT), *side_ends)
    cots = Gather(links, row_part(cot, 0, MAIN_COT), *tensor_ends, None)
    cots_side = Gather(links, row_part(cot, MAIN_COT, D - MAIN_COT), *side_ends)
    wides = Gather(links, row_part(wide, 0, QKV, core), *data_ends, near["core"])
    wups = Gather(links, row_part(wide, QKV, UNITS, core), *data_ends, near["core"])
    deeps = Gather(links, deep_part, *data_ends, near["core"])

    side_branch = row_part(branch, MAIN_BRANCH, D - MAIN_BRANCH)
    side_grad = row_part(cot, MAIN_GRAD, D - MAIN_GRAD)
    branch_main = Scatter(
        links, row_part(branch, 0, MAIN_BRANCH), branch_slots, branch_last, *tensor_ends
    )
    branch_side = Scatter(links, side_branch, branch_side_slots, None, *tensor_ends)
    branch_pair = PairSum(links, side_branch, branch_pairs, zl, x, near["zl"])
    unit_main = Scatter(links, row_part(cot, 0, MAIN_GRAD), unit_slots, unit_last, *tensor_ends)
    unit_side = Scatter(links, side_grad, unit_side_slots, None, *tensor_ends)
    unit_pair = PairSum(links, side_grad, unit_pairs, zl, x, near["zl"])
    qkv_grid = Scatter(links, row_part(wide, 0, QKV, core), qkv_slots, qkv_last, *data_ends)
    up_grid = Scatter(links, row_part(up, 0, UNITS, core), up_slots, up_last, *data_ends)
    deep_grid = Scatter(links, deep_part, deep_slots, deep_last, *data_ends)
    go, free, turned = ("own", "ready"), ("rows", "free"), ("turn", "free")
    transfers = {
        "unit": units.own(("unit", "ready")),
        "unit_far": units.far(("unit", "sent")),
        "unit_side": units_side.own(("unit", "ready")),
        "cot": cots.own(("wide", "ready")),
        "cot_far": cots.far(("cot", "sent")),
        "cot_side": cots_side.own(("wide", "ready")),
        "wide": wides.own(("wide", "ready")),
        "wide_far": wides.far(("wide", "sent")),
        "wup": wups.own(("wide", "ready")),
        "wup_far": wups.far(("wup", "sent")),
        "deep": deeps.own(("wide", "ready")),
        "deep_far": deeps.far(("deep", "sent")),
        "branch_feed": branch_main.feed("branch", done),
        "branch": branch_main.run("branch", row_total.at[:, pl.ds(0, MAIN_BRANCH)], turned),
        "branch_pair": branch_pair.run("branch", "branch_side", done),
        "branch_side_feed": branch_side.feed("branch_side", done),
        "branch_side": branch_side.run(
            "branch_side", row_total.at[:, pl.ds(MAIN_BRANCH, D - MAIN_BRANCH)], turned
        ),
        "unit_grad_feed": unit_main.feed("unit_grad", done),
        "unit_grad": unit_main.run("unit_grad", row_total.at[:, pl.ds(0, MAIN_GRAD)], free),
        "unit_grad_pair": unit_pair.run("unit_grad", "unit_grad_side", done),
        "unit_grad_side_feed": unit_side.feed("unit_grad_side", done),
        "unit_grad_side": unit_side.run(
            "unit_grad_side", row_total.at[:, pl.ds(MAIN_GRAD, D - MAIN_GRAD)], free
        ),
        "deep_share": share(0, "deep_grad"),
        "deep_grad_feed": deep_grid.feed("deep_grad", done),
        "deep_grad": keep(deep_grid.run("deep_grad", deep_total, go), deep_total, deep_sum),
        "up_share": share(1, "up_grad"),
        "up_grad_feed": up_grid.feed("up_grad", done),
        "up_grad": keep(up_grid.run("up_grad", up_total, go), up_total, up_sum),
        "qkv_share": share(2, "qkv_grad"),
        "qkv_grad_feed": qkv_grid.feed("qkv_grad", done),
        "qkv_grad": keep(qkv_grid.run("qkv_grad", qkv_total, go), qkv_total, qkv_sum),
        "vector": add_vectors(),
    }

    ends = [lens[0, 0]]
    for seq in range(1, 3):
        ends.append(ends[-1] + lens[0, seq])

    def begin_of(index):
        begin = jnp.zeros_like(index)
        for end in ends:
            begin = jnp.where(index >= end, end, begin)
        return begin

    def own_rows():
        loads[0].wait()
        rows = unit[mine, :].astype(F32)
        centred = rows - jnp.mean(rows, axis=-1, keepdims=True)
        variance = jnp.mean(centred * centred, axis=-1, keepdims=True)
        unit[mine, :] = (centred * lax.rsqrt(variance + NORM_EPS)).astype(BF16)
        pl.semaphore_wait(barrier, len(near))
        done.update([("unit", "ready"), go])

    def own_weights():
        for load in loads[1:]:
            load.wait()
        wide[own, :QKV] = qkv_total[...].astype(BF16)
        wide[own, QKV:] = up_total[...].astype(BF16)
        deep[:, own] = deep_total[...].astype(BF16)
        done.add(("wide", "ready"))

    def tables():
        sums[...] = jnp.zeros_like(sums)
        low_sums[...] = jnp.zeros_like(low_sums)
        sums[4:5, :] = jnp.sum(cot[mine, :].astype(F32), axis=0, keepdims=True)
        row = lax.broadcasted_iota(jnp.int32, (OWN, 128), 0)
        lane = lax.broadcasted_iota(jnp.int32, (OWN, 128), 1)
        rate = jnp.exp(lax.rem(lane, 32).astype(F32) * (-2.0 * math.log(10000.0) / ROT))
        for block in range(TOK // OWN):
            index = row + block * OWN
            angle = (index - begin_of(index)).astype(F32) * rate
            columns = slice(block * 128, (block + 1) * 128)
            row_total[:, columns] = jnp.where(lane < ROT, jnp.cos(angle), 1.0)
            columns = slice(TOK + block * 128, TOK + (block + 1) * 128)
            row_total[:, columns] = jnp.where(lane < ROT, jnp.sin(angle), 0.0)

    def turn(which, part):
        blocks = range(part.start // OWN, part.stop // OWN)
        starts = [which * TOK + block * 128 for block in blocks]
        return jnp.concatenate([row_total[:, start : start + 128] for start in starts], axis=0)

    def norm_tile(tile, which):
        part = slice(tile * TILE, (tile + 1) * TILE)
        span = slice(which * TILE, (which + 1) * TILE)
        rows = unit[part, :].astype(F32)
        branch[span, :] = (
            rows * gains[which : which + 1, :] + biases[which : which + 1, :]
        ).astype(BF16)

    def heads(tile):
        part = slice(tile * TILE, (tile + 1) * TILE)
        norm_tile(tile, 0)
        for which, target in enumerate((q, k, v)):
            columns = slice(which * HEAD, (which + 1) * HEAD)
            head = jnp.dot(branch[:TILE, :], wide[:, columns], preferred_element_type=F32)
            head = head + b_qkv[which : which + 1, :]
            if which < 2:
                head = spin(head, turn(0, part), turn(1, part), False)
            target[part, :] = head.astype(BF16)

    def hidden(tile, half):
        part = slice(tile * TILE, (tile + 1) * TILE)
        if half == 0:
            norm_tile(tile, 1)

        def one(piece, _):
            shift = pl.multiple_of(piece * 256, 256)
            pre = jnp.dot(
                branch[TILE:, :], wide[:, pl.ds(QKV + shift, 256)], preferred_element_type=F32
            )
            pre = pre + b_up[0:1, pl.ds(shift, 256)]
            value, rise = gelu_parts(pre)
            acts[part, pl.ds(HEAD + shift, 256)] = value.astype(BF16)
            grads[part, pl.ds(QKV + shift, 256)] = rise.astype(BF16)
            return 0

        lax.fori_loop(2 * half, 2 * half + 2, one, 0)

    def attend(block):
        part = slice(block * QROWS, (block + 1) * QROWS)
        keys = (block + 1) * QROWS
        whole = by_rows(q[part, :], k[:keys, :]) * (HEAD**-0.5)
        for start in range(0, QROWS, OWN):
            scores = whole[start : start + OWN]
            start = block * QROWS + start
            key = lax.broadcasted_iota(jnp.int32, (OWN, keys), 1)
            row = lax.broadcasted_iota(jnp.int32, (OWN, 1), 0) + start
            scores = jnp.where((key <= row) & (key >= begin_of(row)), scores, -jnp.inf)
            expo = jnp.exp(scores - jnp.max(scores, axis=-1, keepdims=True))
            mass = expo / jnp.sum(expo, axis=-1, keepdims=True)
            probs[start : start + OWN, :keys] = mass.astype(BF16)
        acts[part, :HEAD] = jnp.dot(
            probs[part, :keys], v[:keys, :], preferred_element_type=F32
        ).astype(BF16)

    def pieces_of(ring):
        starts = (around(x, ring) * OWN, (4 + around(x, ring)) * OWN)
        return [pl.ds(pl.multiple_of(start, OWN), OWN) for start in starts]

    def mix(step):
        pieces = pieces_of(step)

        def one(piece, _):
            columns = pl.ds(pl.multiple_of(piece * 512, 512), 512)
            rows = jnp.concatenate([acts[each, :] for each in pieces], axis=0)
            both = jnp.dot(rows, deep[:, columns], preferred_element_type=F32).astype(BF16)
            branch[pieces[0], columns] = both[:OWN]
            branch[pieces[1], columns] = both[OWN:]
            return 0

        lax.fori_loop(0, D // 512, one, 0)
        done.add(("branch", step))

    def back(tile, half):
        part = slice(tile * TILE, (tile + 1) * TILE)
        if half == 0:
            mixed_grad[part, :] = by_rows(cot[part, :], deep[:HEAD, :]).astype(BF16)

        def one(piece, _):
            shift = pl.multiple_of(piece * 256, 256)
            columns = pl.ds(QKV + shift, 256)
            grad = by_rows(cot[part, :], deep[pl.ds(HEAD + shift, 256), :])
            grad = grad * grads[part, columns].astype(F32)
            low_sums[0:1, columns] += jnp.sum(grad, axis=0, keepdims=True)
            grads[part, columns] = grad.astype(BF16)
            return 0

        lax.fori_loop(2 * half, 2 * half + 2, one, 0)

    def deep_grads(step):
        if step == 2:
            links.settle(deeps.sent)

        def one(turn_of, _):
            columns = pl.ds(pl.multiple_of(chip_at(step, turn_of) * 256, 256), 256)
            for half in range(2):
                part = slice(half * (DEEP // 2), (half + 1) * (DEEP // 2))
                deep[part, columns] = over_rows(acts[:, part], cot[:, columns]).astype(BF16)
            core_copy(0, step, turn_of).start()
            return 0

        lax.fori_loop(0, 2, one, 0)
        done.add(("deep_grad_raw", step))

    def norm_columns(span, which):
        acts[:, :256] = (
            unit[:, span].astype(F32) * gains[which : which + 1, span]
            + biases[which : which + 1, span]
        ).astype(BF16)

    def up_grads(step):
        def one(turn_of, _):
            span = pl.ds(pl.multiple_of(chip_at(step, turn_of) * 256, 256), 256)
            norm_columns(span, 1)
            up[span, :] = over_rows(acts[:, :256], grads[:, QKV:]).astype(BF16)
            core_copy(1, step, turn_of).start()
            return 0

        lax.fori_loop(0, 2, one, 0)
        done.add(("up_grad_raw", step))

    def qkv_grads(step):
        if step == 2:
            links.settle(wides.sent)

        def one(turn_of, _):
            span = pl.ds(pl.multiple_of(chip_at(step, turn_of) * 256, 256), 256)
            norm_columns(span, 0)
            wide[span, :QKV] = over_rows(acts[:, :256], grads[:, :QKV]).astype(BF16)
            core_copy(2, step, turn_of).start()
            return 0

        lax.fori_loop(0, 2, one, 0)
        done.add(("qkv_grad_raw", step))

    def put_grad(grad, part, which):
        columns = slice(which * HEAD, (which + 1) * HEAD)
        if which < 2:
            grad = spin(grad * (HEAD**-0.5), turn(0, part), turn(1, part), True)
        low_sums[0:1, columns] += jnp.sum(grad, axis=0, keepdims=True)
        grads[part, columns] = grad.astype(BF16)

    def value_grads():
        for block in range(TOK // QROWS):
            part = slice(block * QROWS, (block + 1) * QROWS)
            below = slice(block * QROWS, TOK)
            put_grad(over_rows(probs[below, part], mixed_grad[below, :]), part, 2)

    def query_grads(block):
        part = slice(block * QROWS, (block + 1) * QROWS)
        keys = (block + 1) * QROWS
        whole = by_rows(mixed_grad[part, :], v[:keys, :])
        for start in range(0, QROWS, OWN):
            prob_grad = whole[start : start + OWN]
            rows = slice(block * QROWS + start, block * QROWS + start + OWN)
            mass = probs[rows, :keys].astype(F32)
            delta = jnp.sum(mass * prob_grad, axis=-1, keepdims=True)
            probs[rows, :keys] = (mass * (prob_grad - delta)).astype(BF16)
        put_grad(jnp.dot(probs[part, :keys], k[:keys, :], preferred_element_type=F32), part, 0)

    def key_grads():
        for block in range(TOK // QROWS):
            part = slice(block * QROWS, (block + 1) * QROWS)
            below = slice(block * QROWS, TOK)
            put_grad(over_rows(probs[below, part], q[below, :]), part, 1)
        done.add(turned)

    def unit_grads(step):
        if step == 2:
            links.settle(cots.sent + cots_side.sent)
        pieces = pieces_of(step)
        for half in range(2):
            acts[half * OWN : (half + 1) * OWN, :QKV] = grads[pieces[half], :QKV]
            acts[(2 + half) * OWN : (3 + half) * OWN, :UNITS] = grads[pieces[half], QKV:]

        def one(piece, _):
            columns = pl.ds(pl.multiple_of(piece * 512, 512), 512)
            first = by_rows(acts[: 2 * OWN, :QKV], wide[columns, :QKV])
            second = by_rows(acts[2 * OWN : 4 * OWN, :UNITS], wide[columns, QKV:])
            rows = jnp.concatenate([unit[each, columns] for each in pieces], axis=0).astype(F32)
            sums[0:1, columns] += jnp.sum(first * rows, axis=0, keepdims=True)
            sums[1:2, columns] += jnp.sum(second * rows, axis=0, keepdims=True)
            sums[2:3, columns] += jnp.sum(first, axis=0, keepdims=True)
            sums[3:4, columns] += jnp.sum(second, axis=0, keepdims=True)
            both = (first * gains[0:1, columns] + second * gains[1:2, columns]).astype(BF16)
            cot[pieces[0], columns] = both[:OWN]
            cot[pieces[1], columns] = both[OWN:]
            return 0

        lax.fori_loop(0, D // 512, one, 0)
        done.add(("unit_grad", step))

    def pack():
        for row in range(5):
            for column in range(16):
                vectors[0, row * 16 + column : row * 16 + column + 1, :] = sums[
                    row : row + 1, column * 128 : (column + 1) * 128
                ]
        for column in range(14):
            vectors[0, 80 + column : 81 + column, :] = low_sums[
                0:1, column * 128 : (column + 1) * 128
            ]
        vectors[0, 94:96, :] = jnp.zeros((2, 128), F32)
        done.add(("sums", "ready"))

    branch_stores = []

    def branch_out():
        branch_stores.append(pltpu.make_async_copy(row_total, branch_sum, store_sems.at[7]))
        branch_stores[0].start()
        branch_stores[0].wait()
        done.add(free)

    compute = {
        ".init": own_rows,
        ".weights": own_weights,
        ".tables": tables,
        ".dv": value_grads,
        ".dk": key_grads,
        ".pack": pack,
        ".branch_out": branch_out,
    }
    for tile in range(TOK // TILE):
        compute[f".qkv{tile}"] = functools.partial(heads, tile)
        for half, letter in enumerate("ab"):
            compute[f".hid{tile}{letter}"] = functools.partial(hidden, tile, half)
            compute[f".back{tile}{letter}"] = functools.partial(back, tile, half)
    for step in range(4):
        compute[f".att{step}"] = functools.partial(attend, step)
        compute[f".dp{step}"] = functools.partial(query_grads, step)
        compute[f".mix{step}"] = functools.partial(mix, step)
        compute[f".deepg{step}"] = functools.partial(deep_grads, step)
        compute[f".upg{step}"] = functools.partial(up_grads, step)
        compute[f".qg{step}"] = functools.partial(qkv_grads, step)
        compute[f".g{step}"] = functools.partial(unit_grads, step)

    waiting = {name: next(steps) for name, steps in transfers.items()}
    for name in ORDER:
        if name in compute:
            compute.pop(name)()
            continue
        assert all(each in done for each in waiting[name] if isinstance(each, tuple)), name
        waiting[name] = next(transfers[name], None)
        done.add((name, "sent"))
        if waiting[name] is None:
            del waiting[name]
    assert not waiting and not compute
    store(row_total, unit_sum)

    for which in range(3):
        for step in range(4):
            for turn_of in range(2):
                core_copy(which, step, turn_of).wait_send()
    for copy in stores:
        copy.wait()
    links.settle(links.open)


SUMS = (
    ((OWN, D), F32),
    ((OWN, D), F32),
    ((OWN, QKV), F32),
    ((OWN, UNITS), F32),
    ((DEEP, OWN), F32),
    ((8, D), F32),
    ((8, WIDE), F32),
)
HALF = OWN // 2
SCRATCH = (
    ((TOK, D), BF16),
    ((TOK, D), BF16),
    ((D, WIDE), BF16),
    ((DEEP, D), BF16),
    ((D, UNITS), BF16),
    ((TOK, HEAD), BF16),
    ((TOK, HEAD), BF16),
    ((TOK, HEAD), BF16),
    ((TOK, DEEP), BF16),
    ((TOK, TOK), BF16),
    ((TOK, D), BF16),
    ((TOK, WIDE), BF16),
    ((TOK, HEAD), BF16),
    ((8, D), F32),
    ((8, WIDE), F32),
    ((6, 96, 128), F32),
    ((9, 96, 128), F32),
    ((8, OWN, UNITS), BF16),
    ((8, DEEP, OWN), BF16),
    ((2, 3, 2, HALF, QKV), BF16),
    ((2, 3, 2, HALF, UNITS), BF16),
    ((2, 3, 2, DEEP // 2, OWN), BF16),
    ((2, 3, 2, HALF, MAIN_BRANCH), BF16),
    ((2, 3, 2, HALF, MAIN_GRAD), BF16),
    ((2, 3, 1, HALF, D - MAIN_BRANCH), BF16),
    ((2, 3, 1, HALF, D - MAIN_GRAD), BF16),
    ((4, OWN, D - MAIN_BRANCH), BF16),
    ((4, OWN, D - MAIN_GRAD), BF16),
    ((OWN, QKV), BF16),
    ((OWN, UNITS), BF16),
    ((DEEP, OWN), BF16),
    ((OWN, MAIN_BRANCH), BF16),
    ((OWN, MAIN_GRAD), BF16),
    ((OWN, D), F32),
    ((OWN, QKV), F32),
    ((OWN, UNITS), F32),
    ((DEEP, OWN), F32),
)


def run_layer(lens, layer_in, cotangent, w_qkv, w_out, w_up, w_down, *vectors):
    anywhere = pl.BlockSpec(memory_space=pl.ANY)
    vmem = pl.BlockSpec(memory_space=pltpu.VMEM)
    return pl.pallas_call(
        layer_kernel,
        out_shape=[jax.ShapeDtypeStruct(*each) for each in SUMS],
        in_specs=[pl.BlockSpec(memory_space=pltpu.SMEM)] + [anywhere] * 6 + [vmem] * len(vectors),
        out_specs=[anywhere] * len(SUMS),
        scratch_shapes=[pltpu.VMEM(*each) for each in SCRATCH]
        + [
            pltpu.SemaphoreType.DMA((180,)),
            pltpu.SemaphoreType.DMA((180,)),
            pltpu.SemaphoreType.DMA((24,)),
            pltpu.SemaphoreType.DMA((24,)),
            pltpu.SemaphoreType.DMA((8,)),
            pltpu.SemaphoreType.DMA((8,)),
        ],
        compiler_params=pltpu.CompilerParams(
            collective_id=0, has_side_effects=True, vmem_limit_bytes=63 * 2**20
        ),
        cost_estimate=pl.CostEstimate(flops=42 * 10**9, bytes_accessed=10**7, transcendentals=0),
        name="layer",
    )(lens, layer_in, cotangent, w_qkv, w_out, w_up, w_down, *vectors)


def adam_step(weight, gradient, moment_one, moment_two, step_rate, decay_rate):
    moment_one = BETA_ONE * moment_one + (1.0 - BETA_ONE) * gradient
    moment_two = BETA_TWO * moment_two + (1.0 - BETA_TWO) * gradient * gradient
    ratio = (
        moment_one
        / (1.0 - BETA_ONE**STEP)
        / (jnp.sqrt(moment_two / (1.0 - BETA_TWO**STEP)) + ADAM_EPS)
    )
    return (moment_one, moment_two, weight - step_rate * (ratio + decay_rate * weight))


BIG = 14


def update_kernel(*refs):
    sums, refs = refs[:7], refs[7:]
    big, refs = refs[:BIG], refs[BIG:]
    small, refs = refs[:12], refs[12:]
    big_out, refs = refs[:BIG], refs[BIG:]
    small_out, refs = refs[:12], refs[12:]
    sum_bufs, refs = refs[:7], refs[7:]
    in_bufs, refs = refs[:BIG], refs[BIG:]
    row_bufs, load_sems, store_sems = refs[:2], refs[2], refs[3]
    sources = list(zip(sums, sum_bufs)) + list(zip(big, in_bufs))
    order = [4, 12, 13, 14, 18, 19, 20, 3, 15, 16, 17, 2, 9, 10, 11, 5, 6, 0, 1, 7, 8]
    copies = [
        pltpu.make_async_copy(src, dst, load_sems.at[index])
        for index, (src, dst) in enumerate(sources)
    ]
    for index in order:
        copies[index].start()
    stores = []

    def put(src, dst):
        copy = pltpu.make_async_copy(src, dst, store_sems.at[len(stores)])
        copy.start()
        stores.append(copy)

    branch, unit_grad, qkv, up, deep, vectors, low_vectors = sum_bufs
    copies[4].wait()
    for which, part in ((1, slice(0, HEAD)), (3, slice(HEAD, DEEP)), (2, None), (0, None)):
        if which == 2:
            copies[3].wait()
        elif which == 0:
            copies[2].wait()
        first = 2 + 3 * which
        bufs = in_bufs[first : first + 3]
        for index in range(3):
            copies[7 + first + index].wait()
        weight, one, two = bufs
        for head in range(3 if which == 0 else 1):
            if which == 0:
                place_of = (head,)
                gradient = qkv[:, head * HEAD : (head + 1) * HEAD]
            else:
                place_of = (slice(None),)
                gradient = deep[part, :] if part is not None else up[...]
            results = adam_step(
                weight[place_of],
                gradient,
                one[place_of],
                two[place_of],
                STEP_RATES[which],
                DECAY_RATES[which],
            )
            one[place_of], two[place_of], weight[place_of] = results
        put(one, big_out[first])
        put(two, big_out[first + 1])
        put(weight, big_out[first + 2])

    for index in (5, 6, 0, 1, 7, 8):
        copies[index].wait()
    slots = (
        (0, 4, [low_vectors[0:1, head * HEAD : (head + 1) * HEAD] for head in range(3)]),
        (3, 5, [low_vectors[0:1, QKV:]]),
        (6, 6, [vectors[0:1, :], vectors[1:2, :]]),
        (9, 7, [vectors[2:3, :], vectors[3:4, :], vectors[4:5, :], vectors[4:5, :]]),
    )
    for first, which, rows in slots:
        weight, one, two = small[first : first + 3]
        for row, gradient in enumerate(rows):
            at = slice(row, row + 1)
            results = adam_step(
                weight[at, :], gradient, one[at, :], two[at, :], STEP_RATES[which], DECAY_RATES[which]
            )
            for index in range(3):
                small_out[first + index][at, :] = results[index]
    biases = small[9]
    resid = in_bufs[0][...].astype(F32)
    row_bufs[0][...] = (resid + branch[...] + biases[2:3, :] + biases[3:4, :]).astype(BF16)
    put(row_bufs[0], big_out[0])
    centred = resid - jnp.mean(resid, axis=-1, keepdims=True)
    inverse = lax.rsqrt(jnp.mean(centred * centred, axis=-1, keepdims=True) + NORM_EPS)
    unit = centred * inverse
    grad = unit_grad[...]
    mean = jnp.mean(grad, axis=-1, keepdims=True)
    along = jnp.mean(grad * unit, axis=-1, keepdims=True)
    row_bufs[1][...] = in_bufs[1][...].astype(F32) + inverse * (grad - mean - unit * along)
    put(row_bufs[1], big_out[1])
    for copy in stores:
        copy.wait()


def run_update(sums, big, small):
    anywhere = pl.BlockSpec(memory_space=pl.ANY)
    vmem = pl.BlockSpec(memory_space=pltpu.VMEM)
    matrices = [jax.ShapeDtypeStruct(each.shape, F32) for each in big[2:]]
    rows = [jax.ShapeDtypeStruct((OWN, D), BF16), jax.ShapeDtypeStruct((OWN, D), F32)]
    return pl.pallas_call(
        update_kernel,
        out_shape=rows + matrices + [jax.ShapeDtypeStruct(each.shape, F32) for each in small],
        in_specs=[anywhere] * (len(sums) + BIG) + [vmem] * 12,
        out_specs=[anywhere] * BIG + [vmem] * 12,
        scratch_shapes=[pltpu.VMEM(each.shape, F32) for each in sums]
        + [pltpu.VMEM(each.shape, each.dtype) for each in big]
        + [pltpu.VMEM((OWN, D), BF16), pltpu.VMEM((OWN, D), F32)]
        + [pltpu.SemaphoreType.DMA((len(sums) + BIG,)), pltpu.SemaphoreType.DMA((BIG,))],
        compiler_params=pltpu.CompilerParams(vmem_limit_bytes=32 * 2**20),
        cost_estimate=pl.CostEstimate(flops=10**7, bytes_accessed=16 * 10**6, transcendentals=0),
        name="update",
    )(*sums, *big, *small)


def local(layer_in, cotangent, seq_lengths, *state):
    params, moments = list(state[:8]), list(state[8:])
    params[0] = params[0].transpose(1, 0, 2)
    moments[0], moments[1] = (each.transpose(1, 0, 2) for each in moments[:2])
    params[5] = params[5].reshape(1, UNITS)
    moments[10], moments[11] = (each.reshape(1, UNITS) for each in moments[10:12])
    sums = run_layer(seq_lengths, layer_in, cotangent, *params)
    groups = [(params[which], moments[2 * which], moments[2 * which + 1]) for which in range(8)]
    big = [layer_in, cotangent] + [each for group in groups[:4] for each in group]
    small = [each for group in groups[4:] for each in group]
    results = list(run_update(sums, big, small))
    for index in range(2, 5):
        results[index] = results[index].transpose(1, 0, 2)
    for index in range(17, 20):
        results[index] = results[index].reshape(UNITS)
    return tuple(results)


def solution(mesh):
    rows = P(("dp", "tensor"), None)
    out, up = P("tensor", "dp"), P("dp", "tensor")
    params = (P("dp", None, "tensor"), out, up, out, P(None, "tensor"), P("tensor"), P(), P())
    moments = [spec for spec in params for _ in range(2)]
    return jax.shard_map(
        local,
        mesh=mesh,
        in_specs=(rows, rows, P("dp", None), *params, *moments),
        out_specs=(rows, rows, *[spec for spec in params for _ in range(3)]),
        check_vma=False,
    )
```

```python
import functools
import math

import jax
import jax.numpy as jnp
from jax import lax
from jax.experimental import pallas as pl
from jax.experimental.pallas import tpu as pltpu
from jax.sharding import PartitionSpec as P

F32 = jnp.float32
BF16 = jnp.bfloat16
MESH = pl.DeviceIdType.MESH

D = 2048
HEAD = 256
QKV = 3 * HEAD
UNITS = 1024
WIDE = QKV + UNITS
DEEP = HEAD + UNITS
TOK = 1024
OWN = 128
TILE = 512
MAIN_UNIT, MAIN_COT, MAIN_BRANCH, MAIN_GRAD = 1664, 1408, 1664, 1664
QROWS = 256
ROT = 64
STEP = 10

NORM_EPS = 1e-05
BETA_ONE = 0.9
BETA_TWO = 0.95
ADAM_EPS = 1e-08
STEP_RATES = (0.04, 0.2, 0.04, 0.02, 0.3, 0.3, 0.5, 0.3)
DECAY_RATES = (0.01, 0.01, 0.01, 0.01, 0.0, 0.0, 0.0, 0.0)


def place():
    dp = lax.axis_index("dp")
    tensor = lax.axis_index("tensor")
    return (
        lax.div(dp, 8),
        lax.rem(lax.div(dp, 2), 4),
        lax.rem(dp, 2),
        lax.div(tensor, 4),
        lax.rem(tensor, 4),
    )


def device(zh, y, core, zl, x):
    return ((zh * 4 + y) * 2 + core, zl * 4 + x)


def around(pos, step):
    return lax.rem(pos + step + 4, 4)


def neighbours(spot):
    zh, y, core, zl, x = spot
    return {
        "x+": device(zh, y, core, zl, around(x, 1)),
        "x-": device(zh, y, core, zl, around(x, -1)),
        "y+": device(zh, around(y, 1), core, zl, x),
        "y-": device(zh, around(y, -1), core, zl, x),
        "zl": device(zh, y, core, 1 - zl, x),
        "zh": device(1 - zh, y, core, zl, x),
        "core": device(zh, y, 1 - core, zl, x),
    }


class Links:
    def __init__(self, send_sems, recv_sems):
        self.send_sems, self.recv_sems = send_sems, recv_sems
        self.copies, self.open = [], []

    def send(self, src, dst, target):
        index = len(self.copies)
        copy = pltpu.make_async_remote_copy(
            src_ref=src,
            dst_ref=dst,
            send_sem=self.send_sems.at[index],
            recv_sem=self.recv_sems.at[index],
            device_id=target,
            device_id_type=MESH,
        )
        copy.start()
        self.copies.append(copy)
        self.open.append(copy)
        return copy

    def settle(self, copies):
        for copy in copies:
            copy.wait_send()
        self.open = [each for each in self.open if not any(each is copy for copy in copies)]


class Gather:
    def __init__(self, links, block, z, ring, z_dev, plus, minus, onward):
        self.links, self.block, self.z, self.ring = links, block, z, ring
        self.z_dev, self.ways, self.onward = z_dev, (plus, minus), onward
        self.by_z, self.sent = None, []

    def to(self, z, ring, half, target):
        part = self.block(z, ring, half)
        self.sent.append(self.links.send(part, part, target))
        return self.sent[-1]

    def round(self, z):
        passed = []

        def pass_on(ring):
            if self.onward is not None:
                passed.append(self.to(z, ring, None, self.onward))

        whole = [self.to(z, self.ring, None, way) for way in self.ways]
        pass_on(self.ring)
        halves = []
        for way in range(2):
            yield [whole[way]]
            whole[way].wait_recv()
            from_ring = around(self.ring, 1 if way else -1)
            halves.append(self.to(z, from_ring, way, self.ways[way]))
            pass_on(from_ring)
        yield halves
        for copy in halves:
            copy.wait_recv()
        pass_on(around(self.ring, 2))
        yield passed
        for copy in passed:
            copy.wait_recv()

    def own(self, gate):
        yield [gate]
        if self.z_dev is not None:
            self.by_z = self.to(self.z, self.ring, None, self.z_dev)
        yield from self.round(self.z)

    def far(self, gate):
        yield [gate]
        yield [self.by_z]
        self.by_z.wait_recv()
        yield from self.round(1 - self.z)


class Scatter:
    def __init__(self, links, part, slots, last, z, ring, z_dev, plus, minus):
        self.links, self.part, self.slots, self.last = links, part, slots, last
        self.ring, self.z_dev, self.ways = ring, z_dev, (plus, minus)
        self.zs = (z,) if last is None else (1 - z, z)
        self.sent = {}

    def push(self, way, message, order, ring, half):
        self.sent[way, message, order] = self.links.send(
            self.part(self.zs[order], ring, half),
            self.slots.at[way, message, order],
            self.ways[way],
        )

    def arrived(self, way, message, order):
        self.sent[way, message, order].wait_recv()
        return self.slots[way, message, order].astype(F32)

    def total(self, order, half):
        part = self.part(self.zs[order], self.ring, half)
        return (
            part[...].astype(F32) + self.arrived(half, 2, order) + self.arrived(1 - half, 1, order)
        )

    def feed(self, name, done):
        yield [(name, 2)]
        for order in range(len(self.zs)):
            for way in range(2):
                self.push(way, 0, order, around(self.ring, 2), way)
        for way, step in ((0, 1), (1, 3)):
            yield [(name, step)]
            for order in range(len(self.zs)):
                self.push(way, 1, order, around(self.ring, step), 1 - way)
        done.add((name, "fed"))

    def run(self, name, out, gate):
        yield [(name, "fed")]
        for order in range(len(self.zs)):
            for way in range(2):
                yield [self.sent[way, 0, order]]
                ring = around(self.ring, -1 if way else 1)
                part = self.part(self.zs[order], ring, way)
                part[...] = (part[...].astype(F32) + self.arrived(way, 0, order)).astype(BF16)
                self.push(way, 2, order, ring, way)
        by_z = None
        if self.last is not None:
            yield [(name, 0)] + [self.sent[way, each, 0] for way in range(2) for each in (1, 2)]
            for half in range(2):
                part = self.part(self.zs[0], self.ring, half)
                part[...] = self.total(0, half).astype(BF16)
            by_z = self.links.send(self.part(self.zs[0], self.ring, None), self.last, self.z_dev)
        order = len(self.zs) - 1
        yield [(name, 0), gate] + [
            self.sent[way, each, order] for way in range(2) for each in (1, 2)
        ]
        rows = out.shape[0] // 2
        for half in range(2):
            out[pl.ds(half * rows, rows), :] = self.total(order, half)
        if by_z is not None:
            yield [by_z]
            by_z.wait_recv()
            out[...] = out[...] + self.last[...].astype(F32)


class PairSum:
    def __init__(self, links, part, slots, z, ring, z_dev):
        self.links, self.part, self.slots = links, part, slots
        self.z, self.ring, self.z_dev = z, ring, z_dev

    def run(self, name, flag, done):
        for step in (2, 1, 3, 0):
            yield [(name, step)]
            part = self.part(1 - self.z, around(self.ring, step), None)
            moved = self.links.send(part, self.slots.at[step], self.z_dev)
            yield [moved]
            moved.wait_recv()
            part = self.part(self.z, around(self.ring, step), None)
            part[...] = (part[...].astype(F32) + self.slots[step].astype(F32)).astype(BF16)
            done.add((flag, step))


def rows_of(ref, start, count):
    return ref.at[pl.ds(pl.multiple_of(start, 16), count)]


def row_part(ref, first, count, core=None):
    def part(z, ring, half):
        index, rows = z * 4 + ring, OWN
        if core is not None:
            index = index * 2 + core
        start = index * OWN
        if half is not None:
            start, rows = start + half * (OWN // 2), OWN // 2
        return ref.at[pl.ds(pl.multiple_of(start, 16), rows), pl.ds(first, count)]

    return part


def over_rows(left, right):
    return lax.dot_general(left, right, (((0,), (0,)), ((), ())), preferred_element_type=F32)


def by_rows(left, right):
    return lax.dot_general(left, right, (((1,), (1,)), ((), ())), preferred_element_type=F32)


def gelu_parts(pre):
    cdf = 0.5 * (1.0 + lax.erf(pre * (1.0 / math.sqrt(2.0))))
    density = jnp.exp(-0.5 * pre * pre) * (1.0 / math.sqrt(2.0 * math.pi))
    return pre * cdf, cdf + pre * density


def spin(rows, cosines, sines, back):
    low = rows[:, :128]
    lane = lax.broadcasted_iota(jnp.int32, low.shape, 1)
    ahead = pltpu.roll(low, 96, 1)
    behind = pltpu.roll(low, 32, 1)
    turned = jnp.where(lane < 32, -ahead, jnp.where(lane < 64, behind, 0.0))
    if back:
        turned = -turned
    return jnp.concatenate([low * cosines + turned * sines, rows[:, 128:]], axis=1)


ORDER = (
    ".init", "unit_side", "unit", "unit_far", ".weights", "wide", "wup", "wup_far", "wide_far", ".tables",
    "unit_side", "unit_side", "wide", "wide", "wup", "wup", "unit_far", "unit", "unit", "unit_side", "wide", "wide",
    "wup", "wide_far", "wup", "wide_far", "wide_far", "wup_far", "deep", "deep_far", "unit_far", "unit_far", "cot",
    "cot_far", "cot_side", "wide_far", "wide_far", "unit", "unit", "unit_side", "wup_far", "wup_far", "unit_far",
    "unit_far", ".qkv0", ".qkv1", "deep_far", ".att0", ".att1", "deep", "deep", ".att2", "cot", "cot", ".att3",
    "wup_far", "cot_side", "cot_side", "cot_far", "wup_far", ".hid0a", ".hid0b", "cot", "cot", "cot_side", "deep_far",
    "deep_far", ".hid1a", "deep", ".hid1b", "deep", "deep_far", "cot_far", "cot_far", "deep_far", ".mix2", "cot_side",
    "branch_feed", "branch_pair", ".mix1", "branch_feed", ".mix3", "branch_feed", "branch", ".mix0", "cot_far",
    "cot_far", "branch_pair", "branch_pair", "branch_side_feed", ".back0a", ".back0b", "branch", "branch",
    "branch_pair", "branch_pair", "branch_side_feed", ".back1a", ".back1b", "branch_pair", "branch_pair",
    "branch_side_feed", "branch_side", ".deepg2", "branch", "branch", "deep_share", ".deepg1", "branch_pair",
    ".deepg3", "deep_share", "deep_share", "deep_share", "deep_share", "deep_grad_feed", "deep_grad_feed", ".deepg0",
    "deep_share", "deep_share", "deep_grad_feed", "deep_grad", ".dv", ".dp0", "deep_share", ".dp1", "deep_grad",
    "deep_grad", "branch_side", "branch_side", ".dp2", ".dp3", "deep_grad", "branch", "deep_grad", ".dk", ".g2",
    "unit_grad_feed", "unit_grad_pair", ".g1", "branch", "unit_grad_feed", "branch_side", ".g3", "unit_grad_feed",
    "unit_grad", ".g0", "branch", "unit_grad", "unit_grad", "deep_grad", "unit_grad_pair", "unit_grad_pair",
    "unit_grad_side_feed", ".pack", "vector", ".upg2", "deep_grad", "up_share", "vector", ".upg1", "unit_grad",
    "unit_grad", "up_share", "up_share", "up_grad_feed", ".upg3", "up_share", "up_share", "up_grad_feed", "vector",
    ".upg0", ".qg2", "deep_grad", "up_share", "up_share", "up_grad_feed", "up_grad", "up_grad", "up_grad",
    "qkv_share", ".qg1", "up_share", "qkv_share", "qkv_share", "qkv_grad_feed", "unit_grad_pair", "unit_grad_pair",
    "unit_grad_side_feed", ".qg3", "up_grad", "up_grad", "qkv_share", "qkv_share", "qkv_grad_feed", "vector", ".qg0",
    ".branch_out", "qkv_share", "qkv_share", "qkv_grad_feed", "qkv_grad", "unit_grad_pair", "unit_grad_pair",
    "unit_grad_side_feed", "unit_grad_side", "vector", "qkv_share", "unit_grad", "unit_grad_side", "unit_grad_pair",
    "unit_grad_side", "up_grad", "qkv_grad", "qkv_grad", "unit_grad", "qkv_grad", "qkv_grad", "vector",
    "unit_grad_side", "up_grad", "unit_grad", "up_grad", "qkv_grad", "qkv_grad", "qkv_grad",
)


def layer_kernel(
    lens,
    x_in,
    cot_in,
    w_qkv,
    w_out,
    w_up,
    w_down,
    b_qkv,
    b_up,
    gains,
    biases,
    branch_sum,
    unit_sum,
    qkv_sum,
    up_sum,
    deep_sum,
    vector_sum,
    low_sum,
    unit,
    cot,
    wide,
    deep,
    up,
    q,
    k,
    v,
    acts,
    probs,
    branch,
    grads,
    mixed_grad,
    sums,
    low_sums,
    vectors,
    vector_slots,
    up_core,
    deep_core,
    qkv_slots,
    up_slots,
    deep_slots,
    branch_slots,
    unit_slots,
    branch_side_slots,
    unit_side_slots,
    branch_pairs,
    unit_pairs,
    qkv_last,
    up_last,
    deep_last,
    branch_last,
    unit_last,
    row_total,
    qkv_total,
    up_total,
    deep_total,
    send_sems,
    recv_sems,
    core_send,
    core_recv,
    load_sems,
    store_sems,
):
    spot = place()
    zh, y, core, zl, x = spot
    near = neighbours(spot)
    near["x2"] = device(zh, y, core, zl, around(x, 2))
    near["y2"] = device(zh, around(y, 2), core, zl, x)
    barrier = pltpu.get_barrier_semaphore()
    for target in near.values():
        pl.semaphore_signal(barrier, inc=1, device_id=target, device_id_type=MESH)

    mine = pl.ds(pl.multiple_of((zl * 4 + x) * OWN, OWN), OWN)
    own = pl.ds(pl.multiple_of(((zh * 4 + y) * 2 + core) * OWN, OWN), OWN)
    loads = []
    for src, dst in (
        (x_in, unit.at[mine, :]),
        *((w_qkv.at[head], qkv_total.at[:, pl.ds(head * HEAD, HEAD)]) for head in range(3)),
        (w_up, up_total),
        (w_out, deep_total.at[pl.ds(0, HEAD), :]),
        (w_down, deep_total.at[pl.ds(HEAD, UNITS), :]),
        (cot_in, cot.at[mine, :]),
    ):
        loads.append(pltpu.make_async_copy(src, dst, load_sems.at[len(loads)]))
        loads[-1].start()

    links = Links(send_sems, recv_sems)
    stores = []
    done = set()

    def store(src, dst):
        copy = pltpu.make_async_copy(src, dst, store_sems.at[len(stores)])
        copy.start()
        stores.append(copy)
        return copy

    def deep_part(z, ring, half):
        columns = pl.ds(pl.multiple_of(((z * 4 + ring) * 2 + core) * OWN, OWN), OWN)
        if half is None:
            return deep.at[:, columns]
        return deep.at[pl.ds(half * (DEEP // 2), DEEP // 2), columns]

    def deep_place(chip, who):
        return deep.at[:, pl.ds(pl.multiple_of((chip * 2 + who) * OWN, OWN), OWN)]

    def up_place(chip, who):
        return rows_of(up, (chip * 2 + who) * OWN, OWN)

    def qkv_place(chip, who):
        return rows_of(wide, (chip * 2 + who) * OWN, OWN).at[:, pl.ds(0, QKV)]

    shares = (
        (deep_place, lambda slot: deep_core.at[slot]),
        (up_place, lambda slot: up_core.at[slot]),
        (qkv_place, lambda slot: rows_of(probs, slot * OWN, OWN).at[:, pl.ds(0, QKV)]),
    )

    def chip_at(ring, turn_of):
        return (zh + (1 - 2 * zh) * turn_of) * 4 + around(y, ring)

    def core_copy(which, ring, turn_of):
        number = which * 8 + ring * 2 + turn_of
        place_of, slots = shares[which]
        return pltpu.make_async_remote_copy(
            src_ref=place_of(chip_at(ring, turn_of), 1 - core),
            dst_ref=slots(ring * 2 + turn_of),
            send_sem=core_send.at[number],
            recv_sem=core_recv.at[number],
            device_id=near["core"],
            device_id_type=MESH,
        )

    def share(which, name):
        place_of, slots = shares[which]

        def add(ring, turn_of):
            core_copy(which, ring, turn_of).wait_recv()
            part = place_of(chip_at(ring, turn_of), core)
            part[...] = (
                part[...].astype(F32) + slots(ring * 2 + turn_of)[...].astype(F32)
            ).astype(BF16)
            return ring

        for step in (2, 1, 3, 0):
            yield [(name + "_raw", step)]
            yield []
            lax.fori_loop(0, 2, lambda turn_of, _: add(step, turn_of), 0)
            done.add((name, step))

    def add_vectors():
        yield [("sums", "ready")]
        slot = 0
        for stage, (names, count) in enumerate(
            (
                (("core",), 96),
                (("y+", "y-", "y2"), 96),
                (("zh",), 96),
                (("zl",), 80),
                (("x+", "x-", "x2"), 80),
            )
        ):
            span = pl.ds(0, count)
            copies = [
                links.send(
                    vectors.at[stage, span], vector_slots.at[slot + index, span], near[name]
                )
                for index, name in enumerate(names)
            ]
            yield copies
            for copy in copies:
                copy.wait_recv()
            parts = [vectors[stage, :count, :]]
            parts += [vector_slots[slot + index, :count, :] for index in range(len(copies))]
            if len(parts) == 2:
                total = parts[0] + parts[1]
            else:
                total = (parts[0] + parts[3]) + (parts[1] + parts[2])
            vectors[stage + 1, :count, :] = total
            slot += len(names)
        for row in range(5):
            for column in range(16):
                sums[row : row + 1, column * 128 : (column + 1) * 128] = vectors[
                    5, row * 16 + column : row * 16 + column + 1, :
                ]
        for column in range(14):
            low_sums[0:1, column * 128 : (column + 1) * 128] = vectors[
                3, 80 + column : 81 + column, :
            ]
        store(sums, vector_sum)
        store(low_sums, low_sum)

    def keep(steps, src, dst):
        yield from steps
        store(src, dst)

    tensor_ends = (zl, x, near["zl"], near["x+"], near["x-"])
    side_ends = (zl, x, None, near["x+"], near["x-"], near["zl"])
    data_ends = (zh, y, near["zh"], near["y+"], near["y-"])
    units = Gather(links, row_part(unit, 0, MAIN_UNIT), *tensor_ends, None)
    units_side = Gather(links, row_part(unit, MAIN_UNIT, D - MAIN_UNIT), *side_ends)
    cots = Gather(links, row_part(cot, 0, MAIN_COT), *tensor_ends, None)
    cots_side = Gather(links, row_part(cot, MAIN_COT, D - MAIN_COT), *side_ends)
    wides = Gather(links, row_part(wide, 0, QKV, core), *data_ends, near["core"])
    wups = Gather(links, row_part(wide, QKV, UNITS, core), *data_ends, near["core"])
    deeps = Gather(links, deep_part, *data_ends, near["core"])

    side_branch = row_part(branch, MAIN_BRANCH, D - MAIN_BRANCH)
    side_grad = row_part(cot, MAIN_GRAD, D - MAIN_GRAD)
    branch_main = Scatter(
        links, row_part(branch, 0, MAIN_BRANCH), branch_slots, branch_last, *tensor_ends
    )
    branch_side = Scatter(links, side_branch, branch_side_slots, None, *tensor_ends)
    branch_pair = PairSum(links, side_branch, branch_pairs, zl, x, near["zl"])
    unit_main = Scatter(links, row_part(cot, 0, MAIN_GRAD), unit_slots, unit_last, *tensor_ends)
    unit_side = Scatter(links, side_grad, unit_side_slots, None, *tensor_ends)
    unit_pair = PairSum(links, side_grad, unit_pairs, zl, x, near["zl"])
    qkv_grid = Scatter(links, row_part(wide, 0, QKV, core), qkv_slots, qkv_last, *data_ends)
    up_grid = Scatter(links, row_part(up, 0, UNITS, core), up_slots, up_last, *data_ends)
    deep_grid = Scatter(links, deep_part, deep_slots, deep_last, *data_ends)
    go, free, turned = ("own", "ready"), ("rows", "free"), ("turn", "free")
    transfers = {
        "unit": units.own(("unit", "ready")),
        "unit_far": units.far(("unit", "sent")),
        "unit_side": units_side.own(("unit", "ready")),
        "cot": cots.own(("wide", "ready")),
        "cot_far": cots.far(("cot", "sent")),
        "cot_side": cots_side.own(("wide", "ready")),
        "wide": wides.own(("wide", "ready")),
        "wide_far": wides.far(("wide", "sent")),
        "wup": wups.own(("wide", "ready")),
        "wup_far": wups.far(("wup", "sent")),
        "deep": deeps.own(("wide", "ready")),
        "deep_far": deeps.far(("deep", "sent")),
        "branch_feed": branch_main.feed("branch", done),
        "branch": branch_main.run("branch", row_total.at[:, pl.ds(0, MAIN_BRANCH)], turned),
        "branch_pair": branch_pair.run("branch", "branch_side", done),
        "branch_side_feed": branch_side.feed("branch_side", done),
        "branch_side": branch_side.run(
            "branch_side", row_total.at[:, pl.ds(MAIN_BRANCH, D - MAIN_BRANCH)], turned
        ),
        "unit_grad_feed": unit_main.feed("unit_grad", done),
        "unit_grad": unit_main.run("unit_grad", row_total.at[:, pl.ds(0, MAIN_GRAD)], free),
        "unit_grad_pair": unit_pair.run("unit_grad", "unit_grad_side", done),
        "unit_grad_side_feed": unit_side.feed("unit_grad_side", done),
        "unit_grad_side": unit_side.run(
            "unit_grad_side", row_total.at[:, pl.ds(MAIN_GRAD, D - MAIN_GRAD)], free
        ),
        "deep_share": share(0, "deep_grad"),
        "deep_grad_feed": deep_grid.feed("deep_grad", done),
        "deep_grad": keep(deep_grid.run("deep_grad", deep_total, go), deep_total, deep_sum),
        "up_share": share(1, "up_grad"),
        "up_grad_feed": up_grid.feed("up_grad", done),
        "up_grad": keep(up_grid.run("up_grad", up_total, go), up_total, up_sum),
        "qkv_share": share(2, "qkv_grad"),
        "qkv_grad_feed": qkv_grid.feed("qkv_grad", done),
        "qkv_grad": keep(qkv_grid.run("qkv_grad", qkv_total, go), qkv_total, qkv_sum),
        "vector": add_vectors(),
    }

    ends = [lens[0, 0]]
    for seq in range(1, 3):
        ends.append(ends[-1] + lens[0, seq])

    def begin_of(index):
        begin = jnp.zeros_like(index)
        for end in ends:
            begin = jnp.where(index >= end, end, begin)
        return begin

    def own_rows():
        loads[0].wait()
        rows = unit[mine, :].astype(F32)
        centred = rows - jnp.mean(rows, axis=-1, keepdims=True)
        variance = jnp.mean(centred * centred, axis=-1, keepdims=True)
        unit[mine, :] = (centred * lax.rsqrt(variance + NORM_EPS)).astype(BF16)
        pl.semaphore_wait(barrier, len(near))
        done.update([("unit", "ready"), go])

    def own_weights():
        for load in loads[1:]:
            load.wait()
        wide[own, :QKV] = qkv_total[...].astype(BF16)
        wide[own, QKV:] = up_total[...].astype(BF16)
        deep[:, own] = deep_total[...].astype(BF16)
        done.add(("wide", "ready"))

    def tables():
        sums[...] = jnp.zeros_like(sums)
        low_sums[...] = jnp.zeros_like(low_sums)
        sums[4:5, :] = jnp.sum(cot[mine, :].astype(F32), axis=0, keepdims=True)
        row = lax.broadcasted_iota(jnp.int32, (OWN, 128), 0)
        lane = lax.broadcasted_iota(jnp.int32, (OWN, 128), 1)
        rate = jnp.exp(lax.rem(lane, 32).astype(F32) * (-2.0 * math.log(10000.0) / ROT))
        for block in range(TOK // OWN):
            index = row + block * OWN
            angle = (index - begin_of(index)).astype(F32) * rate
            columns = slice(block * 128, (block + 1) * 128)
            row_total[:, columns] = jnp.where(lane < ROT, jnp.cos(angle), 1.0)
            columns = slice(TOK + block * 128, TOK + (block + 1) * 128)
            row_total[:, columns] = jnp.where(lane < ROT, jnp.sin(angle), 0.0)

    def turn(which, part):
        blocks = range(part.start // OWN, part.stop // OWN)
        starts = [which * TOK + block * 128 for block in blocks]
        return jnp.concatenate([row_total[:, start : start + 128] for start in starts], axis=0)

    def norm_tile(tile, which):
        part = slice(tile * TILE, (tile + 1) * TILE)
        span = slice(which * TILE, (which + 1) * TILE)
        rows = unit[part, :].astype(F32)
        branch[span, :] = (
            rows * gains[which : which + 1, :] + biases[which : which + 1, :]
        ).astype(BF16)

    def heads(tile):
        part = slice(tile * TILE, (tile + 1) * TILE)
        norm_tile(tile, 0)
        for which, target in enumerate((q, k, v)):
            columns = slice(which * HEAD, (which + 1) * HEAD)
            head = jnp.dot(branch[:TILE, :], wide[:, columns], preferred_element_type=F32)
            head = head + b_qkv[which : which + 1, :]
            if which < 2:
                head = spin(head, turn(0, part), turn(1, part), False)
            target[part, :] = head.astype(BF16)

    def hidden(tile, half):
        part = slice(tile * TILE, (tile + 1) * TILE)
        if half == 0:
            norm_tile(tile, 1)

        def one(piece, _):
            shift = pl.multiple_of(piece * 256, 256)
            pre = jnp.dot(
                branch[TILE:, :], wide[:, pl.ds(QKV + shift, 256)], preferred_element_type=F32
            )
            pre = pre + b_up[0:1, pl.ds(shift, 256)]
            value, rise = gelu_parts(pre)
            acts[part, pl.ds(HEAD + shift, 256)] = value.astype(BF16)
            grads[part, pl.ds(QKV + shift, 256)] = rise.astype(BF16)
            return 0

        lax.fori_loop(2 * half, 2 * half + 2, one, 0)

    def attend(block):
        part = slice(block * QROWS, (block + 1) * QROWS)
        keys = (block + 1) * QROWS
        whole = by_rows(q[part, :], k[:keys, :]) * (HEAD**-0.5)
        for start in range(0, QROWS, OWN):
            scores = whole[start : start + OWN]
            start = block * QROWS + start
            key = lax.broadcasted_iota(jnp.int32, (OWN, keys), 1)
            row = lax.broadcasted_iota(jnp.int32, (OWN, 1), 0) + start
            scores = jnp.where((key <= row) & (key >= begin_of(row)), scores, -jnp.inf)
            expo = jnp.exp(scores - jnp.max(scores, axis=-1, keepdims=True))
            mass = expo / jnp.sum(expo, axis=-1, keepdims=True)
            probs[start : start + OWN, :keys] = mass.astype(BF16)
        acts[part, :HEAD] = jnp.dot(
            probs[part, :keys], v[:keys, :], preferred_element_type=F32
        ).astype(BF16)

    def pieces_of(ring):
        starts = (around(x, ring) * OWN, (4 + around(x, ring)) * OWN)
        return [pl.ds(pl.multiple_of(start, OWN), OWN) for start in starts]

    def mix(step):
        pieces = pieces_of(step)

        def one(piece, _):
            columns = pl.ds(pl.multiple_of(piece * 512, 512), 512)
            rows = jnp.concatenate([acts[each, :] for each in pieces], axis=0)
            both = jnp.dot(rows, deep[:, columns], preferred_element_type=F32).astype(BF16)
            branch[pieces[0], columns] = both[:OWN]
            branch[pieces[1], columns] = both[OWN:]
            return 0

        lax.fori_loop(0, D // 512, one, 0)
        done.add(("branch", step))

    def back(tile, half):
        part = slice(tile * TILE, (tile + 1) * TILE)
        if half == 0:
            mixed_grad[part, :] = by_rows(cot[part, :], deep[:HEAD, :]).astype(BF16)

        def one(piece, _):
            shift = pl.multiple_of(piece * 256, 256)
            columns = pl.ds(QKV + shift, 256)
            grad = by_rows(cot[part, :], deep[pl.ds(HEAD + shift, 256), :])
            grad = grad * grads[part, columns].astype(F32)
            low_sums[0:1, columns] += jnp.sum(grad, axis=0, keepdims=True)
            grads[part, columns] = grad.astype(BF16)
            return 0

        lax.fori_loop(2 * half, 2 * half + 2, one, 0)

    def deep_grads(step):
        if step == 2:
            links.settle(deeps.sent)

        def one(turn_of, _):
            columns = pl.ds(pl.multiple_of(chip_at(step, turn_of) * 256, 256), 256)
            for half in range(2):
                part = slice(half * (DEEP // 2), (half + 1) * (DEEP // 2))
                deep[part, columns] = over_rows(acts[:, part], cot[:, columns]).astype(BF16)
            core_copy(0, step, turn_of).start()
            return 0

        lax.fori_loop(0, 2, one, 0)
        done.add(("deep_grad_raw", step))

    def norm_columns(span, which):
        acts[:, :256] = (
            unit[:, span].astype(F32) * gains[which : which + 1, span]
            + biases[which : which + 1, span]
        ).astype(BF16)

    def up_grads(step):
        def one(turn_of, _):
            span = pl.ds(pl.multiple_of(chip_at(step, turn_of) * 256, 256), 256)
            norm_columns(span, 1)
            up[span, :] = over_rows(acts[:, :256], grads[:, QKV:]).astype(BF16)
            core_copy(1, step, turn_of).start()
            return 0

        lax.fori_loop(0, 2, one, 0)
        done.add(("up_grad_raw", step))

    def qkv_grads(step):
        if step == 2:
            links.settle(wides.sent)

        def one(turn_of, _):
            span = pl.ds(pl.multiple_of(chip_at(step, turn_of) * 256, 256), 256)
            norm_columns(span, 0)
            wide[span, :QKV] = over_rows(acts[:, :256], grads[:, :QKV]).astype(BF16)
            core_copy(2, step, turn_of).start()
            return 0

        lax.fori_loop(0, 2, one, 0)
        done.add(("qkv_grad_raw", step))

    def put_grad(grad, part, which):
        columns = slice(which * HEAD, (which + 1) * HEAD)
        if which < 2:
            grad = spin(grad * (HEAD**-0.5), turn(0, part), turn(1, part), True)
        low_sums[0:1, columns] += jnp.sum(grad, axis=0, keepdims=True)
        grads[part, columns] = grad.astype(BF16)

    def value_grads():
        for block in range(TOK // QROWS):
            part = slice(block * QROWS, (block + 1) * QROWS)
            below = slice(block * QROWS, TOK)
            put_grad(over_rows(probs[below, part], mixed_grad[below, :]), part, 2)

    def query_grads(block):
        part = slice(block * QROWS, (block + 1) * QROWS)
        keys = (block + 1) * QROWS
        whole = by_rows(mixed_grad[part, :], v[:keys, :])
        for start in range(0, QROWS, OWN):
            prob_grad = whole[start : start + OWN]
            rows = slice(block * QROWS + start, block * QROWS + start + OWN)
            mass = probs[rows, :keys].astype(F32)
            delta = jnp.sum(mass * prob_grad, axis=-1, keepdims=True)
            probs[rows, :keys] = (mass * (prob_grad - delta)).astype(BF16)
        put_grad(jnp.dot(probs[part, :keys], k[:keys, :], preferred_element_type=F32), part, 0)

    def key_grads():
        for block in range(TOK // QROWS):
            part = slice(block * QROWS, (block + 1) * QROWS)
            below = slice(block * QROWS, TOK)
            put_grad(over_rows(probs[below, part], q[below, :]), part, 1)
        done.add(turned)

    def unit_grads(step):
        if step == 2:
            links.settle(cots.sent + cots_side.sent)
        pieces = pieces_of(step)
        for half in range(2):
            acts[half * OWN : (half + 1) * OWN, :QKV] = grads[pieces[half], :QKV]
            acts[(2 + half) * OWN : (3 + half) * OWN, :UNITS] = grads[pieces[half], QKV:]

        def one(piece, _):
            columns = pl.ds(pl.multiple_of(piece * 512, 512), 512)
            first = by_rows(acts[: 2 * OWN, :QKV], wide[columns, :QKV])
            second = by_rows(acts[2 * OWN : 4 * OWN, :UNITS], wide[columns, QKV:])
            rows = jnp.concatenate([unit[each, columns] for each in pieces], axis=0).astype(F32)
            sums[0:1, columns] += jnp.sum(first * rows, axis=0, keepdims=True)
            sums[1:2, columns] += jnp.sum(second * rows, axis=0, keepdims=True)
            sums[2:3, columns] += jnp.sum(first, axis=0, keepdims=True)
            sums[3:4, columns] += jnp.sum(second, axis=0, keepdims=True)
            both = (first * gains[0:1, columns] + second * gains[1:2, columns]).astype(BF16)
            cot[pieces[0], columns] = both[:OWN]
            cot[pieces[1], columns] = both[OWN:]
            return 0

        lax.fori_loop(0, D // 512, one, 0)
        done.add(("unit_grad", step))

    def pack():
        for row in range(5):
            for column in range(16):
                vectors[0, row * 16 + column : row * 16 + column + 1, :] = sums[
                    row : row + 1, column * 128 : (column + 1) * 128
                ]
        for column in range(14):
            vectors[0, 80 + column : 81 + column, :] = low_sums[
                0:1, column * 128 : (column + 1) * 128
            ]
        vectors[0, 94:96, :] = jnp.zeros((2, 128), F32)
        done.add(("sums", "ready"))

    branch_stores = []

    def branch_out():
        branch_stores.append(pltpu.make_async_copy(row_total, branch_sum, store_sems.at[7]))
        branch_stores[0].start()
        branch_stores[0].wait()
        done.add(free)

    compute = {
        ".init": own_rows,
        ".weights": own_weights,
        ".tables": tables,
        ".dv": value_grads,
        ".dk": key_grads,
        ".pack": pack,
        ".branch_out": branch_out,
    }
    for tile in range(TOK // TILE):
        compute[f".qkv{tile}"] = functools.partial(heads, tile)
        for half, letter in enumerate("ab"):
            compute[f".hid{tile}{letter}"] = functools.partial(hidden, tile, half)
            compute[f".back{tile}{letter}"] = functools.partial(back, tile, half)
    for step in range(4):
        compute[f".att{step}"] = functools.partial(attend, step)
        compute[f".dp{step}"] = functools.partial(query_grads, step)
        compute[f".mix{step}"] = functools.partial(mix, step)
        compute[f".deepg{step}"] = functools.partial(deep_grads, step)
        compute[f".upg{step}"] = functools.partial(up_grads, step)
        compute[f".qg{step}"] = functools.partial(qkv_grads, step)
        compute[f".g{step}"] = functools.partial(unit_grads, step)

    waiting = {name: next(steps) for name, steps in transfers.items()}
    for name in ORDER:
        if name in compute:
            compute.pop(name)()
            continue
        assert all(each in done for each in waiting[name] if isinstance(each, tuple)), name
        waiting[name] = next(transfers[name], None)
        done.add((name, "sent"))
        if waiting[name] is None:
            del waiting[name]
    assert not waiting and not compute
    store(row_total, unit_sum)

    for which in range(3):
        for step in range(4):
            for turn_of in range(2):
                core_copy(which, step, turn_of).wait_send()
    for copy in stores:
        copy.wait()
    links.settle(links.open)


SUMS = (
    ((OWN, D), F32),
    ((OWN, D), F32),
    ((OWN, QKV), F32),
    ((OWN, UNITS), F32),
    ((DEEP, OWN), F32),
    ((8, D), F32),
    ((8, WIDE), F32),
)
HALF = OWN // 2
SCRATCH = (
    ((TOK, D), BF16),
    ((TOK, D), BF16),
    ((D, WIDE), BF16),
    ((DEEP, D), BF16),
    ((D, UNITS), BF16),
    ((TOK, HEAD), BF16),
    ((TOK, HEAD), BF16),
    ((TOK, HEAD), BF16),
    ((TOK, DEEP), BF16),
    ((TOK, TOK), BF16),
    ((TOK, D), BF16),
    ((TOK, WIDE), BF16),
    ((TOK, HEAD), BF16),
    ((8, D), F32),
    ((8, WIDE), F32),
    ((6, 96, 128), F32),
    ((9, 96, 128), F32),
    ((8, OWN, UNITS), BF16),
    ((8, DEEP, OWN), BF16),
    ((2, 3, 2, HALF, QKV), BF16),
    ((2, 3, 2, HALF, UNITS), BF16),
    ((2, 3, 2, DEEP // 2, OWN), BF16),
    ((2, 3, 2, HALF, MAIN_BRANCH), BF16),
    ((2, 3, 2, HALF, MAIN_GRAD), BF16),
    ((2, 3, 1, HALF, D - MAIN_BRANCH), BF16),
    ((2, 3, 1, HALF, D - MAIN_GRAD), BF16),
    ((4, OWN, D - MAIN_BRANCH), BF16),
    ((4, OWN, D - MAIN_GRAD), BF16),
    ((OWN, QKV), BF16),
    ((OWN, UNITS), BF16),
    ((DEEP, OWN), BF16),
    ((OWN, MAIN_BRANCH), BF16),
    ((OWN, MAIN_GRAD), BF16),
    ((OWN, D), F32),
    ((OWN, QKV), F32),
    ((OWN, UNITS), F32),
    ((DEEP, OWN), F32),
)


def run_layer(lens, layer_in, cotangent, w_qkv, w_out, w_up, w_down, *vectors):
    anywhere = pl.BlockSpec(memory_space=pl.ANY)
    vmem = pl.BlockSpec(memory_space=pltpu.VMEM)
    return pl.pallas_call(
        layer_kernel,
        out_shape=[jax.ShapeDtypeStruct(*each) for each in SUMS],
        in_specs=[pl.BlockSpec(memory_space=pltpu.SMEM)] + [anywhere] * 6 + [vmem] * len(vectors),
        out_specs=[anywhere] * len(SUMS),
        scratch_shapes=[pltpu.VMEM(*each) for each in SCRATCH]
        + [
            pltpu.SemaphoreType.DMA((180,)),
            pltpu.SemaphoreType.DMA((180,)),
            pltpu.SemaphoreType.DMA((24,)),
            pltpu.SemaphoreType.DMA((24,)),
            pltpu.SemaphoreType.DMA((8,)),
            pltpu.SemaphoreType.DMA((8,)),
        ],
        compiler_params=pltpu.CompilerParams(
            collective_id=0, has_side_effects=True, vmem_limit_bytes=63 * 2**20
        ),
        cost_estimate=pl.CostEstimate(flops=42 * 10**9, bytes_accessed=10**7, transcendentals=0),
        name="layer",
    )(lens, layer_in, cotangent, w_qkv, w_out, w_up, w_down, *vectors)


def adam_step(weight, gradient, moment_one, moment_two, step_rate, decay_rate):
    moment_one = BETA_ONE * moment_one + (1.0 - BETA_ONE) * gradient
    moment_two = BETA_TWO * moment_two + (1.0 - BETA_TWO) * gradient * gradient
    ratio = (
        moment_one
        / (1.0 - BETA_ONE**STEP)
        / (jnp.sqrt(moment_two / (1.0 - BETA_TWO**STEP)) + ADAM_EPS)
    )
    return (moment_one, moment_two, weight - step_rate * (ratio + decay_rate * weight))


BIG = 14


def update_kernel(*refs):
    sums, refs = refs[:7], refs[7:]
    big, refs = refs[:BIG], refs[BIG:]
    small, refs = refs[:12], refs[12:]
    big_out, refs = refs[:BIG], refs[BIG:]
    small_out, refs = refs[:12], refs[12:]
    sum_bufs, refs = refs[:7], refs[7:]
    in_bufs, refs = refs[:BIG], refs[BIG:]
    row_bufs, load_sems, store_sems = refs[:2], refs[2], refs[3]
    sources = list(zip(sums, sum_bufs)) + list(zip(big, in_bufs))
    order = [4, 12, 13, 14, 18, 19, 20, 3, 15, 16, 17, 2, 9, 10, 11, 5, 6, 0, 1, 7, 8]
    copies = [
        pltpu.make_async_copy(src, dst, load_sems.at[index])
        for index, (src, dst) in enumerate(sources)
    ]
    for index in order:
        copies[index].start()
    stores = []

    def put(src, dst):
        copy = pltpu.make_async_copy(src, dst, store_sems.at[len(stores)])
        copy.start()
        stores.append(copy)

    branch, unit_grad, qkv, up, deep, vectors, low_vectors = sum_bufs
    copies[4].wait()
    for which, part in ((1, slice(0, HEAD)), (3, slice(HEAD, DEEP)), (2, None), (0, None)):
        if which == 2:
            copies[3].wait()
        elif which == 0:
            copies[2].wait()
        first = 2 + 3 * which
        bufs = in_bufs[first : first + 3]
        for index in range(3):
            copies[7 + first + index].wait()
        weight, one, two = bufs
        for head in range(3 if which == 0 else 1):
            if which == 0:
                place_of = (head,)
                gradient = qkv[:, head * HEAD : (head + 1) * HEAD]
            else:
                place_of = (slice(None),)
                gradient = deep[part, :] if part is not None else up[...]
            results = adam_step(
                weight[place_of],
                gradient,
                one[place_of],
                two[place_of],
                STEP_RATES[which],
                DECAY_RATES[which],
            )
            one[place_of], two[place_of], weight[place_of] = results
        put(one, big_out[first])
        put(two, big_out[first + 1])
        put(weight, big_out[first + 2])

    for index in (5, 6, 0, 1, 7, 8):
        copies[index].wait()
    slots = (
        (0, 4, [low_vectors[0:1, head * HEAD : (head + 1) * HEAD] for head in range(3)]),
        (3, 5, [low_vectors[0:1, QKV:]]),
        (6, 6, [vectors[0:1, :], vectors[1:2, :]]),
        (9, 7, [vectors[2:3, :], vectors[3:4, :], vectors[4:5, :], vectors[4:5, :]]),
    )
    for first, which, rows in slots:
        weight, one, two = small[first : first + 3]
        for row, gradient in enumerate(rows):
            at = slice(row, row + 1)
            results = adam_step(
                weight[at, :], gradient, one[at, :], two[at, :], STEP_RATES[which], DECAY_RATES[which]
            )
            for index in range(3):
                small_out[first + index][at, :] = results[index]
    biases = small[9]
    resid = in_bufs[0][...].astype(F32)
    row_bufs[0][...] = (resid + branch[...] + biases[2:3, :] + biases[3:4, :]).astype(BF16)
    put(row_bufs[0], big_out[0])
    centred = resid - jnp.mean(resid, axis=-1, keepdims=True)
    inverse = lax.rsqrt(jnp.mean(centred * centred, axis=-1, keepdims=True) + NORM_EPS)
    unit = centred * inverse
    grad = unit_grad[...]
    mean = jnp.mean(grad, axis=-1, keepdims=True)
    along = jnp.mean(grad * unit, axis=-1, keepdims=True)
    row_bufs[1][...] = in_bufs[1][...].astype(F32) + inverse * (grad - mean - unit * along)
    put(row_bufs[1], big_out[1])
    for copy in stores:
        copy.wait()


def run_update(sums, big, small):
    anywhere = pl.BlockSpec(memory_space=pl.ANY)
    vmem = pl.BlockSpec(memory_space=pltpu.VMEM)
    matrices = [jax.ShapeDtypeStruct(each.shape, F32) for each in big[2:]]
    rows = [jax.ShapeDtypeStruct((OWN, D), BF16), jax.ShapeDtypeStruct((OWN, D), F32)]
    return pl.pallas_call(
        update_kernel,
        out_shape=rows + matrices + [jax.ShapeDtypeStruct(each.shape, F32) for each in small],
        in_specs=[anywhere] * (len(sums) + BIG) + [vmem] * 12,
        out_specs=[anywhere] * BIG + [vmem] * 12,
        scratch_shapes=[pltpu.VMEM(each.shape, F32) for each in sums]
        + [pltpu.VMEM(each.shape, each.dtype) for each in big]
        + [pltpu.VMEM((OWN, D), BF16), pltpu.VMEM((OWN, D), F32)]
        + [pltpu.SemaphoreType.DMA((len(sums) + BIG,)), pltpu.SemaphoreType.DMA((BIG,))],
        compiler_params=pltpu.CompilerParams(vmem_limit_bytes=63 * 2**20),
        cost_estimate=pl.CostEstimate(flops=10**7, bytes_accessed=16 * 10**6, transcendentals=0),
        name="update",
    )(*sums, *big, *small)


def local(layer_in, cotangent, seq_lengths, *state):
    params, moments = list(state[:8]), list(state[8:])
    params[0] = params[0].transpose(1, 0, 2)
    moments[0], moments[1] = (each.transpose(1, 0, 2) for each in moments[:2])
    params[5] = params[5].reshape(1, UNITS)
    moments[10], moments[11] = (each.reshape(1, UNITS) for each in moments[10:12])
    sums = run_layer(seq_lengths, layer_in, cotangent, *params)
    groups = [(params[which], moments[2 * which], moments[2 * which + 1]) for which in range(8)]
    big = [layer_in, cotangent] + [each for group in groups[:4] for each in group]
    small = [each for group in groups[4:] for each in group]
    results = list(run_update(sums, big, small))
    for index in range(2, 5):
        results[index] = results[index].transpose(1, 0, 2)
    for index in range(17, 20):
        results[index] = results[index].reshape(UNITS)
    return tuple(results)


def solution(mesh):
    rows = P(("dp", "tensor"), None)
    out, up = P("tensor", "dp"), P("dp", "tensor")
    params = (P("dp", None, "tensor"), out, up, out, P(None, "tensor"), P("tensor"), P(), P())
    moments = [spec for spec in params for _ in range(2)]
    return jax.shard_map(
        local,
        mesh=mesh,
        in_specs=(rows, rows, P("dp", None), *params, *moments),
        out_specs=(rows, rows, *[spec for spec in params for _ in range(3)]),
        check_vma=False,
    )
```

```python
import functools
import math

import jax
import jax.numpy as jnp
from jax import lax
from jax.experimental import pallas as pl
from jax.experimental.pallas import tpu as pltpu
from jax.sharding import PartitionSpec as P

F32 = jnp.float32
BF16 = jnp.bfloat16
MESH = pl.DeviceIdType.MESH

D = 2048
HEAD = 256
QKV = 3 * HEAD
UNITS = 1024
WIDE = QKV + UNITS
DEEP = HEAD + UNITS
TOK = 1024
OWN = 128
TILE = 512
MAIN_UNIT, MAIN_COT, MAIN_BRANCH, MAIN_GRAD = 1792, 1024, 1536, 1536
QROWS = 256
ROT = 64
STEP = 10

NORM_EPS = 1e-05
BETA_ONE = 0.9
BETA_TWO = 0.95
ADAM_EPS = 1e-08
STEP_RATES = (0.04, 0.2, 0.04, 0.02, 0.3, 0.3, 0.5, 0.3)
DECAY_RATES = (0.01, 0.01, 0.01, 0.01, 0.0, 0.0, 0.0, 0.0)


def place():
    dp = lax.axis_index("dp")
    tensor = lax.axis_index("tensor")
    return (
        lax.div(dp, 8),
        lax.rem(lax.div(dp, 2), 4),
        lax.rem(dp, 2),
        lax.div(tensor, 4),
        lax.rem(tensor, 4),
    )


def device(zh, y, core, zl, x):
    return ((zh * 4 + y) * 2 + core, zl * 4 + x)


def around(pos, step):
    return lax.rem(pos + step + 4, 4)


def neighbours(spot):
    zh, y, core, zl, x = spot
    return {
        "x+": device(zh, y, core, zl, around(x, 1)),
        "x-": device(zh, y, core, zl, around(x, -1)),
        "y+": device(zh, around(y, 1), core, zl, x),
        "y-": device(zh, around(y, -1), core, zl, x),
        "zl": device(zh, y, core, 1 - zl, x),
        "zh": device(1 - zh, y, core, zl, x),
        "core": device(zh, y, 1 - core, zl, x),
    }


class Links:
    def __init__(self, send_sems, recv_sems):
        self.send_sems, self.recv_sems = send_sems, recv_sems
        self.copies, self.open = [], []

    def send(self, src, dst, target):
        index = len(self.copies)
        copy = pltpu.make_async_remote_copy(
            src_ref=src,
            dst_ref=dst,
            send_sem=self.send_sems.at[index],
            recv_sem=self.recv_sems.at[index],
            device_id=target,
            device_id_type=MESH,
        )
        copy.start()
        self.copies.append(copy)
        self.open.append(copy)
        return copy

    def settle(self, copies):
        for copy in copies:
            copy.wait_send()
        self.open = [each for each in self.open if not any(each is copy for copy in copies)]


class Gather:
    def __init__(self, links, block, z, ring, z_dev, plus, minus, onward):
        self.links, self.block, self.z, self.ring = links, block, z, ring
        self.z_dev, self.ways, self.onward = z_dev, (plus, minus), onward
        self.by_z, self.sent = None, []

    def to(self, z, ring, half, target):
        part = self.block(z, ring, half)
        self.sent.append(self.links.send(part, part, target))
        return self.sent[-1]

    def round(self, z):
        passed = []

        def pass_on(ring):
            if self.onward is not None:
                passed.append(self.to(z, ring, None, self.onward))

        whole = [self.to(z, self.ring, None, way) for way in self.ways]
        pass_on(self.ring)
        halves = []
        for way in range(2):
            yield [whole[way]]
            whole[way].wait_recv()
            from_ring = around(self.ring, 1 if way else -1)
            halves.append(self.to(z, from_ring, way, self.ways[way]))
            pass_on(from_ring)
        yield halves
        for copy in halves:
            copy.wait_recv()
        pass_on(around(self.ring, 2))
        yield passed
        for copy in passed:
            copy.wait_recv()

    def own(self, gate):
        yield [gate]
        if self.z_dev is not None:
            self.by_z = self.to(self.z, self.ring, None, self.z_dev)
        yield from self.round(self.z)

    def far(self, gate):
        yield [gate]
        yield [self.by_z]
        self.by_z.wait_recv()
        yield from self.round(1 - self.z)


class Scatter:
    def __init__(self, links, part, slots, last, z, ring, z_dev, plus, minus):
        self.links, self.part, self.slots, self.last = links, part, slots, last
        self.ring, self.z_dev, self.ways = ring, z_dev, (plus, minus)
        self.zs = (z,) if last is None else (1 - z, z)
        self.sent = {}

    def push(self, way, message, order, ring, half):
        self.sent[way, message, order] = self.links.send(
            self.part(self.zs[order], ring, half),
            self.slots.at[way, message, order],
            self.ways[way],
        )

    def arrived(self, way, message, order):
        self.sent[way, message, order].wait_recv()
        return self.slots[way, message, order].astype(F32)

    def total(self, order, half):
        part = self.part(self.zs[order], self.ring, half)
        return (
            part[...].astype(F32) + self.arrived(half, 2, order) + self.arrived(1 - half, 1, order)
        )

    def feed(self, name, order, gate, done):
        yield [gate, (name, 2)]
        for way in range(2):
            self.push(way, 0, order, around(self.ring, 2), way)
        for way, step in ((0, 1), (1, 3)):
            yield [(name, step)]
            self.push(way, 1, order, around(self.ring, step), 1 - way)
        done.add((name, "fed", order))

    def run(self, name, out, gate, done):
        for order in range(len(self.zs)):
            yield [(name, "fed", order)]
            for way in range(2):
                yield [self.sent[way, 0, order]]
                ring = around(self.ring, -1 if way else 1)
                part = self.part(self.zs[order], ring, way)
                part[...] = (part[...].astype(F32) + self.arrived(way, 0, order)).astype(BF16)
                self.push(way, 2, order, ring, way)
            done.add((name, "joined", order))
        by_z = None
        if self.last is not None:
            yield [(name, 0)] + [self.sent[way, each, 0] for way in range(2) for each in (1, 2)]
            for half in range(2):
                part = self.part(self.zs[0], self.ring, half)
                part[...] = self.total(0, half).astype(BF16)
            by_z = self.links.send(self.part(self.zs[0], self.ring, None), self.last, self.z_dev)
        order = len(self.zs) - 1
        yield [(name, 0), gate] + [
            self.sent[way, each, order] for way in range(2) for each in (1, 2)
        ]
        rows = out.shape[0] // 2
        for half in range(2):
            out[pl.ds(half * rows, rows), :] = self.total(order, half)
        if by_z is not None:
            yield [by_z]
            by_z.wait_recv()
            out[...] = out[...] + self.last[...].astype(F32)


class PairSum:
    def __init__(self, links, part, slots, z, ring, z_dev):
        self.links, self.part, self.slots = links, part, slots
        self.z, self.ring, self.z_dev = z, ring, z_dev

    def run(self, name, flag, done):
        for step in (2, 1, 3, 0):
            yield [(name, step)]
            part = self.part(1 - self.z, around(self.ring, step), None)
            moved = self.links.send(part, self.slots.at[step], self.z_dev)
            yield [moved]
            moved.wait_recv()
            part = self.part(self.z, around(self.ring, step), None)
            part[...] = (part[...].astype(F32) + self.slots[step].astype(F32)).astype(BF16)
            done.add((flag, step))


def rows_of(ref, start, count):
    return ref.at[pl.ds(pl.multiple_of(start, 16), count)]


def row_part(ref, first, count, core=None):
    def part(z, ring, half):
        index, rows = z * 4 + ring, OWN
        if core is not None:
            index = index * 2 + core
        start = index * OWN
        if half is not None:
            start, rows = start + half * (OWN // 2), OWN // 2
        return ref.at[pl.ds(pl.multiple_of(start, 16), rows), pl.ds(first, count)]

    return part


def over_rows(left, right):
    return lax.dot_general(left, right, (((0,), (0,)), ((), ())), preferred_element_type=F32)


def by_rows(left, right):
    return lax.dot_general(left, right, (((1,), (1,)), ((), ())), preferred_element_type=F32)


def gelu_parts(pre):
    cdf = 0.5 * (1.0 + lax.erf(pre * (1.0 / math.sqrt(2.0))))
    density = jnp.exp(-0.5 * pre * pre) * (1.0 / math.sqrt(2.0 * math.pi))
    return pre * cdf, cdf + pre * density


def spin(rows, cosines, sines, back):
    low = rows[:, :128]
    lane = lax.broadcasted_iota(jnp.int32, low.shape, 1)
    ahead = pltpu.roll(low, 96, 1)
    behind = pltpu.roll(low, 32, 1)
    turned = jnp.where(lane < 32, -ahead, jnp.where(lane < 64, behind, 0.0))
    if back:
        turned = -turned
    return jnp.concatenate([low * cosines + turned * sines, rows[:, 128:]], axis=1)


LATE = ("branch", "up_grad", "qkv_grad",)
ORDER = (
    ".init", "wide", "unit", "wup", "wide_far", "unit_side", "wup_far", "unit_far", ".tables", "wide", "wide",
    "wide_far", "unit", "unit", "wup", "wup", "unit_side", "unit_side", "wide", "wide", "unit_far", "wide_far",
    "wide_far", "unit", "unit", "unit_side", "wup", "wup_far", "deep", "deep_far", "wup", "wide_far", "wide_far",
    "unit_side", "wup_far", "wup_far", "unit_far", "unit_far", "cot_side", "cot", "cot_far", "deep_far", "unit_far",
    "unit_far", ".qkv0", "deep", "deep", ".qkv1", "wup_far", ".att0", ".att1", ".att2", ".att3", "wup_far",
    "cot_side", "cot_side", ".hid0a", ".hid0b", ".hid1a", "cot_far", "deep_far", "deep_far", "cot", "cot", ".hid1b",
    "deep", "cot_side", "deep", "deep_far", "deep_far", ".mix2", "cot_far", "cot_far", "branch_pair", "branch_feed0",
    ".mix1", "branch_feed0", "cot", "cot", ".mix3", "branch_feed0", "branch", ".mix0", "cot_far", "cot_far",
    "cot_side", ".back0a", "branch_pair", "branch_pair", "branch_side_feed0", ".back0b", "branch", "branch",
    "branch_feed1", "branch_feed1", "branch_feed1", "branch", ".back1a", ".back1b", "branch_pair", "branch_pair",
    "branch_side_feed0", ".dv", ".deepg2", "deep_share", ".dp0", ".dp1", ".deepg1", "deep_share", "deep_share",
    "deep_grad_feed1", "deep_grad_feed0", "branch_pair", "branch_pair", "branch_side_feed0", "branch_side",
    "branch_side", "branch_side", ".deepg3", "deep_share", "deep_share", "deep_grad_feed1", "deep_grad_feed0", ".dp2",
    "branch", "branch", "branch", ".dp3", ".dk", "deep_share", "deep_grad_feed1", "deep_grad_feed0", "branch_pair",
    "deep_grad", ".deepg0", "deep_share", ".upg2", "up_share", "deep_grad", "deep_grad", "deep_grad", "deep_grad",
    "deep_grad", ".g2", "deep_share", "unit_grad_feed1", "unit_grad_pair", "up_share", "up_grad_feed0",
    "unit_grad_feed0", "branch_side", ".g1", "unit_grad_feed1", "branch", "branch", "unit_grad_feed0", ".branch_out",
    "unit_grad_pair", "unit_grad_pair", "unit_grad_side_feed0", ".upg1", "up_share", "deep_grad", ".upg3", ".upg0",
    "unit_grad_pair", "unit_grad_side_feed0", "up_share", "up_share", "up_grad_feed0", "deep_grad", "up_share",
    "up_share", "up_grad_feed0", "up_grad", ".g3", "unit_grad_feed1", "unit_grad_pair", "up_grad", "up_grad",
    "up_grad_feed1", "up_grad_feed1", "up_grad_feed1", "up_grad", "up_share", "unit_grad_feed0", "unit_grad",
    "unit_grad", "unit_grad", "unit_grad", "unit_grad", "unit_grad", ".g0", "deep_grad", ".pack", "vector",
    "unit_grad_pair", "unit_grad_pair", "unit_grad_side_feed0", "unit_grad_side", "unit_grad_side", "unit_grad_side",
    "vector", ".qg2", "up_grad", "up_grad", "up_grad", "qkv_share", ".qg1", ".qg3", "unit_grad_pair", "qkv_share",
    "qkv_grad_feed0", "qkv_share", ".qg0", "vector", "qkv_share", "qkv_grad_feed0", "qkv_share", "qkv_share",
    "qkv_grad_feed0", "qkv_share", "qkv_grad", "unit_grad", "qkv_share", "up_grad", "up_grad", "vector", "qkv_grad",
    "qkv_grad", "qkv_grad_feed1", "qkv_grad_feed1", "qkv_grad_feed1", "qkv_grad", "unit_grad", "unit_grad_side",
    "qkv_grad", "qkv_grad", "qkv_grad", "unit_grad", "vector", "qkv_grad", "vector", "qkv_grad",
)


def layer_kernel(
    lens,
    x_in,
    cot_in,
    w_qkv,
    w_out,
    w_up,
    w_down,
    b_qkv,
    b_up,
    gains,
    biases,
    branch_sum,
    unit_sum,
    qkv_sum,
    up_sum,
    deep_sum,
    vector_sum,
    low_sum,
    unit,
    cot,
    wide,
    deep,
    up,
    q,
    k,
    v,
    acts,
    probs,
    branch,
    grads,
    mixed_grad,
    sums,
    low_sums,
    vectors,
    vector_slots,
    up_core,
    deep_core,
    qkv_slots,
    up_slots,
    deep_slots,
    branch_slots,
    unit_slots,
    branch_side_slots,
    unit_side_slots,
    branch_pairs,
    unit_pairs,
    qkv_last,
    up_last,
    deep_last,
    branch_last,
    unit_last,
    row_total,
    qkv_total,
    up_total,
    deep_total,
    send_sems,
    recv_sems,
    core_send,
    core_recv,
    load_sems,
    store_sems,
):
    spot = place()
    zh, y, core, zl, x = spot
    near = neighbours(spot)
    near["x2"] = device(zh, y, core, zl, around(x, 2))
    near["y2"] = device(zh, around(y, 2), core, zl, x)
    barrier = pltpu.get_barrier_semaphore()
    for target in near.values():
        pl.semaphore_signal(barrier, inc=1, device_id=target, device_id_type=MESH)

    mine = pl.ds(pl.multiple_of((zl * 4 + x) * OWN, OWN), OWN)
    own = pl.ds(pl.multiple_of(((zh * 4 + y) * 2 + core) * OWN, OWN), OWN)
    loads = []
    for src, dst in (
        (x_in, unit.at[mine, :]),
        *((w_qkv.at[head], qkv_total.at[:, pl.ds(head * HEAD, HEAD)]) for head in range(3)),
        (w_up, up_total),
        (w_out, deep_total.at[pl.ds(0, HEAD), :]),
        (w_down, deep_total.at[pl.ds(HEAD, UNITS), :]),
        (cot_in, cot.at[mine, :]),
    ):
        loads.append(pltpu.make_async_copy(src, dst, load_sems.at[len(loads)]))
        loads[-1].start()

    links = Links(send_sems, recv_sems)
    stores = []
    done = set()

    def store(src, dst):
        copy = pltpu.make_async_copy(src, dst, store_sems.at[len(stores)])
        copy.start()
        stores.append(copy)
        return copy

    def deep_part(z, ring, half):
        columns = pl.ds(pl.multiple_of(((z * 4 + ring) * 2 + core) * OWN, OWN), OWN)
        if half is None:
            return deep.at[:, columns]
        return deep.at[pl.ds(half * (DEEP // 2), DEEP // 2), columns]

    def deep_place(chip, who):
        return deep.at[:, pl.ds(pl.multiple_of((chip * 2 + who) * OWN, OWN), OWN)]

    def up_place(chip, who):
        return rows_of(up, (chip * 2 + who) * OWN, OWN)

    def qkv_place(chip, who):
        return rows_of(wide, (chip * 2 + who) * OWN, OWN).at[:, pl.ds(0, QKV)]

    shares = (
        (deep_place, lambda slot: deep_core.at[slot]),
        (up_place, lambda slot: up_core.at[slot]),
        (qkv_place, lambda slot: rows_of(probs, slot * OWN, OWN).at[:, pl.ds(0, QKV)]),
    )

    def chip_at(ring, turn_of):
        return (zh + (1 - 2 * zh) * turn_of) * 4 + around(y, ring)

    def core_copy(which, ring, turn_of):
        number = which * 8 + ring * 2 + turn_of
        place_of, slots = shares[which]
        return pltpu.make_async_remote_copy(
            src_ref=place_of(chip_at(ring, turn_of), 1 - core),
            dst_ref=slots(ring * 2 + turn_of),
            send_sem=core_send.at[number],
            recv_sem=core_recv.at[number],
            device_id=near["core"],
            device_id_type=MESH,
        )

    def share(which, name):
        place_of, slots = shares[which]

        def add(ring, turn_of):
            core_copy(which, ring, turn_of).wait_recv()
            part = place_of(chip_at(ring, turn_of), core)
            part[...] = (
                part[...].astype(F32) + slots(ring * 2 + turn_of)[...].astype(F32)
            ).astype(BF16)
            return ring

        for step in (2, 1, 3, 0):
            yield [(name + "_raw", step)]
            yield []
            lax.fori_loop(0, 2, lambda turn_of, _: add(step, turn_of), 0)
            done.add((name, step))

    def add_vectors():
        yield [("sums", "ready")]
        slot = 0
        for stage, (names, count) in enumerate(
            (
                (("core",), 96),
                (("y+", "y-", "y2"), 96),
                (("zh",), 96),
                (("zl",), 80),
                (("x+", "x-", "x2"), 80),
            )
        ):
            span = pl.ds(0, count)
            copies = [
                links.send(
                    vectors.at[stage, span], vector_slots.at[slot + index, span], near[name]
                )
                for index, name in enumerate(names)
            ]
            yield copies
            for copy in copies:
                copy.wait_recv()
            parts = [vectors[stage, :count, :]]
            parts += [vector_slots[slot + index, :count, :] for index in range(len(copies))]
            if len(parts) == 2:
                total = parts[0] + parts[1]
            else:
                total = (parts[0] + parts[3]) + (parts[1] + parts[2])
            vectors[stage + 1, :count, :] = total
            slot += len(names)
        for row in range(5):
            for column in range(16):
                sums[row : row + 1, column * 128 : (column + 1) * 128] = vectors[
                    5, row * 16 + column : row * 16 + column + 1, :
                ]
        for column in range(14):
            low_sums[0:1, column * 128 : (column + 1) * 128] = vectors[
                3, 80 + column : 81 + column, :
            ]
        store(sums, vector_sum)
        store(low_sums, low_sum)

    def keep(steps, src, dst):
        yield from steps
        store(src, dst)

    tensor_ends = (zl, x, near["zl"], near["x+"], near["x-"])
    side_ends = (zl, x, None, near["x+"], near["x-"], near["zl"])
    data_ends = (zh, y, near["zh"], near["y+"], near["y-"])
    units = Gather(links, row_part(unit, 0, MAIN_UNIT), *tensor_ends, None)
    units_side = Gather(links, row_part(unit, MAIN_UNIT, D - MAIN_UNIT), *side_ends)
    cots = Gather(links, row_part(cot, 0, MAIN_COT), *tensor_ends, None)
    cots_side = Gather(links, row_part(cot, MAIN_COT, D - MAIN_COT), *side_ends)
    wides = Gather(links, row_part(wide, 0, QKV, core), *data_ends, near["core"])
    wups = Gather(links, row_part(wide, QKV, UNITS, core), *data_ends, near["core"])
    deeps = Gather(links, deep_part, *data_ends, near["core"])

    side_branch = row_part(branch, MAIN_BRANCH, D - MAIN_BRANCH)
    side_grad = row_part(cot, MAIN_GRAD, D - MAIN_GRAD)
    branch_main = Scatter(
        links, row_part(branch, 0, MAIN_BRANCH), branch_slots, branch_last, *tensor_ends
    )
    branch_side = Scatter(links, side_branch, branch_side_slots, None, *tensor_ends)
    branch_pair = PairSum(links, side_branch, branch_pairs, zl, x, near["zl"])
    unit_main = Scatter(links, row_part(cot, 0, MAIN_GRAD), unit_slots, unit_last, *tensor_ends)
    unit_side = Scatter(links, side_grad, unit_side_slots, None, *tensor_ends)
    unit_pair = PairSum(links, side_grad, unit_pairs, zl, x, near["zl"])
    qkv_grid = Scatter(links, row_part(wide, 0, QKV, core), qkv_slots, qkv_last, *data_ends)
    up_grid = Scatter(links, row_part(up, 0, UNITS, core), up_slots, up_last, *data_ends)
    deep_grid = Scatter(links, deep_part, deep_slots, deep_last, *data_ends)
    go, free, turned = ("own", "ready"), ("rows", "free"), ("turn", "free")

    def late(name):
        return (name, "joined", 0) if name in LATE else go

    transfers = {
        "unit": units.own(("unit", "ready")),
        "unit_far": units.far(("unit", "sent")),
        "unit_side": units_side.own(("unit", "ready")),
        "cot": cots.own(("wide", "ready")),
        "cot_far": cots.far(("cot", "sent")),
        "cot_side": cots_side.own(("wide", "ready")),
        "wide": wides.own(("wide", "ready")),
        "wide_far": wides.far(("wide", "sent")),
        "wup": wups.own(("wide", "ready")),
        "wup_far": wups.far(("wup", "sent")),
        "deep": deeps.own(("wide", "ready")),
        "deep_far": deeps.far(("deep", "sent")),
        "branch_feed0": branch_main.feed("branch", 0, go, done),
        "branch_feed1": branch_main.feed("branch", 1, late("branch"), done),
        "branch": branch_main.run(
            "branch", row_total.at[:, pl.ds(0, MAIN_BRANCH)], turned, done
        ),
        "branch_pair": branch_pair.run("branch", "branch_side", done),
        "branch_side_feed0": branch_side.feed("branch_side", 0, go, done),
        "branch_side": branch_side.run(
            "branch_side", row_total.at[:, pl.ds(MAIN_BRANCH, D - MAIN_BRANCH)], turned, done
        ),
        "unit_grad_feed0": unit_main.feed("unit_grad", 0, go, done),
        "unit_grad_feed1": unit_main.feed("unit_grad", 1, late("unit_grad"), done),
        "unit_grad": unit_main.run(
            "unit_grad", row_total.at[:, pl.ds(0, MAIN_GRAD)], free, done
        ),
        "unit_grad_pair": unit_pair.run("unit_grad", "unit_grad_side", done),
        "unit_grad_side_feed0": unit_side.feed("unit_grad_side", 0, go, done),
        "unit_grad_side": unit_side.run(
            "unit_grad_side", row_total.at[:, pl.ds(MAIN_GRAD, D - MAIN_GRAD)], free, done
        ),
        "deep_share": share(0, "deep_grad"),
        "deep_grad_feed0": deep_grid.feed("deep_grad", 0, go, done),
        "deep_grad_feed1": deep_grid.feed("deep_grad", 1, late("deep_grad"), done),
        "deep_grad": keep(deep_grid.run("deep_grad", deep_total, go, done), deep_total, deep_sum),
        "up_share": share(1, "up_grad"),
        "up_grad_feed0": up_grid.feed("up_grad", 0, go, done),
        "up_grad_feed1": up_grid.feed("up_grad", 1, late("up_grad"), done),
        "up_grad": keep(up_grid.run("up_grad", up_total, go, done), up_total, up_sum),
        "qkv_share": share(2, "qkv_grad"),
        "qkv_grad_feed0": qkv_grid.feed("qkv_grad", 0, go, done),
        "qkv_grad_feed1": qkv_grid.feed("qkv_grad", 1, late("qkv_grad"), done),
        "qkv_grad": keep(qkv_grid.run("qkv_grad", qkv_total, go, done), qkv_total, qkv_sum),
        "vector": add_vectors(),
    }

    ends = [lens[0, 0]]
    for seq in range(1, 3):
        ends.append(ends[-1] + lens[0, seq])

    def begin_of(index):
        begin = jnp.zeros_like(index)
        for end in ends:
            begin = jnp.where(index >= end, end, begin)
        return begin

    def own_blocks():
        loads[0].wait()
        rows = unit[mine, :].astype(F32)
        centred = rows - jnp.mean(rows, axis=-1, keepdims=True)
        variance = jnp.mean(centred * centred, axis=-1, keepdims=True)
        unit[mine, :] = (centred * lax.rsqrt(variance + NORM_EPS)).astype(BF16)
        for load in loads[1:]:
            load.wait()
        wide[own, :QKV] = qkv_total[...].astype(BF16)
        wide[own, QKV:] = up_total[...].astype(BF16)
        deep[:, own] = deep_total[...].astype(BF16)
        pl.semaphore_wait(barrier, len(near))
        done.update([("unit", "ready"), ("wide", "ready"), go])

    def tables():
        sums[...] = jnp.zeros_like(sums)
        low_sums[...] = jnp.zeros_like(low_sums)
        sums[4:5, :] = jnp.sum(cot[mine, :].astype(F32), axis=0, keepdims=True)
        row = lax.broadcasted_iota(jnp.int32, (OWN, 128), 0)
        lane = lax.broadcasted_iota(jnp.int32, (OWN, 128), 1)
        rate = jnp.exp(lax.rem(lane, 32).astype(F32) * (-2.0 * math.log(10000.0) / ROT))
        for block in range(TOK // OWN):
            index = row + block * OWN
            angle = (index - begin_of(index)).astype(F32) * rate
            columns = slice(block * 128, (block + 1) * 128)
            row_total[:, columns] = jnp.where(lane < ROT, jnp.cos(angle), 1.0)
            columns = slice(TOK + block * 128, TOK + (block + 1) * 128)
            row_total[:, columns] = jnp.where(lane < ROT, jnp.sin(angle), 0.0)

    def turn(which, part):
        blocks = range(part.start // OWN, part.stop // OWN)
        starts = [which * TOK + block * 128 for block in blocks]
        return jnp.concatenate([row_total[:, start : start + 128] for start in starts], axis=0)

    def norm_tile(tile, which):
        part = slice(tile * TILE, (tile + 1) * TILE)
        span = slice(which * TILE, (which + 1) * TILE)
        rows = unit[part, :].astype(F32)
        branch[span, :] = (
            rows * gains[which : which + 1, :] + biases[which : which + 1, :]
        ).astype(BF16)

    def heads(tile):
        part = slice(tile * TILE, (tile + 1) * TILE)
        norm_tile(tile, 0)
        for which, target in enumerate((q, k, v)):
            columns = slice(which * HEAD, (which + 1) * HEAD)
            head = jnp.dot(branch[:TILE, :], wide[:, columns], preferred_element_type=F32)
            head = head + b_qkv[which : which + 1, :]
            if which < 2:
                head = spin(head, turn(0, part), turn(1, part), False)
            target[part, :] = head.astype(BF16)

    def hidden(tile, half):
        part = slice(tile * TILE, (tile + 1) * TILE)
        if half == 0:
            norm_tile(tile, 1)

        def one(piece, _):
            shift = pl.multiple_of(piece * 256, 256)
            pre = jnp.dot(
                branch[TILE:, :], wide[:, pl.ds(QKV + shift, 256)], preferred_element_type=F32
            )
            pre = pre + b_up[0:1, pl.ds(shift, 256)]
            value, rise = gelu_parts(pre)
            acts[part, pl.ds(HEAD + shift, 256)] = value.astype(BF16)
            grads[part, pl.ds(QKV + shift, 256)] = rise.astype(BF16)
            return 0

        lax.fori_loop(2 * half, 2 * half + 2, one, 0)

    def attend(block):
        part = slice(block * QROWS, (block + 1) * QROWS)
        keys = (block + 1) * QROWS
        whole = by_rows(q[part, :], k[:keys, :]) * (HEAD**-0.5)
        for start in range(0, QROWS, OWN):
            scores = whole[start : start + OWN]
            start = block * QROWS + start
            key = lax.broadcasted_iota(jnp.int32, (OWN, keys), 1)
            row = lax.broadcasted_iota(jnp.int32, (OWN, 1), 0) + start
            scores = jnp.where((key <= row) & (key >= begin_of(row)), scores, -jnp.inf)
            expo = jnp.exp(scores - jnp.max(scores, axis=-1, keepdims=True))
            mass = expo / jnp.sum(expo, axis=-1, keepdims=True)
            probs[start : start + OWN, :keys] = mass.astype(BF16)
        acts[part, :HEAD] = jnp.dot(
            probs[part, :keys], v[:keys, :], preferred_element_type=F32
        ).astype(BF16)

    def pieces_of(ring):
        starts = (around(x, ring) * OWN, (4 + around(x, ring)) * OWN)
        return [pl.ds(pl.multiple_of(start, OWN), OWN) for start in starts]

    def mix(step):
        pieces = pieces_of(step)

        def one(piece, _):
            columns = pl.ds(pl.multiple_of(piece * 512, 512), 512)
            rows = jnp.concatenate([acts[each, :] for each in pieces], axis=0)
            both = jnp.dot(rows, deep[:, columns], preferred_element_type=F32).astype(BF16)
            branch[pieces[0], columns] = both[:OWN]
            branch[pieces[1], columns] = both[OWN:]
            return 0

        lax.fori_loop(0, D // 512, one, 0)
        done.add(("branch", step))

    def back(tile, half):
        part = slice(tile * TILE, (tile + 1) * TILE)
        if half == 0:
            mixed_grad[part, :] = by_rows(cot[part, :], deep[:HEAD, :]).astype(BF16)

        def one(piece, _):
            shift = pl.multiple_of(piece * 256, 256)
            columns = pl.ds(QKV + shift, 256)
            grad = by_rows(cot[part, :], deep[pl.ds(HEAD + shift, 256), :])
            grad = grad * grads[part, columns].astype(F32)
            low_sums[0:1, columns] += jnp.sum(grad, axis=0, keepdims=True)
            grads[part, columns] = grad.astype(BF16)
            return 0

        lax.fori_loop(2 * half, 2 * half + 2, one, 0)

    def deep_grads(step):
        if step == 2:
            links.settle(deeps.sent)

        def one(turn_of, _):
            columns = pl.ds(pl.multiple_of(chip_at(step, turn_of) * 256, 256), 256)
            for half in range(2):
                part = slice(half * (DEEP // 2), (half + 1) * (DEEP // 2))
                deep[part, columns] = over_rows(acts[:, part], cot[:, columns]).astype(BF16)
            core_copy(0, step, turn_of).start()
            return 0

        lax.fori_loop(0, 2, one, 0)
        done.add(("deep_grad_raw", step))

    def norm_columns(span, which):
        acts[:, :256] = (
            unit[:, span].astype(F32) * gains[which : which + 1, span]
            + biases[which : which + 1, span]
        ).astype(BF16)

    def up_grads(step):
        def one(turn_of, _):
            span = pl.ds(pl.multiple_of(chip_at(step, turn_of) * 256, 256), 256)
            norm_columns(span, 1)
            up[span, :] = over_rows(acts[:, :256], grads[:, QKV:]).astype(BF16)
            core_copy(1, step, turn_of).start()
            return 0

        lax.fori_loop(0, 2, one, 0)
        done.add(("up_grad_raw", step))

    def qkv_grads(step):
        if step == 2:
            links.settle(wides.sent)

        def one(turn_of, _):
            span = pl.ds(pl.multiple_of(chip_at(step, turn_of) * 256, 256), 256)
            norm_columns(span, 0)
            wide[span, :QKV] = over_rows(acts[:, :256], grads[:, :QKV]).astype(BF16)
            core_copy(2, step, turn_of).start()
            return 0

        lax.fori_loop(0, 2, one, 0)
        done.add(("qkv_grad_raw", step))

    def put_grad(grad, part, which):
        columns = slice(which * HEAD, (which + 1) * HEAD)
        if which < 2:
            grad = spin(grad * (HEAD**-0.5), turn(0, part), turn(1, part), True)
        low_sums[0:1, columns] += jnp.sum(grad, axis=0, keepdims=True)
        grads[part, columns] = grad.astype(BF16)

    def value_grads():
        for block in range(TOK // QROWS):
            part = slice(block * QROWS, (block + 1) * QROWS)
            below = slice(block * QROWS, TOK)
            put_grad(over_rows(probs[below, part], mixed_grad[below, :]), part, 2)

    def query_grads(block):
        part = slice(block * QROWS, (block + 1) * QROWS)
        keys = (block + 1) * QROWS
        whole = by_rows(mixed_grad[part, :], v[:keys, :])
        for start in range(0, QROWS, OWN):
            prob_grad = whole[start : start + OWN]
            rows = slice(block * QROWS + start, block * QROWS + start + OWN)
            mass = probs[rows, :keys].astype(F32)
            delta = jnp.sum(mass * prob_grad, axis=-1, keepdims=True)
            probs[rows, :keys] = (mass * (prob_grad - delta)).astype(BF16)
        put_grad(jnp.dot(probs[part, :keys], k[:keys, :], preferred_element_type=F32), part, 0)

    def key_grads():
        for block in range(TOK // QROWS):
            part = slice(block * QROWS, (block + 1) * QROWS)
            below = slice(block * QROWS, TOK)
            put_grad(over_rows(probs[below, part], q[below, :]), part, 1)
        done.add(turned)

    def unit_grads(step):
        if step == 2:
            links.settle(cots.sent + cots_side.sent)
        pieces = pieces_of(step)
        for half in range(2):
            acts[half * OWN : (half + 1) * OWN, :QKV] = grads[pieces[half], :QKV]
            acts[(2 + half) * OWN : (3 + half) * OWN, :UNITS] = grads[pieces[half], QKV:]

        def one(piece, _):
            columns = pl.ds(pl.multiple_of(piece * 512, 512), 512)
            first = by_rows(acts[: 2 * OWN, :QKV], wide[columns, :QKV])
            second = by_rows(acts[2 * OWN : 4 * OWN, :UNITS], wide[columns, QKV:])
            rows = jnp.concatenate([unit[each, columns] for each in pieces], axis=0).astype(F32)
            sums[0:1, columns] += jnp.sum(first * rows, axis=0, keepdims=True)
            sums[1:2, columns] += jnp.sum(second * rows, axis=0, keepdims=True)
            sums[2:3, columns] += jnp.sum(first, axis=0, keepdims=True)
            sums[3:4, columns] += jnp.sum(second, axis=0, keepdims=True)
            both = (first * gains[0:1, columns] + second * gains[1:2, columns]).astype(BF16)
            cot[pieces[0], columns] = both[:OWN]
            cot[pieces[1], columns] = both[OWN:]
            return 0

        lax.fori_loop(0, D // 512, one, 0)
        done.add(("unit_grad", step))

    def pack():
        for row in range(5):
            for column in range(16):
                vectors[0, row * 16 + column : row * 16 + column + 1, :] = sums[
                    row : row + 1, column * 128 : (column + 1) * 128
                ]
        for column in range(14):
            vectors[0, 80 + column : 81 + column, :] = low_sums[
                0:1, column * 128 : (column + 1) * 128
            ]
        vectors[0, 94:96, :] = jnp.zeros((2, 128), F32)
        done.add(("sums", "ready"))

    branch_stores = []

    def branch_out():
        branch_stores.append(pltpu.make_async_copy(row_total, branch_sum, store_sems.at[7]))
        branch_stores[0].start()
        branch_stores[0].wait()
        done.add(free)

    compute = {
        ".init": own_blocks,
        ".tables": tables,
        ".dv": value_grads,
        ".dk": key_grads,
        ".pack": pack,
        ".branch_out": branch_out,
    }
    for tile in range(TOK // TILE):
        compute[f".qkv{tile}"] = functools.partial(heads, tile)
        for half, letter in enumerate("ab"):
            compute[f".hid{tile}{letter}"] = functools.partial(hidden, tile, half)
            compute[f".back{tile}{letter}"] = functools.partial(back, tile, half)
    for step in range(4):
        compute[f".att{step}"] = functools.partial(attend, step)
        compute[f".dp{step}"] = functools.partial(query_grads, step)
        compute[f".mix{step}"] = functools.partial(mix, step)
        compute[f".deepg{step}"] = functools.partial(deep_grads, step)
        compute[f".upg{step}"] = functools.partial(up_grads, step)
        compute[f".qg{step}"] = functools.partial(qkv_grads, step)
        compute[f".g{step}"] = functools.partial(unit_grads, step)

    waiting = {name: next(steps) for name, steps in transfers.items()}
    for name in ORDER:
        if name in compute:
            compute.pop(name)()
            continue
        assert all(each in done for each in waiting[name] if isinstance(each, tuple)), name
        waiting[name] = next(transfers[name], None)
        done.add((name, "sent"))
        if waiting[name] is None:
            del waiting[name]
    assert not waiting and not compute
    store(row_total, unit_sum)

    for which in range(3):
        for step in range(4):
            for turn_of in range(2):
                core_copy(which, step, turn_of).wait_send()
    for copy in stores:
        copy.wait()
    links.settle(links.open)


SUMS = (
    ((OWN, D), F32),
    ((OWN, D), F32),
    ((OWN, QKV), F32),
    ((OWN, UNITS), F32),
    ((DEEP, OWN), F32),
    ((8, D), F32),
    ((8, WIDE), F32),
)
HALF = OWN // 2
SCRATCH = (
    ((TOK, D), BF16),
    ((TOK, D), BF16),
    ((D, WIDE), BF16),
    ((DEEP, D), BF16),
    ((D, UNITS), BF16),
    ((TOK, HEAD), BF16),
    ((TOK, HEAD), BF16),
    ((TOK, HEAD), BF16),
    ((TOK, DEEP), BF16),
    ((TOK, TOK), BF16),
    ((TOK, D), BF16),
    ((TOK, WIDE), BF16),
    ((TOK, HEAD), BF16),
    ((8, D), F32),
    ((8, WIDE), F32),
    ((6, 96, 128), F32),
    ((9, 96, 128), F32),
    ((8, OWN, UNITS), BF16),
    ((8, DEEP, OWN), BF16),
    ((2, 3, 2, HALF, QKV), BF16),
    ((2, 3, 2, HALF, UNITS), BF16),
    ((2, 3, 2, DEEP // 2, OWN), BF16),
    ((2, 3, 2, HALF, MAIN_BRANCH), BF16),
    ((2, 3, 2, HALF, MAIN_GRAD), BF16),
    ((2, 3, 1, HALF, D - MAIN_BRANCH), BF16),
    ((2, 3, 1, HALF, D - MAIN_GRAD), BF16),
    ((4, OWN, D - MAIN_BRANCH), BF16),
    ((4, OWN, D - MAIN_GRAD), BF16),
    ((OWN, QKV), BF16),
    ((OWN, UNITS), BF16),
    ((DEEP, OWN), BF16),
    ((OWN, MAIN_BRANCH), BF16),
    ((OWN, MAIN_GRAD), BF16),
    ((OWN, D), F32),
    ((OWN, QKV), F32),
    ((OWN, UNITS), F32),
    ((DEEP, OWN), F32),
)


def run_layer(lens, layer_in, cotangent, w_qkv, w_out, w_up, w_down, *vectors):
    anywhere = pl.BlockSpec(memory_space=pl.ANY)
    vmem = pl.BlockSpec(memory_space=pltpu.VMEM)
    return pl.pallas_call(
        layer_kernel,
        out_shape=[jax.ShapeDtypeStruct(*each) for each in SUMS],
        in_specs=[pl.BlockSpec(memory_space=pltpu.SMEM)] + [anywhere] * 6 + [vmem] * len(vectors),
        out_specs=[anywhere] * len(SUMS),
        scratch_shapes=[pltpu.VMEM(*each) for each in SCRATCH]
        + [
            pltpu.SemaphoreType.DMA((180,)),
            pltpu.SemaphoreType.DMA((180,)),
            pltpu.SemaphoreType.DMA((24,)),
            pltpu.SemaphoreType.DMA((24,)),
            pltpu.SemaphoreType.DMA((8,)),
            pltpu.SemaphoreType.DMA((8,)),
        ],
        compiler_params=pltpu.CompilerParams(
            collective_id=0, has_side_effects=True, vmem_limit_bytes=63 * 2**20
        ),
        cost_estimate=pl.CostEstimate(flops=42 * 10**9, bytes_accessed=10**7, transcendentals=0),
        name="layer",
    )(lens, layer_in, cotangent, w_qkv, w_out, w_up, w_down, *vectors)


def adam_step(weight, gradient, moment_one, moment_two, step_rate, decay_rate):
    moment_one = BETA_ONE * moment_one + (1.0 - BETA_ONE) * gradient
    moment_two = BETA_TWO * moment_two + (1.0 - BETA_TWO) * gradient * gradient
    spread = jnp.sqrt(moment_two * (1.0 / (1.0 - BETA_TWO**STEP))) + ADAM_EPS
    ratio = moment_one * (1.0 / (1.0 - BETA_ONE**STEP)) / spread
    return (moment_one, moment_two, weight - step_rate * (ratio + decay_rate * weight))


BIG = 14
AHEAD = 4


def update_kernel(*refs):
    sums, refs = refs[:7], refs[7:]
    big, refs = refs[:BIG], refs[BIG:]
    small, refs = refs[:12], refs[12:]
    big_out, refs = refs[:BIG], refs[BIG:]
    small_out, refs = refs[:12], refs[12:]
    sum_bufs, refs = refs[:7], refs[7:]
    in_bufs, refs = refs[:BIG], refs[BIG:]
    small_bufs, refs = refs[:12], refs[12:]
    row_bufs, bias_rows, load_sems, store_sems = refs[:2], refs[2], refs[3], refs[4]
    branch, unit_grad, qkv, up, deep, vectors, low_vectors = sum_bufs
    loads, stores = [], []

    def fetch(src, dst):
        copy = pltpu.make_async_copy(src, dst, load_sems.at[len(loads)])
        loads.append(copy)
        copy.start()
        return copy

    def put(src, dst):
        copy = pltpu.make_async_copy(src, dst, store_sems.at[len(stores)])
        stores.append(copy)
        copy.start()

    def matrix(which, at, sum_index, sum_at, gradient_of):
        first = 2 + 3 * which

        def start():
            copies = [fetch(sums[sum_index].at[sum_at], sum_bufs[sum_index].at[sum_at])]
            for index in range(first, first + 3):
                copies.append(fetch(big[index].at[at], in_bufs[index].at[at]))
            return copies

        def finish():
            weight, one, two = (each.at[at] for each in in_bufs[first : first + 3])
            for part, gradient in gradient_of(sum_bufs[sum_index].at[sum_at]):
                results = adam_step(
                    weight[part],
                    gradient,
                    one[part],
                    two[part],
                    STEP_RATES[which],
                    DECAY_RATES[which],
                )
                one[part], two[part], weight[part] = results
            for index, src in enumerate((one, two, weight)):
                put(src, big_out[first + index].at[at])

        return start, finish

    def plain(ref):
        return [(slice(None), ref[...])]

    def by_head(ref):
        return [(head, ref[:, head * HEAD : (head + 1) * HEAD]) for head in range(3)]

    def rows_part(at):
        def start():
            return [
                fetch(src.at[at], dst.at[at])
                for src, dst in (
                    (big[0], in_bufs[0]),
                    (big[1], in_bufs[1]),
                    (sums[0], branch),
                    (sums[1], unit_grad),
                )
            ]

        def finish():
            biases = bias_rows
            resid = in_bufs[0][at, :].astype(F32)
            total = resid + branch[at, :] + biases[2:3, :] + biases[3:4, :]
            row_bufs[0][at, :] = total.astype(BF16)
            put(row_bufs[0].at[at], big_out[0].at[at])
            centred = resid - jnp.mean(resid, axis=-1, keepdims=True)
            inverse = lax.rsqrt(jnp.mean(centred * centred, axis=-1, keepdims=True) + NORM_EPS)
            unit = centred * inverse
            grad = unit_grad[at, :]
            mean = jnp.mean(grad, axis=-1, keepdims=True)
            along = jnp.mean(grad * unit, axis=-1, keepdims=True)
            back = in_bufs[1][at, :].astype(F32) + inverse * (grad - mean - unit * along)
            row_bufs[1][at, :] = back
            put(row_bufs[1].at[at], big_out[1].at[at])

        return start, finish

    def vector_part():
        def start():
            copies = [fetch(sums[index], sum_bufs[index]) for index in (5, 6)]
            return copies + [fetch(*each) for each in zip(small, small_bufs)]

        def finish():
            slots = (
                (0, 4, [low_vectors[0:1, head * HEAD : (head + 1) * HEAD] for head in range(3)]),
                (3, 5, [low_vectors[0:1, QKV:]]),
                (6, 6, [vectors[0:1, :], vectors[1:2, :]]),
                (9, 7, [vectors[2:3, :], vectors[3:4, :], vectors[4:5, :], vectors[4:5, :]]),
            )
            bias_rows[...] = small_bufs[9][...]
            for first, which, gradients in slots:
                weight, one, two = small_bufs[first : first + 3]
                for row, gradient in enumerate(gradients):
                    at = slice(row, row + 1)
                    results = adam_step(
                        weight[at, :],
                        gradient,
                        one[at, :],
                        two[at, :],
                        STEP_RATES[which],
                        DECAY_RATES[which],
                    )
                    one[at, :], two[at, :], weight[at, :] = results
                for index, src in enumerate((one, two, weight)):
                    put(src, small_out[first + index])

        return start, finish

    halves = [pl.ds(0, OWN // 2), pl.ds(OWN // 2, OWN // 2)]
    parts = [matrix(1, slice(None), 4, pl.ds(0, HEAD), plain)]
    for start in (0, UNITS // 2):
        at = pl.ds(start, UNITS // 2)
        parts.append(matrix(3, at, 4, pl.ds(HEAD + start, UNITS // 2), plain))
    parts += [matrix(2, at, 3, at, plain) for at in halves]
    parts += [matrix(0, (slice(None), at), 2, at, by_head) for at in halves]
    parts.insert(0, vector_part())
    parts += [rows_part(at) for at in halves]
    copies = [start() for start, _ in parts[:AHEAD]]
    for index, (_, finish) in enumerate(parts):
        if index + AHEAD < len(parts):
            copies.append(parts[index + AHEAD][0]())
        for copy in copies[index]:
            copy.wait()
        finish()
    for copy in stores:
        copy.wait()


def run_update(sums, big, small):
    anywhere = pl.BlockSpec(memory_space=pl.ANY)
    matrices = [jax.ShapeDtypeStruct(each.shape, F32) for each in big[2:]]
    rows = [jax.ShapeDtypeStruct((OWN, D), BF16), jax.ShapeDtypeStruct((OWN, D), F32)]
    return pl.pallas_call(
        update_kernel,
        out_shape=rows + matrices + [jax.ShapeDtypeStruct(each.shape, F32) for each in small],
        in_specs=[anywhere] * (len(sums) + BIG + 12),
        out_specs=[anywhere] * (BIG + 12),
        scratch_shapes=[pltpu.VMEM(each.shape, F32) for each in sums]
        + [pltpu.VMEM(each.shape, each.dtype) for each in big]
        + [pltpu.VMEM(each.shape, F32) for each in small]
        + [pltpu.VMEM((OWN, D), BF16), pltpu.VMEM((OWN, D), F32), pltpu.VMEM((4, D), F32)]
        + [pltpu.SemaphoreType.DMA((64,)), pltpu.SemaphoreType.DMA((48,))],
        compiler_params=pltpu.CompilerParams(vmem_limit_bytes=63 * 2**20),
        cost_estimate=pl.CostEstimate(flops=10**7, bytes_accessed=16 * 10**6, transcendentals=0),
        name="update",
    )(*sums, *big, *small)


def local(layer_in, cotangent, seq_lengths, *state):
    params, moments = list(state[:8]), list(state[8:])
    params[0] = params[0].transpose(1, 0, 2)
    moments[0], moments[1] = (each.transpose(1, 0, 2) for each in moments[:2])
    params[5] = params[5].reshape(1, UNITS)
    moments[10], moments[11] = (each.reshape(1, UNITS) for each in moments[10:12])
    sums = run_layer(seq_lengths, layer_in, cotangent, *params)
    groups = [(params[which], moments[2 * which], moments[2 * which + 1]) for which in range(8)]
    big = [layer_in, cotangent] + [each for group in groups[:4] for each in group]
    small = [each for group in groups[4:] for each in group]
    results = list(run_update(sums, big, small))
    for index in range(2, 5):
        results[index] = results[index].transpose(1, 0, 2)
    for index in range(17, 20):
        results[index] = results[index].reshape(UNITS)
    return tuple(results)


def solution(mesh):
    rows = P(("dp", "tensor"), None)
    out, up = P("tensor", "dp"), P("dp", "tensor")
    params = (P("dp", None, "tensor"), out, up, out, P(None, "tensor"), P("tensor"), P(), P())
    moments = [spec for spec in params for _ in range(2)]
    return jax.shard_map(
        local,
        mesh=mesh,
        in_specs=(rows, rows, P("dp", None), *params, *moments),
        out_specs=(rows, rows, *[spec for spec in params for _ in range(3)]),
        check_vma=False,
    )
```

```python
import functools
import math

import jax
import jax.numpy as jnp
from jax import lax
from jax.experimental import pallas as pl
from jax.experimental.pallas import tpu as pltpu
from jax.sharding import PartitionSpec as P

F32 = jnp.float32
BF16 = jnp.bfloat16
MESH = pl.DeviceIdType.MESH

D = 2048
HEAD = 256
QKV = 3 * HEAD
UNITS = 1024
WIDE = QKV + UNITS
DEEP = HEAD + UNITS
TOK = 1024
OWN = 128
TILE = 512
MAIN_UNIT, MAIN_COT, MAIN_BRANCH, MAIN_GRAD = 1536, 1280, 1536, 1536
CHUNKS = (2, 2, 2, 2)
QROWS = 256
ROT = 64
STEP = 10

NORM_EPS = 1e-05
BETA_ONE = 0.9
BETA_TWO = 0.95
ADAM_EPS = 1e-08
STEP_RATES = (0.04, 0.2, 0.04, 0.02, 0.3, 0.3, 0.5, 0.3)
DECAY_RATES = (0.01, 0.01, 0.01, 0.01, 0.0, 0.0, 0.0, 0.0)


def place():
    dp = lax.axis_index("dp")
    tensor = lax.axis_index("tensor")
    return (
        lax.div(dp, 8),
        lax.rem(lax.div(dp, 2), 4),
        lax.rem(dp, 2),
        lax.div(tensor, 4),
        lax.rem(tensor, 4),
    )


def device(zh, y, core, zl, x):
    return ((zh * 4 + y) * 2 + core, zl * 4 + x)


def around(pos, step):
    return lax.rem(pos + step + 4, 4)


def neighbours(spot):
    zh, y, core, zl, x = spot
    return {
        "x+": device(zh, y, core, zl, around(x, 1)),
        "x-": device(zh, y, core, zl, around(x, -1)),
        "y+": device(zh, around(y, 1), core, zl, x),
        "y-": device(zh, around(y, -1), core, zl, x),
        "zl": device(zh, y, core, 1 - zl, x),
        "zh": device(1 - zh, y, core, zl, x),
        "core": device(zh, y, 1 - core, zl, x),
    }


class Links:
    def __init__(self, send_sems, recv_sems):
        self.send_sems, self.recv_sems = send_sems, recv_sems
        self.copies, self.open = [], []

    def send(self, src, dst, target):
        index = len(self.copies)
        copy = pltpu.make_async_remote_copy(
            src_ref=src,
            dst_ref=dst,
            send_sem=self.send_sems.at[index],
            recv_sem=self.recv_sems.at[index],
            device_id=target,
            device_id_type=MESH,
        )
        copy.start()
        self.copies.append(copy)
        self.open.append(copy)
        return copy

    def settle(self, copies):
        for copy in copies:
            copy.wait_send()
        self.open = [each for each in self.open if not any(each is copy for copy in copies)]


class Gather:
    def __init__(self, links, block, z, ring, z_dev, plus, minus, onward):
        self.links, self.block, self.z, self.ring = links, block, z, ring
        self.z_dev, self.ways, self.onward = z_dev, (plus, minus), onward
        self.by_z, self.sent = None, []

    def to(self, z, ring, half, target):
        part = self.block(z, ring, half)
        self.sent.append(self.links.send(part, part, target))
        return self.sent[-1]

    def round(self, z):
        passed = []

        def pass_on(ring):
            if self.onward is not None:
                passed.append(self.to(z, ring, None, self.onward))

        whole = [self.to(z, self.ring, None, way) for way in self.ways]
        pass_on(self.ring)
        halves = []
        for way in range(2):
            yield [whole[way]]
            whole[way].wait_recv()
            from_ring = around(self.ring, 1 if way else -1)
            halves.append(self.to(z, from_ring, way, self.ways[way]))
            pass_on(from_ring)
        yield halves
        for copy in halves:
            copy.wait_recv()
        pass_on(around(self.ring, 2))
        yield passed
        for copy in passed:
            copy.wait_recv()

    def own(self, gate):
        yield [gate]
        if self.z_dev is not None:
            self.by_z = self.to(self.z, self.ring, None, self.z_dev)
        yield from self.round(self.z)

    def far(self, gate):
        yield [gate]
        yield [self.by_z]
        self.by_z.wait_recv()
        yield from self.round(1 - self.z)


class Scatter:
    def __init__(self, links, part, slots, last, z, ring, z_dev, plus, minus):
        self.links, self.part, self.slots, self.last = links, part, slots, last
        self.ring, self.z_dev, self.ways = ring, z_dev, (plus, minus)
        self.zs = (z,) if last is None else (1 - z, z)
        self.sent = {}

    def push(self, way, message, order, ring, half):
        self.sent[way, message, order] = self.links.send(
            self.part(self.zs[order], ring, half),
            self.slots.at[way, message, order],
            self.ways[way],
        )

    def arrived(self, way, message, order):
        self.sent[way, message, order].wait_recv()
        return self.slots[way, message, order].astype(F32)

    def total(self, order, half):
        part = self.part(self.zs[order], self.ring, half)
        return (
            part[...].astype(F32) + self.arrived(half, 2, order) + self.arrived(1 - half, 1, order)
        )

    def feed(self, name, order, gate, done, which=0):
        yield [gate, (name, 2)]
        for way in range(2):
            self.push(way, 0, order, around(self.ring, 2), way)
        for way, step in ((0, 1), (1, 3)):
            yield [(name, step)]
            self.push(way, 1, order, around(self.ring, step), 1 - way)
        done.add((name, "fed", order, which))

    def run(self, name, out, gate, done, which=0):
        for order in range(len(self.zs)):
            yield [(name, "fed", order, which)]
            for way in range(2):
                yield [self.sent[way, 0, order]]
                ring = around(self.ring, -1 if way else 1)
                part = self.part(self.zs[order], ring, way)
                part[...] = (part[...].astype(F32) + self.arrived(way, 0, order)).astype(BF16)
                self.push(way, 2, order, ring, way)
            done.add((name, "joined", order, which))
        by_z = None
        if self.last is not None:
            yield [(name, 0)] + [self.sent[way, each, 0] for way in range(2) for each in (1, 2)]
            for half in range(2):
                part = self.part(self.zs[0], self.ring, half)
                part[...] = self.total(0, half).astype(BF16)
            by_z = self.links.send(self.part(self.zs[0], self.ring, None), self.last, self.z_dev)
        order = len(self.zs) - 1
        yield [(name, 0), gate] + [
            self.sent[way, each, order] for way in range(2) for each in (1, 2)
        ]
        rows = out.shape[0] // 2
        for half in range(2):
            out[pl.ds(half * rows, rows), :] = self.total(order, half)
        if by_z is not None:
            yield [by_z]
            by_z.wait_recv()
            out[...] = out[...] + self.last[...].astype(F32)


class PairSum:
    def __init__(self, links, part, slots, z, ring, z_dev):
        self.links, self.part, self.slots = links, part, slots
        self.z, self.ring, self.z_dev = z, ring, z_dev

    def run(self, name, flag, done):
        for step in (2, 1, 3, 0):
            yield [(name, step)]
            part = self.part(1 - self.z, around(self.ring, step), None)
            moved = self.links.send(part, self.slots.at[step], self.z_dev)
            yield [moved]
            moved.wait_recv()
            part = self.part(self.z, around(self.ring, step), None)
            part[...] = (part[...].astype(F32) + self.slots[step].astype(F32)).astype(BF16)
            done.add((flag, step))


def rows_of(ref, start, count):
    return ref.at[pl.ds(pl.multiple_of(start, 16), count)]


def row_part(ref, first, count, core=None):
    def part(z, ring, half):
        index, rows = z * 4 + ring, OWN
        if core is not None:
            index = index * 2 + core
        start = index * OWN
        if half is not None:
            start, rows = start + half * (OWN // 2), OWN // 2
        return ref.at[pl.ds(pl.multiple_of(start, 16), rows), pl.ds(first, count)]

    return part


def over_rows(left, right):
    return lax.dot_general(left, right, (((0,), (0,)), ((), ())), preferred_element_type=F32)


def by_rows(left, right):
    return lax.dot_general(left, right, (((1,), (1,)), ((), ())), preferred_element_type=F32)


def gelu_parts(pre):
    cdf = 0.5 * (1.0 + lax.erf(pre * (1.0 / math.sqrt(2.0))))
    density = jnp.exp(-0.5 * pre * pre) * (1.0 / math.sqrt(2.0 * math.pi))
    return pre * cdf, cdf + pre * density


def spin(rows, cosines, sines, back):
    low = rows[:, :128]
    lane = lax.broadcasted_iota(jnp.int32, low.shape, 1)
    ahead = pltpu.roll(low, 96, 1)
    behind = pltpu.roll(low, 32, 1)
    turned = jnp.where(lane < 32, -ahead, jnp.where(lane < 64, behind, 0.0))
    if back:
        turned = -turned
    return jnp.concatenate([low * cosines + turned * sines, rows[:, 128:]], axis=1)


LATE = ("branch", "unit_grad", "up_grad", "qkv_grad",)
ORDER = (
    ".init", "wide", "wide_far", ".rows", "unit0", "unit_side", "unit0_far", "unit1", "unit1_far", ".weights", "wup",
    "wup_far", "deep", "deep_far", ".tables", "wide", "wide", "wide_far", "unit0", "unit0", "unit_side", "unit_side",
    "unit0_far", "wup", "wup", "unit1", "unit1", "unit0", "unit0", "unit1_far", "unit_side", "cot0", "cot_side",
    "cot0_far", "cot1", "cot1_far", "deep", "deep", "wide", "unit0_far", "unit0_far", "wide", "wup_far", "unit1",
    "unit1", "wide_far", "wide_far", "wup", "unit1_far", "unit1_far", "wup", "deep_far", "deep", "cot0", "cot0",
    "deep", "cot_side", "cot_side", "wup_far", "wup_far", "unit_side", "wide_far", "cot1", "cot1", "wide_far",
    "unit0_far", "unit0_far", "cot0_far", "unit1_far", "unit1_far", ".qkv0", "cot0", "cot0", ".qkv1", "deep_far",
    "deep_far", ".att0", "cot_side", ".att1", ".att2", "wup_far", ".att3", "cot1_far", "cot1", "cot1", "wup_far",
    ".hid0a", ".hid0b", "cot0_far", "cot0_far", "deep_far", ".hid1a", ".hid1b", "deep_far", ".mix2", "branch0_feed0",
    "cot1_far", "cot1_far", "branch_pair", "branch1_feed0", ".mix1", "branch0_feed0", "cot0_far", "cot0_far",
    "branch1_feed0", ".mix3", "branch0_feed0", "branch0", "branch1_feed0", "branch1", ".mix0", "branch0", "branch0",
    "branch0_feed1", "branch0_feed1", "branch0_feed1", "branch0", "cot_side", "cot1_far", "cot1_far", ".back0a",
    ".back0b", "branch1", "branch1", "branch_pair", "branch_side_feed0", "branch_pair", "branch1_feed1",
    "branch1_feed1", "branch1_feed1", "branch1", ".back1a", ".back1b", ".deepg2", "branch_pair", "branch_side_feed0",
    "branch_pair", "deep_share", ".dv", ".deepg1", "branch0", "branch0", "branch0", "deep_share", "deep_grad_feed0",
    "deep_grad_feed1", "deep_share", ".deepg3", "branch_pair", "branch_side_feed0", "branch_side", "branch_pair",
    "deep_share", "deep_grad_feed0", "deep_grad_feed1", "deep_share", ".dp0", ".dp1", ".dp2", ".dp3", ".dk",
    "branch_side", "branch_side", "deep_share", "deep_grad_feed0", "deep_grad_feed1", "deep_grad", "deep_grad",
    "deep_grad", "deep_grad", ".deepg0", "branch1", "branch1", "branch1", "deep_share", ".g2", "unit_grad0_feed0",
    "branch_pair", "unit_grad1_feed0", "deep_grad", "deep_grad", "unit_grad_pair", "deep_share", ".g1",
    "unit_grad0_feed0", "branch0", "branch0", "unit_grad1_feed0", ".g3", "unit_grad0_feed0", "unit_grad0",
    "branch_side", "unit_grad1_feed0", "unit_grad1", ".g0", "branch1", "branch1", "unit_grad_pair",
    "unit_grad_side_feed0", "unit_grad_pair", ".pack", "vector", ".upg2", "unit_grad0", "unit_grad0", "vector",
    "up_share", "unit_grad0_feed1", "unit_grad0_feed1", "unit_grad0_feed1", "unit_grad0", "deep_grad", ".qg2",
    "unit_grad1", "unit_grad1", "unit_grad1_feed1", "unit_grad1_feed1", "unit_grad1_feed1", "unit_grad1", "qkv_share",
    ".upg1", "up_share", "up_grad_feed0", "qkv_share", "up_share", "deep_grad", "unit_grad_pair",
    "unit_grad_side_feed0", "unit_grad_pair", "qkv_grad_feed0", ".upg3", "vector", "up_share", "up_grad_feed0",
    "up_share", ".upg0", ".branch_out", "up_share", "up_grad_feed0", "up_share", "up_grad", "up_grad", "deep_grad",
    "up_grad", "up_grad_feed1", "up_grad_feed1", "up_grad_feed1", "up_grad", ".qg1", "unit_grad0", "unit_grad0",
    "unit_grad0", "qkv_share", "up_share", ".qg3", "vector", "qkv_share", "qkv_share", "unit_grad_pair",
    "unit_grad_side_feed0", "unit_grad_side", "unit_grad_side", "unit_grad_side", "unit_grad_pair", "qkv_grad_feed0",
    ".qg0", "qkv_share", "qkv_share", "qkv_grad_feed0", "qkv_grad", "qkv_grad", "qkv_grad", "qkv_grad_feed1",
    "qkv_grad_feed1", "qkv_grad_feed1", "qkv_grad", "unit_grad1", "unit_grad1", "unit_grad1", "qkv_share", "vector",
    "up_grad", "up_grad", "up_grad", "unit_grad_pair", "unit_grad0", "unit_grad0", "unit_grad_side", "unit_grad1",
    "unit_grad1", "vector", "qkv_grad", "qkv_grad", "qkv_grad", "up_grad", "up_grad", "qkv_grad", "qkv_grad",
)


def layer_kernel(
    lens,
    x_in,
    cot_in,
    w_qkv,
    w_out,
    w_up,
    w_down,
    b_qkv,
    b_up,
    gains,
    biases,
    branch_sum,
    unit_sum,
    qkv_sum,
    up_sum,
    deep_sum,
    vector_sum,
    low_sum,
    unit,
    cot,
    wide,
    deep,
    up,
    q,
    k,
    v,
    acts,
    probs,
    branch,
    grads,
    mixed_grad,
    sums,
    low_sums,
    vectors,
    vector_slots,
    up_core,
    deep_core,
    qkv_slots,
    up_slots,
    deep_slots,
    branch_slots,
    unit_slots,
    branch_side_slots,
    unit_side_slots,
    branch_pairs,
    unit_pairs,
    qkv_last,
    up_last,
    deep_last,
    branch_last,
    unit_last,
    row_total,
    qkv_total,
    up_total,
    deep_total,
    send_sems,
    recv_sems,
    core_send,
    core_recv,
    load_sems,
    store_sems,
):
    spot = place()
    zh, y, core, zl, x = spot
    near = neighbours(spot)
    near["x2"] = device(zh, y, core, zl, around(x, 2))
    near["y2"] = device(zh, around(y, 2), core, zl, x)
    barrier = pltpu.get_barrier_semaphore()
    for target in near.values():
        pl.semaphore_signal(barrier, inc=1, device_id=target, device_id_type=MESH)

    mine = pl.ds(pl.multiple_of((zl * 4 + x) * OWN, OWN), OWN)
    own = pl.ds(pl.multiple_of(((zh * 4 + y) * 2 + core) * OWN, OWN), OWN)
    loads = []
    for src, dst in (
        *((w_qkv.at[head], qkv_total.at[:, pl.ds(head * HEAD, HEAD)]) for head in range(3)),
        (x_in, unit.at[mine, :]),
        (w_up, up_total),
        (w_out, deep_total.at[pl.ds(0, HEAD), :]),
        (w_down, deep_total.at[pl.ds(HEAD, UNITS), :]),
        (cot_in, cot.at[mine, :]),
    ):
        loads.append(pltpu.make_async_copy(src, dst, load_sems.at[len(loads)]))
        loads[-1].start()

    links = Links(send_sems, recv_sems)
    stores = []
    done = set()

    def store(src, dst):
        copy = pltpu.make_async_copy(src, dst, store_sems.at[len(stores)])
        copy.start()
        stores.append(copy)
        return copy

    def deep_part(z, ring, half):
        columns = pl.ds(pl.multiple_of(((z * 4 + ring) * 2 + core) * OWN, OWN), OWN)
        if half is None:
            return deep.at[:, columns]
        return deep.at[pl.ds(half * (DEEP // 2), DEEP // 2), columns]

    def deep_place(chip, who):
        return deep.at[:, pl.ds(pl.multiple_of((chip * 2 + who) * OWN, OWN), OWN)]

    def up_place(chip, who):
        return rows_of(up, (chip * 2 + who) * OWN, OWN)

    def qkv_place(chip, who):
        return rows_of(wide, (chip * 2 + who) * OWN, OWN).at[:, pl.ds(0, QKV)]

    shares = (
        (deep_place, lambda slot: deep_core.at[slot]),
        (up_place, lambda slot: up_core.at[slot]),
        (qkv_place, lambda slot: rows_of(probs, slot * OWN, OWN).at[:, pl.ds(0, QKV)]),
    )

    def chip_at(ring, turn_of):
        return (zh + (1 - 2 * zh) * turn_of) * 4 + around(y, ring)

    def core_copy(which, ring, turn_of):
        number = which * 8 + ring * 2 + turn_of
        place_of, slots = shares[which]
        return pltpu.make_async_remote_copy(
            src_ref=place_of(chip_at(ring, turn_of), 1 - core),
            dst_ref=slots(ring * 2 + turn_of),
            send_sem=core_send.at[number],
            recv_sem=core_recv.at[number],
            device_id=near["core"],
            device_id_type=MESH,
        )

    def share(which, name):
        place_of, slots = shares[which]

        def add(ring, turn_of):
            core_copy(which, ring, turn_of).wait_recv()
            part = place_of(chip_at(ring, turn_of), core)
            part[...] = (
                part[...].astype(F32) + slots(ring * 2 + turn_of)[...].astype(F32)
            ).astype(BF16)
            return ring

        for step in (2, 1, 3, 0):
            yield [(name + "_raw", step)]
            yield []
            lax.fori_loop(0, 2, lambda turn_of, _: add(step, turn_of), 0)
            done.add((name, step))

    def add_vectors():
        yield [("sums", "ready")]
        slot = 0
        for stage, (names, count) in enumerate(
            (
                (("core",), 96),
                (("y+", "y-", "y2"), 96),
                (("zh",), 96),
                (("zl",), 80),
                (("x+", "x-", "x2"), 80),
            )
        ):
            span = pl.ds(0, count)
            copies = [
                links.send(
                    vectors.at[stage, span], vector_slots.at[slot + index, span], near[name]
                )
                for index, name in enumerate(names)
            ]
            yield copies
            for copy in copies:
                copy.wait_recv()
            parts = [vectors[stage, :count, :]]
            parts += [vector_slots[slot + index, :count, :] for index in range(len(copies))]
            if len(parts) == 2:
                total = parts[0] + parts[1]
            else:
                total = (parts[0] + parts[3]) + (parts[1] + parts[2])
            vectors[stage + 1, :count, :] = total
            slot += len(names)
        for row in range(5):
            for column in range(16):
                sums[row : row + 1, column * 128 : (column + 1) * 128] = vectors[
                    5, row * 16 + column : row * 16 + column + 1, :
                ]
        for column in range(14):
            low_sums[0:1, column * 128 : (column + 1) * 128] = vectors[
                3, 80 + column : 81 + column, :
            ]
        store(sums, vector_sum)
        store(low_sums, low_sum)

    def keep(steps, src, dst):
        yield from steps
        store(src, dst)

    tensor_ends = (zl, x, near["zl"], near["x+"], near["x-"])
    side_ends = (zl, x, None, near["x+"], near["x-"], near["zl"])
    data_ends = (zh, y, near["zh"], near["y+"], near["y-"])
    units_side = Gather(links, row_part(unit, MAIN_UNIT, D - MAIN_UNIT), *side_ends)
    cots_side = Gather(links, row_part(cot, MAIN_COT, D - MAIN_COT), *side_ends)
    wides = Gather(links, row_part(wide, 0, QKV, core), *data_ends, near["core"])
    wups = Gather(links, row_part(wide, QKV, UNITS, core), *data_ends, near["core"])
    deeps = Gather(links, deep_part, *data_ends, near["core"])

    side_branch = row_part(branch, MAIN_BRANCH, D - MAIN_BRANCH)
    side_grad = row_part(cot, MAIN_GRAD, D - MAIN_GRAD)
    branch_side = Scatter(links, side_branch, branch_side_slots, None, *tensor_ends)
    branch_pair = PairSum(links, side_branch, branch_pairs, zl, x, near["zl"])
    unit_side = Scatter(links, side_grad, unit_side_slots, None, *tensor_ends)
    unit_pair = PairSum(links, side_grad, unit_pairs, zl, x, near["zl"])
    qkv_grid = Scatter(links, row_part(wide, 0, QKV, core), qkv_slots, qkv_last, *data_ends)
    up_grid = Scatter(links, row_part(up, 0, UNITS, core), up_slots, up_last, *data_ends)
    deep_grid = Scatter(links, deep_part, deep_slots, deep_last, *data_ends)
    go, free, turned = ("own", "ready"), ("rows", "free"), ("turn", "free")

    def late(name, which=0):
        return (name, "joined", 0, which) if name in LATE else go

    transfers = {
        "unit_side": units_side.own(("unit", "ready")),
        "cot_side": cots_side.own(("rest", "ready")),
        "wide": wides.own(("wide", "ready")),
        "wide_far": wides.far(("wide", "sent")),
        "wup": wups.own(("rest", "ready")),
        "wup_far": wups.far(("wup", "sent")),
        "deep": deeps.own(("rest", "ready")),
        "deep_far": deeps.far(("deep", "sent")),
        "branch_pair": branch_pair.run("branch", "branch_side", done),
        "branch_side_feed0": branch_side.feed("branch_side", 0, go, done),
        "branch_side": branch_side.run(
            "branch_side", row_total.at[:, pl.ds(MAIN_BRANCH, D - MAIN_BRANCH)], turned, done
        ),
        "unit_grad_pair": unit_pair.run("unit_grad", "unit_grad_side", done),
        "unit_grad_side_feed0": unit_side.feed("unit_grad_side", 0, go, done),
        "unit_grad_side": unit_side.run(
            "unit_grad_side", row_total.at[:, pl.ds(MAIN_GRAD, D - MAIN_GRAD)], free, done
        ),
        "deep_share": share(0, "deep_grad"),
        "deep_grad_feed0": deep_grid.feed("deep_grad", 0, go, done),
        "deep_grad_feed1": deep_grid.feed("deep_grad", 1, late("deep_grad"), done),
        "deep_grad": keep(deep_grid.run("deep_grad", deep_total, go, done), deep_total, deep_sum),
        "up_share": share(1, "up_grad"),
        "up_grad_feed0": up_grid.feed("up_grad", 0, go, done),
        "up_grad_feed1": up_grid.feed("up_grad", 1, late("up_grad"), done),
        "up_grad": keep(up_grid.run("up_grad", up_total, go, done), up_total, up_sum),
        "qkv_share": share(2, "qkv_grad"),
        "qkv_grad_feed0": qkv_grid.feed("qkv_grad", 0, go, done),
        "qkv_grad_feed1": qkv_grid.feed("qkv_grad", 1, late("qkv_grad"), done),
        "qkv_grad": keep(qkv_grid.run("qkv_grad", qkv_total, go, done), qkv_total, qkv_sum),
        "vector": add_vectors(),
    }

    cot_gathers = [cots_side]
    for name, ref, main, chunks, gate in (
        ("unit", unit, MAIN_UNIT, CHUNKS[0], "unit"),
        ("cot", cot, MAIN_COT, CHUNKS[1], "rest"),
    ):
        for which in range(chunks):
            size = main // chunks
            gather = Gather(links, row_part(ref, which * size, size), *tensor_ends, None)
            transfers[f"{name}{which}"] = gather.own((gate, "ready"))
            transfers[f"{name}{which}_far"] = gather.far((f"{name}{which}", "sent"))
            if name == "cot":
                cot_gathers.append(gather)
    for name, ref, slots, last, main, chunks, gate in (
        ("branch", branch, branch_slots, branch_last, MAIN_BRANCH, CHUNKS[2], turned),
        ("unit_grad", cot, unit_slots, unit_last, MAIN_GRAD, CHUNKS[3], free),
    ):
        for which in range(chunks):
            size = main // chunks
            span = pl.ds(which * size, size)
            scatter = Scatter(
                links,
                row_part(ref, which * size, size),
                slots.at[:, :, :, :, span],
                last.at[:, span],
                *tensor_ends,
            )
            transfers[f"{name}{which}_feed0"] = scatter.feed(name, 0, go, done, which)
            transfers[f"{name}{which}_feed1"] = scatter.feed(name, 1, late(name, which), done, which)
            out = row_total.at[:, span]
            transfers[f"{name}{which}"] = scatter.run(name, out, gate, done, which)

    ends = [lens[0, 0]]
    for seq in range(1, 3):
        ends.append(ends[-1] + lens[0, seq])

    def begin_of(index):
        begin = jnp.zeros_like(index)
        for end in ends:
            begin = jnp.where(index >= end, end, begin)
        return begin

    def own_first():
        for load in loads[:3]:
            load.wait()
        wide[own, :QKV] = qkv_total[...].astype(BF16)
        pl.semaphore_wait(barrier, len(near))
        done.update([("wide", "ready"), go])

    def own_rows():
        loads[3].wait()
        rows = unit[mine, :].astype(F32)
        centred = rows - jnp.mean(rows, axis=-1, keepdims=True)
        variance = jnp.mean(centred * centred, axis=-1, keepdims=True)
        unit[mine, :] = (centred * lax.rsqrt(variance + NORM_EPS)).astype(BF16)
        done.add(("unit", "ready"))

    def own_weights():
        for load in loads[4:]:
            load.wait()
        wide[own, QKV:] = up_total[...].astype(BF16)
        deep[:, own] = deep_total[...].astype(BF16)
        done.add(("rest", "ready"))

    def tables():
        sums[...] = jnp.zeros_like(sums)
        low_sums[...] = jnp.zeros_like(low_sums)
        sums[4:5, :] = jnp.sum(cot[mine, :].astype(F32), axis=0, keepdims=True)
        row = lax.broadcasted_iota(jnp.int32, (OWN, 128), 0)
        lane = lax.broadcasted_iota(jnp.int32, (OWN, 128), 1)
        rate = jnp.exp(lax.rem(lane, 32).astype(F32) * (-2.0 * math.log(10000.0) / ROT))
        for block in range(TOK // OWN):
            index = row + block * OWN
            angle = (index - begin_of(index)).astype(F32) * rate
            columns = slice(block * 128, (block + 1) * 128)
            row_total[:, columns] = jnp.where(lane < ROT, jnp.cos(angle), 1.0)
            columns = slice(TOK + block * 128, TOK + (block + 1) * 128)
            row_total[:, columns] = jnp.where(lane < ROT, jnp.sin(angle), 0.0)

    def turn(which, part):
        blocks = range(part.start // OWN, part.stop // OWN)
        starts = [which * TOK + block * 128 for block in blocks]
        return jnp.concatenate([row_total[:, start : start + 128] for start in starts], axis=0)

    def norm_tile(tile, which):
        part = slice(tile * TILE, (tile + 1) * TILE)
        span = slice(which * TILE, (which + 1) * TILE)
        rows = unit[part, :].astype(F32)
        branch[span, :] = (
            rows * gains[which : which + 1, :] + biases[which : which + 1, :]
        ).astype(BF16)

    def heads(tile):
        part = slice(tile * TILE, (tile + 1) * TILE)
        norm_tile(tile, 0)
        for which, target in enumerate((q, k, v)):
            columns = slice(which * HEAD, (which + 1) * HEAD)
            head = jnp.dot(branch[:TILE, :], wide[:, columns], preferred_element_type=F32)
            head = head + b_qkv[which : which + 1, :]
            if which < 2:
                head = spin(head, turn(0, part), turn(1, part), False)
            target[part, :] = head.astype(BF16)

    def hidden(tile, half):
        part = slice(tile * TILE, (tile + 1) * TILE)
        if half == 0:
            norm_tile(tile, 1)

        def one(piece, _):
            shift = pl.multiple_of(piece * 256, 256)
            pre = jnp.dot(
                branch[TILE:, :], wide[:, pl.ds(QKV + shift, 256)], preferred_element_type=F32
            )
            pre = pre + b_up[0:1, pl.ds(shift, 256)]
            value, rise = gelu_parts(pre)
            acts[part, pl.ds(HEAD + shift, 256)] = value.astype(BF16)
            grads[part, pl.ds(QKV + shift, 256)] = rise.astype(BF16)
            return 0

        lax.fori_loop(2 * half, 2 * half + 2, one, 0, unroll=2)

    def attend(block):
        part = slice(block * QROWS, (block + 1) * QROWS)
        keys = (block + 1) * QROWS
        whole = by_rows(q[part, :], k[:keys, :]) * (HEAD**-0.5)
        for start in range(0, QROWS, OWN):
            scores = whole[start : start + OWN]
            start = block * QROWS + start
            key = lax.broadcasted_iota(jnp.int32, (OWN, keys), 1)
            row = lax.broadcasted_iota(jnp.int32, (OWN, 1), 0) + start
            scores = jnp.where((key <= row) & (key >= begin_of(row)), scores, -jnp.inf)
            expo = jnp.exp(scores - jnp.max(scores, axis=-1, keepdims=True))
            mass = expo / jnp.sum(expo, axis=-1, keepdims=True)
            probs[start : start + OWN, :keys] = mass.astype(BF16)
        acts[part, :HEAD] = jnp.dot(
            probs[part, :keys], v[:keys, :], preferred_element_type=F32
        ).astype(BF16)

    def pieces_of(ring):
        starts = (around(x, ring) * OWN, (4 + around(x, ring)) * OWN)
        return [pl.ds(pl.multiple_of(start, OWN), OWN) for start in starts]

    def mix(step):
        pieces = pieces_of(step)

        def one(piece, _):
            columns = pl.ds(pl.multiple_of(piece * 512, 512), 512)
            rows = jnp.concatenate([acts[each, :] for each in pieces], axis=0)
            both = jnp.dot(rows, deep[:, columns], preferred_element_type=F32).astype(BF16)
            branch[pieces[0], columns] = both[:OWN]
            branch[pieces[1], columns] = both[OWN:]
            return 0

        lax.fori_loop(0, D // 512, one, 0, unroll=4)
        done.add(("branch", step))

    def back(tile, half):
        part = slice(tile * TILE, (tile + 1) * TILE)
        if half == 0:
            mixed_grad[part, :] = by_rows(cot[part, :], deep[:HEAD, :]).astype(BF16)

        def one(piece, _):
            shift = pl.multiple_of(piece * 256, 256)
            columns = pl.ds(QKV + shift, 256)
            grad = by_rows(cot[part, :], deep[pl.ds(HEAD + shift, 256), :])
            grad = grad * grads[part, columns].astype(F32)
            low_sums[0:1, columns] += jnp.sum(grad, axis=0, keepdims=True)
            grads[part, columns] = grad.astype(BF16)
            return 0

        lax.fori_loop(2 * half, 2 * half + 2, one, 0, unroll=2)

    def deep_grads(step):
        if step == 2:
            links.settle(deeps.sent)

        def one(turn_of, _):
            columns = pl.ds(pl.multiple_of(chip_at(step, turn_of) * 256, 256), 256)
            for half in range(2):
                part = slice(half * (DEEP // 2), (half + 1) * (DEEP // 2))
                deep[part, columns] = over_rows(acts[:, part], cot[:, columns]).astype(BF16)
            core_copy(0, step, turn_of).start()
            return 0

        lax.fori_loop(0, 2, one, 0)
        done.add(("deep_grad_raw", step))

    def norm_columns(span, which):
        acts[:, :256] = (
            unit[:, span].astype(F32) * gains[which : which + 1, span]
            + biases[which : which + 1, span]
        ).astype(BF16)

    def up_grads(step):
        def one(turn_of, _):
            span = pl.ds(pl.multiple_of(chip_at(step, turn_of) * 256, 256), 256)
            norm_columns(span, 1)
            up[span, :] = over_rows(acts[:, :256], grads[:, QKV:]).astype(BF16)
            core_copy(1, step, turn_of).start()
            return 0

        lax.fori_loop(0, 2, one, 0)
        done.add(("up_grad_raw", step))

    def qkv_grads(step):
        if step == 2:
            links.settle(wides.sent)

        def one(turn_of, _):
            span = pl.ds(pl.multiple_of(chip_at(step, turn_of) * 256, 256), 256)
            norm_columns(span, 0)
            wide[span, :QKV] = over_rows(acts[:, :256], grads[:, :QKV]).astype(BF16)
            core_copy(2, step, turn_of).start()
            return 0

        lax.fori_loop(0, 2, one, 0)
        done.add(("qkv_grad_raw", step))

    def put_grad(grad, part, which):
        columns = slice(which * HEAD, (which + 1) * HEAD)
        if which < 2:
            grad = spin(grad * (HEAD**-0.5), turn(0, part), turn(1, part), True)
        low_sums[0:1, columns] += jnp.sum(grad, axis=0, keepdims=True)
        grads[part, columns] = grad.astype(BF16)

    def value_grads():
        for block in range(TOK // QROWS):
            part = slice(block * QROWS, (block + 1) * QROWS)
            below = slice(block * QROWS, TOK)
            put_grad(over_rows(probs[below, part], mixed_grad[below, :]), part, 2)

    def query_grads(block):
        part = slice(block * QROWS, (block + 1) * QROWS)
        keys = (block + 1) * QROWS
        whole = by_rows(mixed_grad[part, :], v[:keys, :])
        for start in range(0, QROWS, OWN):
            prob_grad = whole[start : start + OWN]
            rows = slice(block * QROWS + start, block * QROWS + start + OWN)
            mass = probs[rows, :keys].astype(F32)
            delta = jnp.sum(mass * prob_grad, axis=-1, keepdims=True)
            probs[rows, :keys] = (mass * (prob_grad - delta)).astype(BF16)
        put_grad(jnp.dot(probs[part, :keys], k[:keys, :], preferred_element_type=F32), part, 0)

    def key_grads():
        for block in range(TOK // QROWS):
            part = slice(block * QROWS, (block + 1) * QROWS)
            below = slice(block * QROWS, TOK)
            put_grad(over_rows(probs[below, part], q[below, :]), part, 1)
        done.add(turned)

    def unit_grads(step):
        if step == 2:
            for gather in cot_gathers:
                links.settle(gather.sent)
        pieces = pieces_of(step)
        for half in range(2):
            acts[half * OWN : (half + 1) * OWN, :QKV] = grads[pieces[half], :QKV]
            acts[(2 + half) * OWN : (3 + half) * OWN, :UNITS] = grads[pieces[half], QKV:]

        def one(piece, _):
            columns = pl.ds(pl.multiple_of(piece * 512, 512), 512)
            first = by_rows(acts[: 2 * OWN, :QKV], wide[columns, :QKV])
            second = by_rows(acts[2 * OWN : 4 * OWN, :UNITS], wide[columns, QKV:])
            rows = jnp.concatenate([unit[each, columns] for each in pieces], axis=0).astype(F32)
            sums[0:1, columns] += jnp.sum(first * rows, axis=0, keepdims=True)
            sums[1:2, columns] += jnp.sum(second * rows, axis=0, keepdims=True)
            sums[2:3, columns] += jnp.sum(first, axis=0, keepdims=True)
            sums[3:4, columns] += jnp.sum(second, axis=0, keepdims=True)
            both = (first * gains[0:1, columns] + second * gains[1:2, columns]).astype(BF16)
            cot[pieces[0], columns] = both[:OWN]
            cot[pieces[1], columns] = both[OWN:]
            return 0

        lax.fori_loop(0, D // 512, one, 0, unroll=4)
        done.add(("unit_grad", step))

    def pack():
        for row in range(5):
            for column in range(16):
                vectors[0, row * 16 + column : row * 16 + column + 1, :] = sums[
                    row : row + 1, column * 128 : (column + 1) * 128
                ]
        for column in range(14):
            vectors[0, 80 + column : 81 + column, :] = low_sums[
                0:1, column * 128 : (column + 1) * 128
            ]
        vectors[0, 94:96, :] = jnp.zeros((2, 128), F32)
        done.add(("sums", "ready"))

    branch_stores = []

    def branch_out():
        branch_stores.append(pltpu.make_async_copy(row_total, branch_sum, store_sems.at[7]))
        branch_stores[0].start()
        branch_stores[0].wait()
        done.add(free)

    compute = {
        ".init": own_first,
        ".rows": own_rows,
        ".weights": own_weights,
        ".tables": tables,
        ".dv": value_grads,
        ".dk": key_grads,
        ".pack": pack,
        ".branch_out": branch_out,
    }
    for tile in range(TOK // TILE):
        compute[f".qkv{tile}"] = functools.partial(heads, tile)
        for half, letter in enumerate("ab"):
            compute[f".hid{tile}{letter}"] = functools.partial(hidden, tile, half)
            compute[f".back{tile}{letter}"] = functools.partial(back, tile, half)
    for step in range(4):
        compute[f".att{step}"] = functools.partial(attend, step)
        compute[f".dp{step}"] = functools.partial(query_grads, step)
        compute[f".mix{step}"] = functools.partial(mix, step)
        compute[f".deepg{step}"] = functools.partial(deep_grads, step)
        compute[f".upg{step}"] = functools.partial(up_grads, step)
        compute[f".qg{step}"] = functools.partial(qkv_grads, step)
        compute[f".g{step}"] = functools.partial(unit_grads, step)

    waiting = {name: next(steps) for name, steps in transfers.items()}
    for name in ORDER:
        if name in compute:
            compute.pop(name)()
            continue
        assert all(each in done for each in waiting[name] if isinstance(each, tuple)), name
        waiting[name] = next(transfers[name], None)
        done.add((name, "sent"))
        if waiting[name] is None:
            del waiting[name]
    assert not waiting and not compute
    store(row_total, unit_sum)

    for which in range(3):
        for step in range(4):
            for turn_of in range(2):
                core_copy(which, step, turn_of).wait_send()
    for copy in stores:
        copy.wait()
    links.settle(links.open)


SUMS = (
    ((OWN, D), F32),
    ((OWN, D), F32),
    ((OWN, QKV), F32),
    ((OWN, UNITS), F32),
    ((DEEP, OWN), F32),
    ((8, D), F32),
    ((8, WIDE), F32),
)
HALF = OWN // 2
SCRATCH = (
    ((TOK, D), BF16),
    ((TOK, D), BF16),
    ((D, WIDE), BF16),
    ((DEEP, D), BF16),
    ((D, UNITS), BF16),
    ((TOK, HEAD), BF16),
    ((TOK, HEAD), BF16),
    ((TOK, HEAD), BF16),
    ((TOK, DEEP), BF16),
    ((TOK, TOK), BF16),
    ((TOK, D), BF16),
    ((TOK, WIDE), BF16),
    ((TOK, HEAD), BF16),
    ((8, D), F32),
    ((8, WIDE), F32),
    ((6, 96, 128), F32),
    ((9, 96, 128), F32),
    ((8, OWN, UNITS), BF16),
    ((8, DEEP, OWN), BF16),
    ((2, 3, 2, HALF, QKV), BF16),
    ((2, 3, 2, HALF, UNITS), BF16),
    ((2, 3, 2, DEEP // 2, OWN), BF16),
    ((2, 3, 2, HALF, MAIN_BRANCH), BF16),
    ((2, 3, 2, HALF, MAIN_GRAD), BF16),
    ((2, 3, 1, HALF, D - MAIN_BRANCH), BF16),
    ((2, 3, 1, HALF, D - MAIN_GRAD), BF16),
    ((4, OWN, D - MAIN_BRANCH), BF16),
    ((4, OWN, D - MAIN_GRAD), BF16),
    ((OWN, QKV), BF16),
    ((OWN, UNITS), BF16),
    ((DEEP, OWN), BF16),
    ((OWN, MAIN_BRANCH), BF16),
    ((OWN, MAIN_GRAD), BF16),
    ((OWN, D), F32),
    ((OWN, QKV), F32),
    ((OWN, UNITS), F32),
    ((DEEP, OWN), F32),
)


def run_layer(lens, layer_in, cotangent, w_qkv, w_out, w_up, w_down, *vectors):
    anywhere = pl.BlockSpec(memory_space=pl.ANY)
    vmem = pl.BlockSpec(memory_space=pltpu.VMEM)
    return pl.pallas_call(
        layer_kernel,
        out_shape=[jax.ShapeDtypeStruct(*each) for each in SUMS],
        in_specs=[pl.BlockSpec(memory_space=pltpu.SMEM)] + [anywhere] * 6 + [vmem] * len(vectors),
        out_specs=[anywhere] * len(SUMS),
        scratch_shapes=[pltpu.VMEM(*each) for each in SCRATCH]
        + [
            pltpu.SemaphoreType.DMA((260,)),
            pltpu.SemaphoreType.DMA((260,)),
            pltpu.SemaphoreType.DMA((24,)),
            pltpu.SemaphoreType.DMA((24,)),
            pltpu.SemaphoreType.DMA((8,)),
            pltpu.SemaphoreType.DMA((8,)),
        ],
        compiler_params=pltpu.CompilerParams(
            collective_id=0, has_side_effects=True, vmem_limit_bytes=63 * 2**20
        ),
        cost_estimate=pl.CostEstimate(flops=42 * 10**9, bytes_accessed=10**7, transcendentals=0),
        name="layer",
    )(lens, layer_in, cotangent, w_qkv, w_out, w_up, w_down, *vectors)


def adam_step(weight, gradient, moment_one, moment_two, step_rate, decay_rate):
    moment_one = BETA_ONE * moment_one + (1.0 - BETA_ONE) * gradient
    moment_two = BETA_TWO * moment_two + (1.0 - BETA_TWO) * gradient * gradient
    spread = jnp.sqrt(moment_two * (1.0 / (1.0 - BETA_TWO**STEP))) + ADAM_EPS
    ratio = moment_one * (1.0 / (1.0 - BETA_ONE**STEP)) / spread
    return (moment_one, moment_two, weight - step_rate * (ratio + decay_rate * weight))


BIG = 14
AHEAD = 4


def update_kernel(*refs):
    sums, refs = refs[:7], refs[7:]
    big, refs = refs[:BIG], refs[BIG:]
    small, refs = refs[:12], refs[12:]
    big_out, refs = refs[:BIG], refs[BIG:]
    small_out, refs = refs[:12], refs[12:]
    sum_bufs, refs = refs[:7], refs[7:]
    in_bufs, refs = refs[:BIG], refs[BIG:]
    small_bufs, refs = refs[:12], refs[12:]
    row_bufs, bias_rows, load_sems, store_sems = refs[:2], refs[2], refs[3], refs[4]
    branch, unit_grad, qkv, up, deep, vectors, low_vectors = sum_bufs
    loads, stores = [], []

    def fetch(src, dst):
        copy = pltpu.make_async_copy(src, dst, load_sems.at[len(loads)])
        loads.append(copy)
        copy.start()
        return copy

    def put(src, dst):
        copy = pltpu.make_async_copy(src, dst, store_sems.at[len(stores)])
        stores.append(copy)
        copy.start()

    def matrix(which, at, sum_index, sum_at, gradient_of):
        first = 2 + 3 * which

        def start():
            copies = [fetch(sums[sum_index].at[sum_at], sum_bufs[sum_index].at[sum_at])]
            for index in range(first, first + 3):
                copies.append(fetch(big[index].at[at], in_bufs[index].at[at]))
            return copies

        def finish():
            weight, one, two = (each.at[at] for each in in_bufs[first : first + 3])
            for part, gradient in gradient_of(sum_bufs[sum_index].at[sum_at]):
                results = adam_step(
                    weight[part],
                    gradient,
                    one[part],
                    two[part],
                    STEP_RATES[which],
                    DECAY_RATES[which],
                )
                one[part], two[part], weight[part] = results
            for index, src in enumerate((one, two, weight)):
                put(src, big_out[first + index].at[at])

        return start, finish

    def plain(ref):
        return [(slice(None), ref[...])]

    def by_head(ref):
        return [(head, ref[:, head * HEAD : (head + 1) * HEAD]) for head in range(3)]

    def rows_part(at):
        def start():
            return [
                fetch(src.at[at], dst.at[at])
                for src, dst in (
                    (big[0], in_bufs[0]),
                    (big[1], in_bufs[1]),
                    (sums[0], branch),
                    (sums[1], unit_grad),
                )
            ]

        def finish():
            biases = bias_rows
            resid = in_bufs[0][at, :].astype(F32)
            total = resid + branch[at, :] + biases[2:3, :] + biases[3:4, :]
            row_bufs[0][at, :] = total.astype(BF16)
            put(row_bufs[0].at[at], big_out[0].at[at])
            centred = resid - jnp.mean(resid, axis=-1, keepdims=True)
            inverse = lax.rsqrt(jnp.mean(centred * centred, axis=-1, keepdims=True) + NORM_EPS)
            unit = centred * inverse
            grad = unit_grad[at, :]
            mean = jnp.mean(grad, axis=-1, keepdims=True)
            along = jnp.mean(grad * unit, axis=-1, keepdims=True)
            back = in_bufs[1][at, :].astype(F32) + inverse * (grad - mean - unit * along)
            row_bufs[1][at, :] = back
            put(row_bufs[1].at[at], big_out[1].at[at])

        return start, finish

    def vector_part():
        def start():
            copies = [fetch(sums[index], sum_bufs[index]) for index in (5, 6)]
            return copies + [fetch(*each) for each in zip(small, small_bufs)]

        def finish():
            slots = (
                (0, 4, [low_vectors[0:1, head * HEAD : (head + 1) * HEAD] for head in range(3)]),
                (3, 5, [low_vectors[0:1, QKV:]]),
                (6, 6, [vectors[0:1, :], vectors[1:2, :]]),
                (9, 7, [vectors[2:3, :], vectors[3:4, :], vectors[4:5, :], vectors[4:5, :]]),
            )
            bias_rows[...] = small_bufs[9][...]
            for first, which, gradients in slots:
                weight, one, two = small_bufs[first : first + 3]
                for row, gradient in enumerate(gradients):
                    at = slice(row, row + 1)
                    results = adam_step(
                        weight[at, :],
                        gradient,
                        one[at, :],
                        two[at, :],
                        STEP_RATES[which],
                        DECAY_RATES[which],
                    )
                    one[at, :], two[at, :], weight[at, :] = results
                for index, src in enumerate((one, two, weight)):
                    put(src, small_out[first + index])

        return start, finish

    halves = [pl.ds(0, OWN // 2), pl.ds(OWN // 2, OWN // 2)]
    parts = [matrix(1, slice(None), 4, pl.ds(0, HEAD), plain)]
    for start in (0, UNITS // 2):
        at = pl.ds(start, UNITS // 2)
        parts.append(matrix(3, at, 4, pl.ds(HEAD + start, UNITS // 2), plain))
    parts += [matrix(2, at, 3, at, plain) for at in halves]
    parts += [matrix(0, (slice(None), at), 2, at, by_head) for at in halves]
    parts.insert(0, vector_part())
    parts += [rows_part(at) for at in halves]
    copies = [start() for start, _ in parts[:AHEAD]]
    for index, (_, finish) in enumerate(parts):
        if index + AHEAD < len(parts):
            copies.append(parts[index + AHEAD][0]())
        for copy in copies[index]:
            copy.wait()
        finish()
    for copy in stores:
        copy.wait()


def run_update(sums, big, small):
    anywhere = pl.BlockSpec(memory_space=pl.ANY)
    matrices = [jax.ShapeDtypeStruct(each.shape, F32) for each in big[2:]]
    rows = [jax.ShapeDtypeStruct((OWN, D), BF16), jax.ShapeDtypeStruct((OWN, D), F32)]
    return pl.pallas_call(
        update_kernel,
        out_shape=rows + matrices + [jax.ShapeDtypeStruct(each.shape, F32) for each in small],
        in_specs=[anywhere] * (len(sums) + BIG + 12),
        out_specs=[anywhere] * (BIG + 12),
        scratch_shapes=[pltpu.VMEM(each.shape, F32) for each in sums]
        + [pltpu.VMEM(each.shape, each.dtype) for each in big]
        + [pltpu.VMEM(each.shape, F32) for each in small]
        + [pltpu.VMEM((OWN, D), BF16), pltpu.VMEM((OWN, D), F32), pltpu.VMEM((4, D), F32)]
        + [pltpu.SemaphoreType.DMA((64,)), pltpu.SemaphoreType.DMA((48,))],
        compiler_params=pltpu.CompilerParams(vmem_limit_bytes=63 * 2**20),
        cost_estimate=pl.CostEstimate(flops=10**7, bytes_accessed=16 * 10**6, transcendentals=0),
        name="update",
    )(*sums, *big, *small)


def local(layer_in, cotangent, seq_lengths, *state):
    params, moments = list(state[:8]), list(state[8:])
    params[0] = params[0].transpose(1, 0, 2)
    moments[0], moments[1] = (each.transpose(1, 0, 2) for each in moments[:2])
    params[5] = params[5].reshape(1, UNITS)
    moments[10], moments[11] = (each.reshape(1, UNITS) for each in moments[10:12])
    sums = run_layer(seq_lengths, layer_in, cotangent, *params)
    groups = [(params[which], moments[2 * which], moments[2 * which + 1]) for which in range(8)]
    big = [layer_in, cotangent] + [each for group in groups[:4] for each in group]
    small = [each for group in groups[4:] for each in group]
    results = list(run_update(sums, big, small))
    for index in range(2, 5):
        results[index] = results[index].transpose(1, 0, 2)
    for index in range(17, 20):
        results[index] = results[index].reshape(UNITS)
    return tuple(results)


def solution(mesh):
    rows = P(("dp", "tensor"), None)
    out, up = P("tensor", "dp"), P("dp", "tensor")
    params = (P("dp", None, "tensor"), out, up, out, P(None, "tensor"), P("tensor"), P(), P())
    moments = [spec for spec in params for _ in range(2)]
    return jax.shard_map(
        local,
        mesh=mesh,
        in_specs=(rows, rows, P("dp", None), *params, *moments),
        out_specs=(rows, rows, *[spec for spec in params for _ in range(3)]),
        check_vma=False,
    )
```

```python
import functools
import math

import jax
import jax.numpy as jnp
from jax import lax
from jax.experimental import pallas as pl
from jax.experimental.pallas import tpu as pltpu
from jax.sharding import PartitionSpec as P

F32 = jnp.float32
BF16 = jnp.bfloat16
MESH = pl.DeviceIdType.MESH

D = 2048
HEAD = 256
QKV = 3 * HEAD
UNITS = 1024
WIDE = QKV + UNITS
DEEP = HEAD + UNITS
TOK = 1024
OWN = 128
TILE = 512
MAIN_UNIT, MAIN_COT, MAIN_BRANCH, MAIN_GRAD = 1536, 1280, 1536, 1536
CHUNKS = (2, 2, 2, 2)
QROWS = 256
ROT = 64
STEP = 10

NORM_EPS = 1e-05
BETA_ONE = 0.9
BETA_TWO = 0.95
ADAM_EPS = 1e-08
STEP_RATES = (0.04, 0.2, 0.04, 0.02, 0.3, 0.3, 0.5, 0.3)
DECAY_RATES = (0.01, 0.01, 0.01, 0.01, 0.0, 0.0, 0.0, 0.0)


def place():
    dp = lax.axis_index("dp")
    tensor = lax.axis_index("tensor")
    return (
        lax.div(dp, 8),
        lax.rem(lax.div(dp, 2), 4),
        lax.rem(dp, 2),
        lax.div(tensor, 4),
        lax.rem(tensor, 4),
    )


def device(zh, y, core, zl, x):
    return ((zh * 4 + y) * 2 + core, zl * 4 + x)


def around(pos, step):
    return lax.rem(pos + step + 4, 4)


def neighbours(spot):
    zh, y, core, zl, x = spot
    return {
        "x+": device(zh, y, core, zl, around(x, 1)),
        "x-": device(zh, y, core, zl, around(x, -1)),
        "y+": device(zh, around(y, 1), core, zl, x),
        "y-": device(zh, around(y, -1), core, zl, x),
        "zl": device(zh, y, core, 1 - zl, x),
        "zh": device(1 - zh, y, core, zl, x),
        "core": device(zh, y, 1 - core, zl, x),
    }


class Links:
    def __init__(self, send_sems, recv_sems):
        self.send_sems, self.recv_sems = send_sems, recv_sems
        self.copies, self.open = [], []

    def send(self, src, dst, target):
        index = len(self.copies)
        copy = pltpu.make_async_remote_copy(
            src_ref=src,
            dst_ref=dst,
            send_sem=self.send_sems.at[index],
            recv_sem=self.recv_sems.at[index],
            device_id=target,
            device_id_type=MESH,
        )
        copy.start()
        self.copies.append(copy)
        self.open.append(copy)
        return copy

    def settle(self, copies):
        for copy in copies:
            copy.wait_send()
        self.open = [each for each in self.open if not any(each is copy for copy in copies)]


class Gather:
    def __init__(self, links, block, z, ring, z_dev, plus, minus, onward):
        self.links, self.block, self.z, self.ring = links, block, z, ring
        self.z_dev, self.ways, self.onward = z_dev, (plus, minus), onward
        self.by_z, self.sent = None, []

    def to(self, z, ring, half, target):
        part = self.block(z, ring, half)
        self.sent.append(self.links.send(part, part, target))
        return self.sent[-1]

    def round(self, z):
        passed = []

        def pass_on(ring):
            if self.onward is not None:
                passed.append(self.to(z, ring, None, self.onward))

        whole = [self.to(z, self.ring, None, way) for way in self.ways]
        pass_on(self.ring)
        halves = []
        for way in range(2):
            yield [whole[way]]
            whole[way].wait_recv()
            from_ring = around(self.ring, 1 if way else -1)
            halves.append(self.to(z, from_ring, way, self.ways[way]))
            pass_on(from_ring)
        yield halves
        for copy in halves:
            copy.wait_recv()
        pass_on(around(self.ring, 2))
        yield passed
        for copy in passed:
            copy.wait_recv()

    def own(self, gate):
        yield [gate]
        if self.z_dev is not None:
            self.by_z = self.to(self.z, self.ring, None, self.z_dev)
        yield from self.round(self.z)

    def far(self, gate):
        yield [gate]
        yield [self.by_z]
        self.by_z.wait_recv()
        yield from self.round(1 - self.z)


class Scatter:
    def __init__(self, links, part, slots, last, z, ring, z_dev, plus, minus):
        self.links, self.part, self.slots, self.last = links, part, slots, last
        self.ring, self.z_dev, self.ways = ring, z_dev, (plus, minus)
        self.zs = (z,) if last is None else (1 - z, z)
        self.sent = {}

    def push(self, way, message, order, ring, half):
        self.sent[way, message, order] = self.links.send(
            self.part(self.zs[order], ring, half),
            self.slots.at[way, message, order],
            self.ways[way],
        )

    def arrived(self, way, message, order):
        self.sent[way, message, order].wait_recv()
        return self.slots[way, message, order].astype(F32)

    def total(self, order, half):
        part = self.part(self.zs[order], self.ring, half)
        return (
            part[...].astype(F32) + self.arrived(half, 2, order) + self.arrived(1 - half, 1, order)
        )

    def feed(self, name, order, gate, done, which=0):
        yield [gate, (name, 2)]
        for way in range(2):
            self.push(way, 0, order, around(self.ring, 2), way)
        for way, step in ((0, 1), (1, 3)):
            yield [(name, step)]
            self.push(way, 1, order, around(self.ring, step), 1 - way)
        done.add((name, "fed", order, which))

    def run(self, name, out, gate, done, which=0):
        for order in range(len(self.zs)):
            yield [(name, "fed", order, which)]
            for way in range(2):
                yield [self.sent[way, 0, order]]
                ring = around(self.ring, -1 if way else 1)
                part = self.part(self.zs[order], ring, way)
                self.sent[way, 0, order].wait_recv()
                part[...] = part[...] + self.slots[way, 0, order]
                self.push(way, 2, order, ring, way)
            done.add((name, "joined", order, which))
        by_z = None
        if self.last is not None:
            yield [(name, 0)] + [self.sent[way, each, 0] for way in range(2) for each in (1, 2)]
            for half in range(2):
                part = self.part(self.zs[0], self.ring, half)
                part[...] = self.total(0, half).astype(BF16)
            by_z = self.links.send(self.part(self.zs[0], self.ring, None), self.last, self.z_dev)
        order = len(self.zs) - 1
        yield [(name, 0), gate] + [
            self.sent[way, each, order] for way in range(2) for each in (1, 2)
        ]
        rows = out.shape[0] // 2
        for half in range(2):
            out[pl.ds(half * rows, rows), :] = self.total(order, half)
        if by_z is not None:
            yield [by_z]
            by_z.wait_recv()
            out[...] = out[...] + self.last[...].astype(F32)


class PairSum:
    def __init__(self, links, part, slots, z, ring, z_dev):
        self.links, self.part, self.slots = links, part, slots
        self.z, self.ring, self.z_dev = z, ring, z_dev

    def run(self, name, flag, done):
        for step in (2, 1, 3, 0):
            yield [(name, step)]
            part = self.part(1 - self.z, around(self.ring, step), None)
            moved = self.links.send(part, self.slots.at[step], self.z_dev)
            yield [moved]
            moved.wait_recv()
            part = self.part(self.z, around(self.ring, step), None)
            part[...] = part[...] + self.slots[step]
            done.add((flag, step))


def rows_of(ref, start, count):
    return ref.at[pl.ds(pl.multiple_of(start, 16), count)]


def row_part(ref, first, count, core=None):
    def part(z, ring, half):
        index, rows = z * 4 + ring, OWN
        if core is not None:
            index = index * 2 + core
        start = index * OWN
        if half is not None:
            start, rows = start + half * (OWN // 2), OWN // 2
        return ref.at[pl.ds(pl.multiple_of(start, 16), rows), pl.ds(first, count)]

    return part


def over_rows(left, right):
    return lax.dot_general(left, right, (((0,), (0,)), ((), ())), preferred_element_type=F32)


def by_rows(left, right):
    return lax.dot_general(left, right, (((1,), (1,)), ((), ())), preferred_element_type=F32)


def gelu_parts(pre):
    cdf = 0.5 * (1.0 + lax.erf(pre * (1.0 / math.sqrt(2.0))))
    density = jnp.exp(-0.5 * pre * pre) * (1.0 / math.sqrt(2.0 * math.pi))
    return pre * cdf, cdf + pre * density


def spin(rows, cosines, sines, back):
    low = rows[:, :128]
    lane = lax.broadcasted_iota(jnp.int32, low.shape, 1)
    ahead = pltpu.roll(low, 96, 1)
    behind = pltpu.roll(low, 32, 1)
    turned = jnp.where(lane < 32, -ahead, jnp.where(lane < 64, behind, 0.0))
    if back:
        turned = -turned
    return jnp.concatenate([low * cosines + turned * sines, rows[:, 128:]], axis=1)


LATE = ("branch", "unit_grad", "up_grad", "qkv_grad",)
ORDER = (
    ".init", "wide", "wide_far", ".rows", "unit0", "unit_side", "unit0_far", "unit1", "unit1_far", ".weights", "wup",
    "wup_far", "deep", "deep_far", ".tables", "wide", "wide", "wide_far", "unit0", "unit0", "unit_side", "unit_side",
    "unit0_far", "wup", "wup", "unit1", "unit1", "unit0", "unit0", "unit1_far", "unit_side", "cot0", "cot_side",
    "cot0_far", "cot1", "cot1_far", "deep", "deep", "wide", "unit0_far", "unit0_far", "wide", "wup_far", "unit1",
    "unit1", "wide_far", "wide_far", "wup", "unit1_far", "unit1_far", "wup", "deep_far", "deep", "cot0", "cot0",
    "deep", "cot_side", "cot_side", "wup_far", "wup_far", "unit_side", "wide_far", "cot1", "cot1", "wide_far",
    "unit0_far", "unit0_far", "cot0_far", "unit1_far", "unit1_far", ".qkv0", "cot0", "cot0", ".qkv1", "deep_far",
    "deep_far", ".att0", "cot_side", ".att1", ".att2", "wup_far", ".att3", "cot1_far", "cot1", "cot1", "wup_far",
    ".hid0a", ".hid0b", "cot0_far", "cot0_far", "deep_far", ".hid1a", ".hid1b", "deep_far", ".mix2", "branch0_feed0",
    "cot1_far", "cot1_far", "branch_pair", "branch1_feed0", ".mix1", "branch0_feed0", "cot0_far", "cot0_far",
    "branch1_feed0", ".mix3", "branch0_feed0", "branch0", "branch1_feed0", "branch1", ".mix0", "branch0", "branch0",
    "branch0_feed1", "branch0_feed1", "branch0_feed1", "branch0", "cot_side", "cot1_far", "cot1_far", ".back0a",
    ".back0b", "branch1", "branch1", "branch_pair", "branch_side_feed0", "branch_pair", "branch1_feed1",
    "branch1_feed1", "branch1_feed1", "branch1", ".back1a", ".back1b", ".deepg2", "branch_pair", "branch_side_feed0",
    "branch_pair", "deep_share", ".dv", ".deepg1", "branch0", "branch0", "branch0", "deep_share", "deep_grad_feed0",
    "deep_grad_feed1", "deep_share", ".deepg3", "branch_pair", "branch_side_feed0", "branch_side", "branch_pair",
    "deep_share", "deep_grad_feed0", "deep_grad_feed1", "deep_share", ".dp0", ".dp1", ".dp2", ".dp3", ".dk",
    "branch_side", "branch_side", "deep_share", "deep_grad_feed0", "deep_grad_feed1", "deep_grad", "deep_grad",
    "deep_grad", "deep_grad", ".deepg0", "branch1", "branch1", "branch1", "deep_share", ".g2", "unit_grad0_feed0",
    "branch_pair", "unit_grad1_feed0", "deep_grad", "deep_grad", "unit_grad_pair", "deep_share", ".g1",
    "unit_grad0_feed0", "branch0", "branch0", "unit_grad1_feed0", ".g3", "unit_grad0_feed0", "unit_grad0",
    "branch_side", "unit_grad1_feed0", "unit_grad1", ".g0", "branch1", "branch1", "unit_grad_pair",
    "unit_grad_side_feed0", "unit_grad_pair", ".pack", "vector", ".upg2", "unit_grad0", "unit_grad0", "vector",
    "up_share", "unit_grad0_feed1", "unit_grad0_feed1", "unit_grad0_feed1", "unit_grad0", "deep_grad", ".qg2",
    "unit_grad1", "unit_grad1", "unit_grad1_feed1", "unit_grad1_feed1", "unit_grad1_feed1", "unit_grad1", "qkv_share",
    ".upg1", "up_share", "up_grad_feed0", "qkv_share", "up_share", "deep_grad", "unit_grad_pair",
    "unit_grad_side_feed0", "unit_grad_pair", "qkv_grad_feed0", ".upg3", "vector", "up_share", "up_grad_feed0",
    "up_share", ".upg0", ".branch_out", "up_share", "up_grad_feed0", "up_share", "up_grad", "up_grad", "deep_grad",
    "up_grad", "up_grad_feed1", "up_grad_feed1", "up_grad_feed1", "up_grad", ".qg1", "unit_grad0", "unit_grad0",
    "unit_grad0", "qkv_share", "up_share", ".qg3", "vector", "qkv_share", "qkv_share", "unit_grad_pair",
    "unit_grad_side_feed0", "unit_grad_side", "unit_grad_side", "unit_grad_side", "unit_grad_pair", "qkv_grad_feed0",
    ".qg0", "qkv_share", "qkv_share", "qkv_grad_feed0", "qkv_grad", "qkv_grad", "qkv_grad", "qkv_grad_feed1",
    "qkv_grad_feed1", "qkv_grad_feed1", "qkv_grad", "unit_grad1", "unit_grad1", "unit_grad1", "qkv_share", "vector",
    "up_grad", "up_grad", "up_grad", "unit_grad_pair", "unit_grad0", "unit_grad0", "unit_grad_side", "unit_grad1",
    "unit_grad1", "vector", "qkv_grad", "qkv_grad", "qkv_grad", "up_grad", "up_grad", "qkv_grad", "qkv_grad",
)


def layer_kernel(
    lens,
    x_in,
    cot_in,
    w_qkv,
    w_out,
    w_up,
    w_down,
    b_qkv,
    b_up,
    gains,
    biases,
    branch_sum,
    unit_sum,
    qkv_sum,
    up_sum,
    deep_sum,
    vector_sum,
    low_sum,
    unit,
    cot,
    wide,
    deep,
    up,
    q,
    k,
    v,
    acts,
    probs,
    branch,
    grads,
    mixed_grad,
    sums,
    low_sums,
    vectors,
    vector_slots,
    up_core,
    deep_core,
    qkv_slots,
    up_slots,
    deep_slots,
    branch_slots,
    unit_slots,
    branch_side_slots,
    unit_side_slots,
    branch_pairs,
    unit_pairs,
    qkv_last,
    up_last,
    deep_last,
    branch_last,
    unit_last,
    row_total,
    qkv_total,
    up_total,
    deep_total,
    send_sems,
    recv_sems,
    core_send,
    core_recv,
    load_sems,
    store_sems,
):
    spot = place()
    zh, y, core, zl, x = spot
    near = neighbours(spot)
    near["x2"] = device(zh, y, core, zl, around(x, 2))
    near["y2"] = device(zh, around(y, 2), core, zl, x)
    barrier = pltpu.get_barrier_semaphore()
    for target in near.values():
        pl.semaphore_signal(barrier, inc=1, device_id=target, device_id_type=MESH)

    mine = pl.ds(pl.multiple_of((zl * 4 + x) * OWN, OWN), OWN)
    own = pl.ds(pl.multiple_of(((zh * 4 + y) * 2 + core) * OWN, OWN), OWN)
    loads = []
    for src, dst in (
        *((w_qkv.at[head], qkv_total.at[:, pl.ds(head * HEAD, HEAD)]) for head in range(3)),
        (x_in, unit.at[mine, :]),
        (w_up, up_total),
        (w_out, deep_total.at[pl.ds(0, HEAD), :]),
        (w_down, deep_total.at[pl.ds(HEAD, UNITS), :]),
        (cot_in, cot.at[mine, :]),
    ):
        loads.append(pltpu.make_async_copy(src, dst, load_sems.at[len(loads)]))
        loads[-1].start()

    links = Links(send_sems, recv_sems)
    stores = []
    done = set()

    def store(src, dst):
        copy = pltpu.make_async_copy(src, dst, store_sems.at[len(stores)])
        copy.start()
        stores.append(copy)
        return copy

    def deep_part(z, ring, half):
        columns = pl.ds(pl.multiple_of(((z * 4 + ring) * 2 + core) * OWN, OWN), OWN)
        if half is None:
            return deep.at[:, columns]
        return deep.at[pl.ds(half * (DEEP // 2), DEEP // 2), columns]

    def deep_place(chip, who):
        return deep.at[:, pl.ds(pl.multiple_of((chip * 2 + who) * OWN, OWN), OWN)]

    def up_place(chip, who):
        return rows_of(up, (chip * 2 + who) * OWN, OWN)

    def qkv_place(chip, who):
        return rows_of(wide, (chip * 2 + who) * OWN, OWN).at[:, pl.ds(0, QKV)]

    shares = (
        (deep_place, lambda slot: deep_core.at[slot]),
        (up_place, lambda slot: up_core.at[slot]),
        (qkv_place, lambda slot: rows_of(probs, slot * OWN, OWN).at[:, pl.ds(0, QKV)]),
    )

    def chip_at(ring, turn_of):
        return (zh + (1 - 2 * zh) * turn_of) * 4 + around(y, ring)

    def core_copy(which, ring, turn_of):
        number = which * 8 + ring * 2 + turn_of
        place_of, slots = shares[which]
        return pltpu.make_async_remote_copy(
            src_ref=place_of(chip_at(ring, turn_of), 1 - core),
            dst_ref=slots(ring * 2 + turn_of),
            send_sem=core_send.at[number],
            recv_sem=core_recv.at[number],
            device_id=near["core"],
            device_id_type=MESH,
        )

    def share(which, name):
        place_of, slots = shares[which]

        def add(ring, turn_of):
            core_copy(which, ring, turn_of).wait_recv()
            part = place_of(chip_at(ring, turn_of), core)
            part[...] = part[...] + slots(ring * 2 + turn_of)[...]
            return ring

        for step in (2, 1, 3, 0):
            yield [(name + "_raw", step)]
            yield []
            lax.fori_loop(0, 2, lambda turn_of, _: add(step, turn_of), 0)
            done.add((name, step))

    def add_vectors():
        yield [("sums", "ready")]
        slot = 0
        for stage, (names, count) in enumerate(
            (
                (("core",), 96),
                (("y+", "y-", "y2"), 96),
                (("zh",), 96),
                (("zl",), 80),
                (("x+", "x-", "x2"), 80),
            )
        ):
            span = pl.ds(0, count)
            copies = [
                links.send(
                    vectors.at[stage, span], vector_slots.at[slot + index, span], near[name]
                )
                for index, name in enumerate(names)
            ]
            yield copies
            for copy in copies:
                copy.wait_recv()
            parts = [vectors[stage, :count, :]]
            parts += [vector_slots[slot + index, :count, :] for index in range(len(copies))]
            if len(parts) == 2:
                total = parts[0] + parts[1]
            else:
                total = (parts[0] + parts[3]) + (parts[1] + parts[2])
            vectors[stage + 1, :count, :] = total
            slot += len(names)
        for row in range(5):
            for column in range(16):
                sums[row : row + 1, column * 128 : (column + 1) * 128] = vectors[
                    5, row * 16 + column : row * 16 + column + 1, :
                ]
        for column in range(14):
            low_sums[0:1, column * 128 : (column + 1) * 128] = vectors[
                3, 80 + column : 81 + column, :
            ]
        store(sums, vector_sum)
        store(low_sums, low_sum)

    def keep(steps, src, dst):
        yield from steps
        store(src, dst)

    tensor_ends = (zl, x, near["zl"], near["x+"], near["x-"])
    side_ends = (zl, x, None, near["x+"], near["x-"], near["zl"])
    data_ends = (zh, y, near["zh"], near["y+"], near["y-"])
    units_side = Gather(links, row_part(unit, MAIN_UNIT, D - MAIN_UNIT), *side_ends)
    cots_side = Gather(links, row_part(cot, MAIN_COT, D - MAIN_COT), *side_ends)
    wides = Gather(links, row_part(wide, 0, QKV, core), *data_ends, near["core"])
    wups = Gather(links, row_part(wide, QKV, UNITS, core), *data_ends, near["core"])
    deeps = Gather(links, deep_part, *data_ends, near["core"])

    side_branch = row_part(branch, MAIN_BRANCH, D - MAIN_BRANCH)
    side_grad = row_part(cot, MAIN_GRAD, D - MAIN_GRAD)
    branch_side = Scatter(links, side_branch, branch_side_slots, None, *tensor_ends)
    branch_pair = PairSum(links, side_branch, branch_pairs, zl, x, near["zl"])
    unit_side = Scatter(links, side_grad, unit_side_slots, None, *tensor_ends)
    unit_pair = PairSum(links, side_grad, unit_pairs, zl, x, near["zl"])
    qkv_grid = Scatter(links, row_part(wide, 0, QKV, core), qkv_slots, qkv_last, *data_ends)
    up_grid = Scatter(links, row_part(up, 0, UNITS, core), up_slots, up_last, *data_ends)
    deep_grid = Scatter(links, deep_part, deep_slots, deep_last, *data_ends)
    go, free, turned = ("own", "ready"), ("rows", "free"), ("turn", "free")

    def late(name, which=0):
        return (name, "joined", 0, which) if name in LATE else go

    transfers = {
        "unit_side": units_side.own(("unit", "ready")),
        "cot_side": cots_side.own(("rest", "ready")),
        "wide": wides.own(("wide", "ready")),
        "wide_far": wides.far(("wide", "sent")),
        "wup": wups.own(("rest", "ready")),
        "wup_far": wups.far(("wup", "sent")),
        "deep": deeps.own(("rest", "ready")),
        "deep_far": deeps.far(("deep", "sent")),
        "branch_pair": branch_pair.run("branch", "branch_side", done),
        "branch_side_feed0": branch_side.feed("branch_side", 0, go, done),
        "branch_side": branch_side.run(
            "branch_side", row_total.at[:, pl.ds(MAIN_BRANCH, D - MAIN_BRANCH)], turned, done
        ),
        "unit_grad_pair": unit_pair.run("unit_grad", "unit_grad_side", done),
        "unit_grad_side_feed0": unit_side.feed("unit_grad_side", 0, go, done),
        "unit_grad_side": unit_side.run(
            "unit_grad_side", row_total.at[:, pl.ds(MAIN_GRAD, D - MAIN_GRAD)], free, done
        ),
        "deep_share": share(0, "deep_grad"),
        "deep_grad_feed0": deep_grid.feed("deep_grad", 0, go, done),
        "deep_grad_feed1": deep_grid.feed("deep_grad", 1, late("deep_grad"), done),
        "deep_grad": keep(deep_grid.run("deep_grad", deep_total, go, done), deep_total, deep_sum),
        "up_share": share(1, "up_grad"),
        "up_grad_feed0": up_grid.feed("up_grad", 0, go, done),
        "up_grad_feed1": up_grid.feed("up_grad", 1, late("up_grad"), done),
        "up_grad": keep(up_grid.run("up_grad", up_total, go, done), up_total, up_sum),
        "qkv_share": share(2, "qkv_grad"),
        "qkv_grad_feed0": qkv_grid.feed("qkv_grad", 0, go, done),
        "qkv_grad_feed1": qkv_grid.feed("qkv_grad", 1, late("qkv_grad"), done),
        "qkv_grad": keep(qkv_grid.run("qkv_grad", qkv_total, go, done), qkv_total, qkv_sum),
        "vector": add_vectors(),
    }

    cot_gathers = [cots_side]
    for name, ref, main, chunks, gate in (
        ("unit", unit, MAIN_UNIT, CHUNKS[0], "unit"),
        ("cot", cot, MAIN_COT, CHUNKS[1], "rest"),
    ):
        for which in range(chunks):
            size = main // chunks
            gather = Gather(links, row_part(ref, which * size, size), *tensor_ends, None)
            transfers[f"{name}{which}"] = gather.own((gate, "ready"))
            transfers[f"{name}{which}_far"] = gather.far((f"{name}{which}", "sent"))
            if name == "cot":
                cot_gathers.append(gather)
    for name, ref, slots, last, main, chunks, gate in (
        ("branch", branch, branch_slots, branch_last, MAIN_BRANCH, CHUNKS[2], turned),
        ("unit_grad", cot, unit_slots, unit_last, MAIN_GRAD, CHUNKS[3], free),
    ):
        for which in range(chunks):
            size = main // chunks
            span = pl.ds(which * size, size)
            scatter = Scatter(
                links,
                row_part(ref, which * size, size),
                slots.at[:, :, :, :, span],
                last.at[:, span],
                *tensor_ends,
            )
            transfers[f"{name}{which}_feed0"] = scatter.feed(name, 0, go, done, which)
            transfers[f"{name}{which}_feed1"] = scatter.feed(name, 1, late(name, which), done, which)
            out = row_total.at[:, span]
            transfers[f"{name}{which}"] = scatter.run(name, out, gate, done, which)

    ends = [lens[0, 0]]
    for seq in range(1, 3):
        ends.append(ends[-1] + lens[0, seq])

    def begin_of(index):
        begin = jnp.zeros_like(index)
        for end in ends:
            begin = jnp.where(index >= end, end, begin)
        return begin

    def own_first():
        for load in loads[:3]:
            load.wait()
        wide[own, :QKV] = qkv_total[...].astype(BF16)
        pl.semaphore_wait(barrier, len(near))
        done.update([("wide", "ready"), go])

    def own_rows():
        loads[3].wait()
        rows = unit[mine, :].astype(F32)
        centred = rows - jnp.mean(rows, axis=-1, keepdims=True)
        variance = jnp.mean(centred * centred, axis=-1, keepdims=True)
        unit[mine, :] = (centred * lax.rsqrt(variance + NORM_EPS)).astype(BF16)
        done.add(("unit", "ready"))

    def own_weights():
        for load in loads[4:]:
            load.wait()
        wide[own, QKV:] = up_total[...].astype(BF16)
        deep[:, own] = deep_total[...].astype(BF16)
        done.add(("rest", "ready"))

    def tables():
        sums[...] = jnp.zeros_like(sums)
        low_sums[...] = jnp.zeros_like(low_sums)
        sums[4:5, :] = jnp.sum(cot[mine, :].astype(F32), axis=0, keepdims=True)
        row = lax.broadcasted_iota(jnp.int32, (OWN, 128), 0)
        lane = lax.broadcasted_iota(jnp.int32, (OWN, 128), 1)
        rate = jnp.exp(lax.rem(lane, 32).astype(F32) * (-2.0 * math.log(10000.0) / ROT))
        for block in range(TOK // OWN):
            index = row + block * OWN
            angle = (index - begin_of(index)).astype(F32) * rate
            columns = slice(block * 128, (block + 1) * 128)
            row_total[:, columns] = jnp.where(lane < ROT, jnp.cos(angle), 1.0)
            columns = slice(TOK + block * 128, TOK + (block + 1) * 128)
            row_total[:, columns] = jnp.where(lane < ROT, jnp.sin(angle), 0.0)

    def turn(which, part):
        blocks = range(part.start // OWN, part.stop // OWN)
        starts = [which * TOK + block * 128 for block in blocks]
        return jnp.concatenate([row_total[:, start : start + 128] for start in starts], axis=0)

    def norm_tile(tile, which):
        part = slice(tile * TILE, (tile + 1) * TILE)
        span = slice(which * TILE, (which + 1) * TILE)
        rows = unit[part, :].astype(F32)
        branch[span, :] = (
            rows * gains[which : which + 1, :] + biases[which : which + 1, :]
        ).astype(BF16)

    def heads(tile):
        part = slice(tile * TILE, (tile + 1) * TILE)
        norm_tile(tile, 0)
        for which, target in enumerate((q, k, v)):
            columns = slice(which * HEAD, (which + 1) * HEAD)
            head = jnp.dot(branch[:TILE, :], wide[:, columns], preferred_element_type=F32)
            head = head + b_qkv[which : which + 1, :]
            if which < 2:
                head = spin(head, turn(0, part), turn(1, part), False)
            target[part, :] = head.astype(BF16)

    def hidden(tile, half):
        part = slice(tile * TILE, (tile + 1) * TILE)
        if half == 0:
            norm_tile(tile, 1)

        def one(piece, _):
            shift = pl.multiple_of(piece * 256, 256)
            pre = jnp.dot(
                branch[TILE:, :], wide[:, pl.ds(QKV + shift, 256)], preferred_element_type=F32
            )
            pre = pre + b_up[0:1, pl.ds(shift, 256)]
            value, rise = gelu_parts(pre)
            acts[part, pl.ds(HEAD + shift, 256)] = value.astype(BF16)
            grads[part, pl.ds(QKV + shift, 256)] = rise.astype(BF16)
            return 0

        lax.fori_loop(2 * half, 2 * half + 2, one, 0, unroll=2)

    def attend(block):
        part = slice(block * QROWS, (block + 1) * QROWS)
        keys = (block + 1) * QROWS
        whole = by_rows(q[part, :], k[:keys, :]) * (HEAD**-0.5)
        for start in range(0, QROWS, OWN):
            scores = whole[start : start + OWN]
            start = block * QROWS + start
            key = lax.broadcasted_iota(jnp.int32, (OWN, keys), 1)
            row = lax.broadcasted_iota(jnp.int32, (OWN, 1), 0) + start
            scores = jnp.where((key <= row) & (key >= begin_of(row)), scores, -jnp.inf)
            expo = jnp.exp(scores - jnp.max(scores, axis=-1, keepdims=True))
            mass = expo / jnp.sum(expo, axis=-1, keepdims=True)
            probs[start : start + OWN, :keys] = mass.astype(BF16)
        acts[part, :HEAD] = jnp.dot(
            probs[part, :keys], v[:keys, :], preferred_element_type=F32
        ).astype(BF16)

    def pieces_of(ring):
        starts = (around(x, ring) * OWN, (4 + around(x, ring)) * OWN)
        return [pl.ds(pl.multiple_of(start, OWN), OWN) for start in starts]

    def mix(step):
        pieces = pieces_of(step)

        def one(piece, _):
            columns = pl.ds(pl.multiple_of(piece * 512, 512), 512)
            rows = jnp.concatenate([acts[each, :] for each in pieces], axis=0)
            both = jnp.dot(rows, deep[:, columns], preferred_element_type=F32).astype(BF16)
            branch[pieces[0], columns] = both[:OWN]
            branch[pieces[1], columns] = both[OWN:]
            return 0

        lax.fori_loop(0, D // 512, one, 0, unroll=4)
        done.add(("branch", step))

    def back(tile, half):
        part = slice(tile * TILE, (tile + 1) * TILE)
        if half == 0:
            mixed_grad[part, :] = by_rows(cot[part, :], deep[:HEAD, :]).astype(BF16)

        def one(piece, _):
            shift = pl.multiple_of(piece * 256, 256)
            columns = pl.ds(QKV + shift, 256)
            grad = by_rows(cot[part, :], deep[pl.ds(HEAD + shift, 256), :])
            grad = grad * grads[part, columns].astype(F32)
            low_sums[0:1, columns] += jnp.sum(grad, axis=0, keepdims=True)
            grads[part, columns] = grad.astype(BF16)
            return 0

        lax.fori_loop(2 * half, 2 * half + 2, one, 0, unroll=2)

    def deep_grads(step):
        if step == 2:
            links.settle(deeps.sent)

        def one(turn_of, _):
            columns = pl.ds(pl.multiple_of(chip_at(step, turn_of) * 256, 256), 256)
            for half in range(2):
                part = slice(half * (DEEP // 2), (half + 1) * (DEEP // 2))
                deep[part, columns] = over_rows(acts[:, part], cot[:, columns]).astype(BF16)
            core_copy(0, step, turn_of).start()
            return 0

        lax.fori_loop(0, 2, one, 0)
        done.add(("deep_grad_raw", step))

    def norm_columns(span, which):
        acts[:, :256] = (
            unit[:, span].astype(F32) * gains[which : which + 1, span]
            + biases[which : which + 1, span]
        ).astype(BF16)

    def up_grads(step):
        def one(turn_of, _):
            span = pl.ds(pl.multiple_of(chip_at(step, turn_of) * 256, 256), 256)
            norm_columns(span, 1)
            up[span, :] = over_rows(acts[:, :256], grads[:, QKV:]).astype(BF16)
            core_copy(1, step, turn_of).start()
            return 0

        lax.fori_loop(0, 2, one, 0)
        done.add(("up_grad_raw", step))

    def qkv_grads(step):
        if step == 2:
            links.settle(wides.sent)

        def one(turn_of, _):
            span = pl.ds(pl.multiple_of(chip_at(step, turn_of) * 256, 256), 256)
            norm_columns(span, 0)
            wide[span, :QKV] = over_rows(acts[:, :256], grads[:, :QKV]).astype(BF16)
            core_copy(2, step, turn_of).start()
            return 0

        lax.fori_loop(0, 2, one, 0)
        done.add(("qkv_grad_raw", step))

    def put_grad(grad, part, which):
        columns = slice(which * HEAD, (which + 1) * HEAD)
        if which < 2:
            grad = spin(grad * (HEAD**-0.5), turn(0, part), turn(1, part), True)
        low_sums[0:1, columns] += jnp.sum(grad, axis=0, keepdims=True)
        grads[part, columns] = grad.astype(BF16)

    def value_grads():
        for block in range(TOK // QROWS):
            part = slice(block * QROWS, (block + 1) * QROWS)
            below = slice(block * QROWS, TOK)
            put_grad(over_rows(probs[below, part], mixed_grad[below, :]), part, 2)

    def query_grads(block):
        part = slice(block * QROWS, (block + 1) * QROWS)
        keys = (block + 1) * QROWS
        whole = by_rows(mixed_grad[part, :], v[:keys, :])
        for start in range(0, QROWS, OWN):
            prob_grad = whole[start : start + OWN]
            rows = slice(block * QROWS + start, block * QROWS + start + OWN)
            mass = probs[rows, :keys].astype(F32)
            delta = jnp.sum(mass * prob_grad, axis=-1, keepdims=True)
            probs[rows, :keys] = (mass * (prob_grad - delta)).astype(BF16)
        put_grad(jnp.dot(probs[part, :keys], k[:keys, :], preferred_element_type=F32), part, 0)

    def key_grads():
        for block in range(TOK // QROWS):
            part = slice(block * QROWS, (block + 1) * QROWS)
            below = slice(block * QROWS, TOK)
            put_grad(over_rows(probs[below, part], q[below, :]), part, 1)
        done.add(turned)

    def unit_grads(step):
        if step == 2:
            for gather in cot_gathers:
                links.settle(gather.sent)
        pieces = pieces_of(step)
        for half in range(2):
            acts[half * OWN : (half + 1) * OWN, :QKV] = grads[pieces[half], :QKV]
            acts[(2 + half) * OWN : (3 + half) * OWN, :UNITS] = grads[pieces[half], QKV:]

        def one(piece, _):
            columns = pl.ds(pl.multiple_of(piece * 512, 512), 512)
            first = by_rows(acts[: 2 * OWN, :QKV], wide[columns, :QKV])
            second = by_rows(acts[2 * OWN : 4 * OWN, :UNITS], wide[columns, QKV:])
            rows = jnp.concatenate([unit[each, columns] for each in pieces], axis=0).astype(F32)
            sums[0:1, columns] += jnp.sum(first * rows, axis=0, keepdims=True)
            sums[1:2, columns] += jnp.sum(second * rows, axis=0, keepdims=True)
            sums[2:3, columns] += jnp.sum(first, axis=0, keepdims=True)
            sums[3:4, columns] += jnp.sum(second, axis=0, keepdims=True)
            both = (first * gains[0:1, columns] + second * gains[1:2, columns]).astype(BF16)
            cot[pieces[0], columns] = both[:OWN]
            cot[pieces[1], columns] = both[OWN:]
            return 0

        lax.fori_loop(0, D // 512, one, 0, unroll=4)
        done.add(("unit_grad", step))

    def pack():
        for row in range(5):
            for column in range(16):
                vectors[0, row * 16 + column : row * 16 + column + 1, :] = sums[
                    row : row + 1, column * 128 : (column + 1) * 128
                ]
        for column in range(14):
            vectors[0, 80 + column : 81 + column, :] = low_sums[
                0:1, column * 128 : (column + 1) * 128
            ]
        vectors[0, 94:96, :] = jnp.zeros((2, 128), F32)
        done.add(("sums", "ready"))

    branch_stores = []

    def branch_out():
        branch_stores.append(pltpu.make_async_copy(row_total, branch_sum, store_sems.at[7]))
        branch_stores[0].start()
        branch_stores[0].wait()
        done.add(free)

    compute = {
        ".init": own_first,
        ".rows": own_rows,
        ".weights": own_weights,
        ".tables": tables,
        ".dv": value_grads,
        ".dk": key_grads,
        ".pack": pack,
        ".branch_out": branch_out,
    }
    for tile in range(TOK // TILE):
        compute[f".qkv{tile}"] = functools.partial(heads, tile)
        for half, letter in enumerate("ab"):
            compute[f".hid{tile}{letter}"] = functools.partial(hidden, tile, half)
            compute[f".back{tile}{letter}"] = functools.partial(back, tile, half)
    for step in range(4):
        compute[f".att{step}"] = functools.partial(attend, step)
        compute[f".dp{step}"] = functools.partial(query_grads, step)
        compute[f".mix{step}"] = functools.partial(mix, step)
        compute[f".deepg{step}"] = functools.partial(deep_grads, step)
        compute[f".upg{step}"] = functools.partial(up_grads, step)
        compute[f".qg{step}"] = functools.partial(qkv_grads, step)
        compute[f".g{step}"] = functools.partial(unit_grads, step)

    waiting = {name: next(steps) for name, steps in transfers.items()}
    for name in ORDER:
        if name in compute:
            compute.pop(name)()
            continue
        assert all(each in done for each in waiting[name] if isinstance(each, tuple)), name
        waiting[name] = next(transfers[name], None)
        done.add((name, "sent"))
        if waiting[name] is None:
            del waiting[name]
    assert not waiting and not compute
    store(row_total, unit_sum)

    for which in range(3):
        for step in range(4):
            for turn_of in range(2):
                core_copy(which, step, turn_of).wait_send()
    for copy in stores:
        copy.wait()
    links.settle(links.open)


SUMS = (
    ((OWN, D), F32),
    ((OWN, D), F32),
    ((OWN, QKV), F32),
    ((OWN, UNITS), F32),
    ((DEEP, OWN), F32),
    ((8, D), F32),
    ((8, WIDE), F32),
)
HALF = OWN // 2
SCRATCH = (
    ((TOK, D), BF16),
    ((TOK, D), BF16),
    ((D, WIDE), BF16),
    ((DEEP, D), BF16),
    ((D, UNITS), BF16),
    ((TOK, HEAD), BF16),
    ((TOK, HEAD), BF16),
    ((TOK, HEAD), BF16),
    ((TOK, DEEP), BF16),
    ((TOK, TOK), BF16),
    ((TOK, D), BF16),
    ((TOK, WIDE), BF16),
    ((TOK, HEAD), BF16),
    ((8, D), F32),
    ((8, WIDE), F32),
    ((6, 96, 128), F32),
    ((9, 96, 128), F32),
    ((8, OWN, UNITS), BF16),
    ((8, DEEP, OWN), BF16),
    ((2, 3, 2, HALF, QKV), BF16),
    ((2, 3, 2, HALF, UNITS), BF16),
    ((2, 3, 2, DEEP // 2, OWN), BF16),
    ((2, 3, 2, HALF, MAIN_BRANCH), BF16),
    ((2, 3, 2, HALF, MAIN_GRAD), BF16),
    ((2, 3, 1, HALF, D - MAIN_BRANCH), BF16),
    ((2, 3, 1, HALF, D - MAIN_GRAD), BF16),
    ((4, OWN, D - MAIN_BRANCH), BF16),
    ((4, OWN, D - MAIN_GRAD), BF16),
    ((OWN, QKV), BF16),
    ((OWN, UNITS), BF16),
    ((DEEP, OWN), BF16),
    ((OWN, MAIN_BRANCH), BF16),
    ((OWN, MAIN_GRAD), BF16),
    ((OWN, D), F32),
    ((OWN, QKV), F32),
    ((OWN, UNITS), F32),
    ((DEEP, OWN), F32),
)


def run_layer(lens, layer_in, cotangent, w_qkv, w_out, w_up, w_down, *vectors):
    anywhere = pl.BlockSpec(memory_space=pl.ANY)
    vmem = pl.BlockSpec(memory_space=pltpu.VMEM)
    return pl.pallas_call(
        layer_kernel,
        out_shape=[jax.ShapeDtypeStruct(*each) for each in SUMS],
        in_specs=[pl.BlockSpec(memory_space=pltpu.SMEM)] + [anywhere] * 6 + [vmem] * len(vectors),
        out_specs=[anywhere] * len(SUMS),
        scratch_shapes=[pltpu.VMEM(*each) for each in SCRATCH]
        + [
            pltpu.SemaphoreType.DMA((260,)),
            pltpu.SemaphoreType.DMA((260,)),
            pltpu.SemaphoreType.DMA((24,)),
            pltpu.SemaphoreType.DMA((24,)),
            pltpu.SemaphoreType.DMA((8,)),
            pltpu.SemaphoreType.DMA((8,)),
        ],
        compiler_params=pltpu.CompilerParams(
            collective_id=0, has_side_effects=True, vmem_limit_bytes=63 * 2**20
        ),
        cost_estimate=pl.CostEstimate(flops=42 * 10**9, bytes_accessed=10**7, transcendentals=0),
        name="layer",
    )(lens, layer_in, cotangent, w_qkv, w_out, w_up, w_down, *vectors)


def adam_step(weight, gradient, moment_one, moment_two, step_rate, decay_rate):
    moment_one = BETA_ONE * moment_one + (1.0 - BETA_ONE) * gradient
    moment_two = BETA_TWO * moment_two + (1.0 - BETA_TWO) * gradient * gradient
    spread = jnp.sqrt(moment_two * (1.0 / (1.0 - BETA_TWO**STEP))) + ADAM_EPS
    ratio = moment_one * (1.0 / (1.0 - BETA_ONE**STEP)) / spread
    return (moment_one, moment_two, weight - step_rate * (ratio + decay_rate * weight))


BIG = 14
AHEAD = 4


def update_kernel(*refs):
    sums, refs = refs[:7], refs[7:]
    big, refs = refs[:BIG], refs[BIG:]
    small, refs = refs[:12], refs[12:]
    big_out, refs = refs[:BIG], refs[BIG:]
    small_out, refs = refs[:12], refs[12:]
    sum_bufs, refs = refs[:7], refs[7:]
    in_bufs, refs = refs[:BIG], refs[BIG:]
    small_bufs, refs = refs[:12], refs[12:]
    row_bufs, bias_rows, load_sems, store_sems = refs[:2], refs[2], refs[3], refs[4]
    branch, unit_grad, qkv, up, deep, vectors, low_vectors = sum_bufs
    loads, stores = [], []

    def fetch(src, dst):
        copy = pltpu.make_async_copy(src, dst, load_sems.at[len(loads)])
        loads.append(copy)
        copy.start()
        return copy

    def put(src, dst):
        copy = pltpu.make_async_copy(src, dst, store_sems.at[len(stores)])
        stores.append(copy)
        copy.start()

    def matrix(which, at, sum_index, sum_at, gradient_of):
        first = 2 + 3 * which

        def start():
            copies = [fetch(sums[sum_index].at[sum_at], sum_bufs[sum_index].at[sum_at])]
            for index in range(first, first + 3):
                copies.append(fetch(big[index].at[at], in_bufs[index].at[at]))
            return copies

        def finish():
            weight, one, two = (each.at[at] for each in in_bufs[first : first + 3])
            for part, gradient in gradient_of(sum_bufs[sum_index].at[sum_at]):
                results = adam_step(
                    weight[part],
                    gradient,
                    one[part],
                    two[part],
                    STEP_RATES[which],
                    DECAY_RATES[which],
                )
                one[part], two[part], weight[part] = results
            for index, src in enumerate((one, two, weight)):
                put(src, big_out[first + index].at[at])

        return start, finish

    def plain(ref):
        return [(slice(None), ref[...])]

    def by_head(ref):
        return [(head, ref[:, head * HEAD : (head + 1) * HEAD]) for head in range(3)]

    def rows_part(at):
        def start():
            return [
                fetch(src.at[at], dst.at[at])
                for src, dst in (
                    (big[0], in_bufs[0]),
                    (big[1], in_bufs[1]),
                    (sums[0], branch),
                    (sums[1], unit_grad),
                )
            ]

        def finish():
            biases = bias_rows
            resid = in_bufs[0][at, :].astype(F32)
            total = resid + branch[at, :] + biases[2:3, :] + biases[3:4, :]
            row_bufs[0][at, :] = total.astype(BF16)
            put(row_bufs[0].at[at], big_out[0].at[at])
            centred = resid - jnp.mean(resid, axis=-1, keepdims=True)
            inverse = lax.rsqrt(jnp.mean(centred * centred, axis=-1, keepdims=True) + NORM_EPS)
            unit = centred * inverse
            grad = unit_grad[at, :]
            mean = jnp.mean(grad, axis=-1, keepdims=True)
            along = jnp.mean(grad * unit, axis=-1, keepdims=True)
            back = in_bufs[1][at, :].astype(F32) + inverse * (grad - mean - unit * along)
            row_bufs[1][at, :] = back
            put(row_bufs[1].at[at], big_out[1].at[at])

        return start, finish

    def vector_part():
        def start():
            copies = [fetch(sums[index], sum_bufs[index]) for index in (5, 6)]
            return copies + [fetch(*each) for each in zip(small, small_bufs)]

        def finish():
            slots = (
                (0, 4, [low_vectors[0:1, head * HEAD : (head + 1) * HEAD] for head in range(3)]),
                (3, 5, [low_vectors[0:1, QKV:]]),
                (6, 6, [vectors[0:1, :], vectors[1:2, :]]),
                (9, 7, [vectors[2:3, :], vectors[3:4, :], vectors[4:5, :], vectors[4:5, :]]),
            )
            bias_rows[...] = small_bufs[9][...]
            for first, which, gradients in slots:
                weight, one, two = small_bufs[first : first + 3]
                for row, gradient in enumerate(gradients):
                    at = slice(row, row + 1)
                    results = adam_step(
                        weight[at, :],
                        gradient,
                        one[at, :],
                        two[at, :],
                        STEP_RATES[which],
                        DECAY_RATES[which],
                    )
                    one[at, :], two[at, :], weight[at, :] = results
                for index, src in enumerate((one, two, weight)):
                    put(src, small_out[first + index])

        return start, finish

    halves = [pl.ds(0, OWN // 2), pl.ds(OWN // 2, OWN // 2)]
    parts = [matrix(1, slice(None), 4, pl.ds(0, HEAD), plain)]
    for start in (0, UNITS // 2):
        at = pl.ds(start, UNITS // 2)
        parts.append(matrix(3, at, 4, pl.ds(HEAD + start, UNITS // 2), plain))
    parts += [matrix(2, at, 3, at, plain) for at in halves]
    parts += [matrix(0, (slice(None), at), 2, at, by_head) for at in halves]
    parts.insert(0, vector_part())
    parts += [rows_part(at) for at in halves]
    copies = [start() for start, _ in parts[:AHEAD]]
    for index, (_, finish) in enumerate(parts):
        if index + AHEAD < len(parts):
            copies.append(parts[index + AHEAD][0]())
        for copy in copies[index]:
            copy.wait()
        finish()
    for copy in stores:
        copy.wait()


def run_update(sums, big, small):
    anywhere = pl.BlockSpec(memory_space=pl.ANY)
    matrices = [jax.ShapeDtypeStruct(each.shape, F32) for each in big[2:]]
    rows = [jax.ShapeDtypeStruct((OWN, D), BF16), jax.ShapeDtypeStruct((OWN, D), F32)]
    return pl.pallas_call(
        update_kernel,
        out_shape=rows + matrices + [jax.ShapeDtypeStruct(each.shape, F32) for each in small],
        in_specs=[anywhere] * (len(sums) + BIG + 12),
        out_specs=[anywhere] * (BIG + 12),
        scratch_shapes=[pltpu.VMEM(each.shape, F32) for each in sums]
        + [pltpu.VMEM(each.shape, each.dtype) for each in big]
        + [pltpu.VMEM(each.shape, F32) for each in small]
        + [pltpu.VMEM((OWN, D), BF16), pltpu.VMEM((OWN, D), F32), pltpu.VMEM((4, D), F32)]
        + [pltpu.SemaphoreType.DMA((64,)), pltpu.SemaphoreType.DMA((48,))],
        compiler_params=pltpu.CompilerParams(vmem_limit_bytes=63 * 2**20),
        cost_estimate=pl.CostEstimate(flops=10**7, bytes_accessed=16 * 10**6, transcendentals=0),
        name="update",
    )(*sums, *big, *small)


def local(layer_in, cotangent, seq_lengths, *state):
    params, moments = list(state[:8]), list(state[8:])
    params[0] = params[0].transpose(1, 0, 2)
    moments[0], moments[1] = (each.transpose(1, 0, 2) for each in moments[:2])
    params[5] = params[5].reshape(1, UNITS)
    moments[10], moments[11] = (each.reshape(1, UNITS) for each in moments[10:12])
    sums = run_layer(seq_lengths, layer_in, cotangent, *params)
    groups = [(params[which], moments[2 * which], moments[2 * which + 1]) for which in range(8)]
    big = [layer_in, cotangent] + [each for group in groups[:4] for each in group]
    small = [each for group in groups[4:] for each in group]
    results = list(run_update(sums, big, small))
    for index in range(2, 5):
        results[index] = results[index].transpose(1, 0, 2)
    for index in range(17, 20):
        results[index] = results[index].reshape(UNITS)
    return tuple(results)


def solution(mesh):
    rows = P(("dp", "tensor"), None)
    out, up = P("tensor", "dp"), P("dp", "tensor")
    params = (P("dp", None, "tensor"), out, up, out, P(None, "tensor"), P("tensor"), P(), P())
    moments = [spec for spec in params for _ in range(2)]
    return jax.shard_map(
        local,
        mesh=mesh,
        in_specs=(rows, rows, P("dp", None), *params, *moments),
        out_specs=(rows, rows, *[spec for spec in params for _ in range(3)]),
        check_vma=False,
    )
```
